32 devices in a mesh: fsdp: 8 (over z, x), seq: 4 (over y, core).
Axes of the slice: x: 2, y: 2, z: 4, core: 2. Of those that a mesh axis runs over, the one named last changes fastest.
Arguments:
- layer_input: bfloat16 [8192, 768], P(('fsdp', 'seq')), may hold values from -6 to 6
- out_grad: bfloat16 [8192, 768], P(('fsdp', 'seq')), may hold values from -6 to 6
- doc_ids: int32 [8192], replicated, may hold values from 0 to 2, as said below
- w_qkv: float32 [768, 2304], P('fsdp'), may hold values from -0.21875 to 0.21875
- w_out: float32 [768, 768], P('fsdp'), may hold values from -12 to 12
- norm1_gain: float32 [768], P('fsdp'), may hold values from 0.25 to 1.75
- norm1_bias: float32 [768], P('fsdp'), may hold values from -1.75 to 1.75
- w_up: float32 [768, 3072], P('fsdp'), may hold values from -0.21875 to 0.21875
- w_gate: float32 [768, 3072], P('fsdp'), may hold values from -0.21875 to 0.21875
- w_down: float32 [3072, 768], P('fsdp'), may hold values from -0.109375 to 0.109375
- norm2_gain: float32 [768], P('fsdp'), may hold values from 0.25 to 1.75
- norm2_bias: float32 [768], P('fsdp'), may hold values from -1.75 to 1.75
Outputs:
- output: bfloat16 [8192, 768], P(('fsdp', 'seq'))
- input_grad: bfloat16 [8192, 768], P(('fsdp', 'seq'))
- grad_w_qkv: float32 [768, 2304], P('fsdp')
- grad_w_out: float32 [768, 768], P('fsdp')
- grad_norm1_gain: float32 [768], P('fsdp')
- grad_norm1_bias: float32 [768], P('fsdp')
- grad_w_up: float32 [768, 3072], P('fsdp')
- grad_w_gate: float32 [768, 3072], P('fsdp')
- grad_w_down: float32 [3072, 768], P('fsdp')
- grad_norm2_gain: float32 [768], P('fsdp')
- grad_norm2_bias: float32 [768], P('fsdp')
The draws below stay inside these ranges and needn't reach their ends.
Inputs may be any that keep to these rules, and one draw needn't show every extreme that they name: `doc_ids`: ids never fall along the tokens. Sequence s (tokens s * 8192 to (s + 1) * 8192 - 1) holds exactly three documents, numbered 3 s, 3 s + 1 and 3 s + 2; its first document ends within its first 1024 tokens and its last one begins within its last 1024 tokens.
All inputs are finite; a program needn't handle non-finite values.
Results may differ from the reference program's by a relative error of at most 0.025.
Values may be sent and summed in bfloat16 or wider, within the bound.
No kernel may reach another device: no remote copies, remote signals or barrier semaphores. Data moves between devices by JAX's collectives and lax.ppermute only.
A program may use at most 128 MiB of HBM per device.

```python
import math
import jax
import jax.numpy as jnp
from jax import lax

D = 768
HEADS = 12
HEAD_DIM = 64
FF = 3072
GROUP = 1024
LENGTH = 8192
TOKENS = 8192


def draw_doc_ids(key, part):
    key = jax.random.fold_in(key, 7)
    key_lead, key_tail = jax.random.split(key)
    seq_count = TOKENS // LENGTH
    lead_end = jax.random.randint(key_lead, (seq_count,), 1, GROUP)
    tail_start = jax.random.randint(key_tail, (seq_count,), LENGTH - GROUP + 1, LENGTH)
    positions = jnp.arange(LENGTH, dtype=jnp.int32)
    local_ids = (positions[None, :] >= lead_end[:, None]).astype(jnp.int32) + (positions[None, :] >= tail_start[:, None]).astype(jnp.int32)
    doc_table = local_ids + 3 * jnp.arange(seq_count, dtype=jnp.int32)[:, None]
    return doc_table.reshape(-1)


def level_of(stream_key, dims, cuts, smallest, high):
    factor_of, own = 1.0, jax.random.fold_in(stream_key, 6)
    for axis_at, parts in cuts:
        steps = jnp.exp(jax.random.uniform(jax.random.fold_in(own, axis_at), (parts,), jnp.float32, smallest / len(cuts), high / len(cuts)))
        factor_of = factor_of * jnp.repeat(steps, dims[axis_at] // parts).reshape([-1 if axis == axis_at else 1 for axis in range(len(dims))])
    return factor_of


def bell_draw(stream_key, shape, scale, bound, shards=(), held_as=jnp.bfloat16):
    entries = scale * jax.random.normal(stream_key, shape, jnp.float32)
    if shards:
        entries = entries * level_of(stream_key, shape, shards, -0.22, 0.18)
    return jnp.clip(entries, -bound, bound).astype(held_as)


def setup_inputs(seed: int = 0) -> dict:
    splits = jax.random.split(jax.random.key(seed), 13)
    layer_input = bell_draw(splits[0], (TOKENS, D), 1.0, 6.0, ((0, 32),))
    out_grad = bell_draw(splits[1], (TOKENS, D), 1.0, 6.0, ((0, 32),))
    doc_ids = draw_doc_ids(jax.random.fold_in(splits[12], 71), 0)
    w_qkv = bell_draw(splits[3], (D, 3 * D), D ** -0.5, 0.21875, ((0, 8),), jnp.float32)
    w_out = bell_draw(splits[4], (D, D), ((LENGTH // 3) ** 0.5 * D ** -0.5), 12.0, ((0, 8),), jnp.float32)
    norm1_gain = jnp.clip(1.0 + 0.15 * jax.random.normal(splits[5], (D,), jnp.float32), 0.25, 1.75)
    norm1_bias = bell_draw(splits[6], (D,), 0.3, 1.75, ((0, 8),), jnp.float32)
    w_up = bell_draw(splits[7], (D, FF), D ** -0.5, 0.21875, ((0, 8),), jnp.float32)
    w_gate = bell_draw(splits[8], (D, FF), D ** -0.5, 0.21875, ((0, 8),), jnp.float32)
    w_down = bell_draw(splits[9], (FF, D), FF ** -0.5, 0.109375, ((0, 8),), jnp.float32)
    norm2_gain = jnp.clip(1.0 + 0.15 * jax.random.normal(splits[10], (D,), jnp.float32), 0.25, 1.75)
    norm2_bias = bell_draw(splits[11], (D,), 0.3, 1.75, ((0, 8),), jnp.float32)
    return dict(layer_input=layer_input, out_grad=out_grad, doc_ids=doc_ids, w_qkv=w_qkv, w_out=w_out, norm1_gain=norm1_gain, norm1_bias=norm1_bias, w_up=w_up, w_gate=w_gate, w_down=w_down, norm2_gain=norm2_gain, norm2_bias=norm2_bias)


@jax.custom_vjp
def low(v):
    return lax.optimization_barrier(v.astype(jnp.bfloat16)).astype(jnp.float32)

@jax.custom_vjp
def low_back(v):
    return v

def low_keep(v):
    return (low(v), None)

def low_pass(kept, grad):
    return (grad,)

def back_keep(v):
    return (v, None)

def back_low(kept, grad):
    return (low(grad),)
low.defvjp(low_keep, low_pass)
low_back.defvjp(back_keep, back_low)
norm_eps = 1e-12
base_log = math.log(1000.0)
highest = lax.Precision.HIGHEST

def rotate(field, cosine_table, sine_table):
    half_dim = field.shape[-1] // 2
    lead_half = field[..., :half_dim]
    tail_half = field[..., half_dim:]
    return jnp.concatenate([lead_half * cosine_table - tail_half * sine_table, tail_half * cosine_table + lead_half * sine_table], axis=-1)

def tables(positions, head_size):
    steps = jnp.arange(head_size // 2, dtype=jnp.float32)
    freqs = jnp.exp(steps * (-2.0 * base_log / head_size))
    angles = positions.astype(jnp.float32)[:, None] * freqs[None, :]
    return (jnp.cos(angles)[:, None, :], jnp.sin(angles)[:, None, :])

def normalize(rows_in, gain, bias):
    centre = rows_in - lax.optimization_barrier(jnp.mean(rows_in, axis=-1, keepdims=True))
    spread = lax.optimization_barrier(jnp.mean(centre * centre, axis=-1, keepdims=True))
    return centre * lax.rsqrt(spread + norm_eps) * gain + bias

def attend_block(queries, keys, values, query_docs, key_docs):
    scores = jnp.einsum('qhd,khd->qhk', queries, keys, precision=highest) * HEAD_DIM ** (-0.5)
    scores = low_back(scores)
    allowed = (query_docs[:, None] == key_docs[None, :])[:, None, :]
    scores = jnp.where(allowed, scores, -1e+30)
    shifted = scores - lax.optimization_barrier(jnp.max(scores, axis=-1, keepdims=True))
    weights = jnp.exp(shifted)
    weights = low(weights / lax.optimization_barrier(jnp.sum(weights, axis=-1, keepdims=True)))
    return jnp.einsum('qhk,khd->qhd', weights, values, precision=highest)

def layer(rows_in, doc_rows, params):
    w_qkv, w_out, gain_one, bias_one, w_up, w_gate, w_down, gain_two, bias_two = [low(item) for item in params]
    seq_len = rows_in.shape[0]
    projected = jnp.dot(rows_in, w_qkv, precision=highest)
    raw_q = low_back(projected[:, :D].reshape(seq_len, HEADS, HEAD_DIM))
    raw_k = low_back(projected[:, D:2 * D].reshape(seq_len, HEADS, HEAD_DIM))
    values = low(low_back(projected[:, 2 * D:].reshape(seq_len, HEADS, HEAD_DIM)))
    cosine_table, sine_table = tables(jnp.arange(seq_len, dtype=jnp.int32), HEAD_DIM)
    queries = low(low_back(rotate(raw_q, cosine_table, sine_table)))
    keys = low(low_back(rotate(raw_k, cosine_table, sine_table)))
    query_rows = 512 if seq_len % 512 == 0 else seq_len
    query_blocks = queries.reshape(seq_len // query_rows, query_rows, HEADS, HEAD_DIM)
    doc_blocks = doc_rows.reshape(seq_len // query_rows, query_rows)
    block_fn = jax.checkpoint(lambda pair_in: attend_block(pair_in[0], keys, values, pair_in[1], doc_rows))
    head_out = lax.map(block_fn, (query_blocks, doc_blocks)).reshape(seq_len, D)
    head_out = low(low_back(head_out))
    branch = low_back(jnp.dot(head_out, w_out, precision=highest))
    hidden = normalize(rows_in + branch, gain_one, bias_one)
    hidden_low = low(hidden)
    up_act = low_back(jnp.dot(hidden_low, w_up, precision=highest))
    gate_act = low_back(jnp.dot(hidden_low, w_gate, precision=highest))
    inner_act = low(gate_act * lax.logistic(gate_act) * up_act)
    ffn_out = low_back(jnp.dot(inner_act, w_down, precision=highest))
    return normalize(hidden + ffn_out, gain_two, bias_two)

def reference(layer_input, out_grad, doc_ids, w_qkv, w_out, norm1_gain, norm1_bias, w_up, w_gate, w_down, norm2_gain, norm2_bias):
    params = (w_qkv, w_out, norm1_gain, norm1_bias, w_up, w_gate, w_down, norm2_gain, norm2_bias)
    seq_count = doc_ids.shape[0] // LENGTH
    inputs = layer_input.astype(jnp.float32).reshape(seq_count, LENGTH, D)
    cotangents = out_grad.astype(jnp.float32).reshape(seq_count, LENGTH, D)
    doc_table = doc_ids.reshape(seq_count, LENGTH)

    def one_seq(totals, seq_item):
        rows_in, cotangent, doc_rows = seq_item
        result, pullback = jax.vjp(lambda rows_arg, param_arg: layer(rows_arg, doc_rows, param_arg), rows_in, params)
        grad_rows, grad_params = pullback(cotangent)
        totals = tuple((total_item + grad_item for total_item, grad_item in zip(totals, grad_params)))
        return (totals, (result.astype(jnp.bfloat16), grad_rows.astype(jnp.bfloat16)))
    zero_grads = tuple((jnp.zeros(item.shape, jnp.float32) for item in params))
    totals, (outputs, grads) = lax.scan(one_seq, zero_grads, (inputs, cotangents, doc_table))
    return (outputs.reshape(-1, D), grads.reshape(-1, D), totals[0], totals[1], totals[2], totals[3], totals[4], totals[5], totals[6], totals[7], totals[8])
```

```python
import functools
import math

import jax
import jax.numpy as jnp
from jax import lax
from jax.experimental import pallas as pl
from jax.experimental.pallas import tpu as pltpu
from jax.sharding import PartitionSpec as P

HEADS = 12
HEAD_DIM = 64
SPAN = 8
EXT = 16
WIDE = HEAD_DIM + EXT
BIG = 2.0**30
SAFE_SUM = 2.0**100
VMEM = 48 * 2**20

bf16 = jnp.bfloat16
f32 = jnp.float32
norm_eps = 1e-12
base_log = math.log(1000.0)
log2e = math.log2(math.e)


def dot(left_op, right_op, left_dim, right_dim):
    return lax.dot_general(
        left_op, right_op, (((left_dim,), (right_dim,)), ((), ())), preferred_element_type=f32
    )


def ring_order(size):
    return list(range(0, size, 2)) + list(range(size - 1, 0, -2))


def ring_place(index, size):
    return jnp.where(index % 2 == 0, index // 2, size - 1 - index // 2)


def ring_index(place, size):
    place = place % size
    return jnp.where(place < size // 2, 2 * place, 2 * (size - 1 - place) + 1)


def ring_shift(value, step, size):
    order = ring_order(size)
    pairs = [
        (base + order[i], base + order[(i + step) % size])
        for base in range(0, lax.axis_size("fsdp"), size)
        for i in range(size)
    ]
    return lax.ppermute(value, "fsdp", pairs)


def seq_swap(value, mask):
    return lax.ppermute(value, "seq", [(i, i ^ mask) for i in range(lax.axis_size("seq"))])


def arrange_kernel(order, *refs):
    for i, ref in enumerate(refs[:-1]):
        refs[-1][order[i]] = ref[...]


def arrange(blocks, order):
    shape = blocks[0].shape
    return pl.pallas_call(
        arrange_kernel,
        in_specs=[pl.BlockSpec(memory_space=pltpu.SMEM)]
        + [pl.BlockSpec(memory_space=pltpu.VMEM)] * len(blocks),
        out_specs=pl.BlockSpec(memory_space=pltpu.VMEM),
        out_shape=jax.ShapeDtypeStruct((len(blocks),) + shape, blocks[0].dtype),
        compiler_params=pltpu.CompilerParams(vmem_limit_bytes=VMEM),
        name="arrange",
    )(jnp.stack(order).astype(jnp.int32), *blocks)


def ring_gather(block, size, place):
    half = block.shape[0] // 2
    right, left = block, block
    blocks, order = [block], [ring_index(place, size)]
    for t in range(1, size // 2):
        right, left = ring_shift(right, 1, size), ring_shift(left, -1, size)
        blocks += [right, left]
        order += [ring_index(place - t, size), ring_index(place + t, size)]
    last = jnp.concatenate(
        [ring_shift(right[:half], 1, size), ring_shift(left[half:], -1, size)], axis=0
    )
    return arrange(blocks + [last], order + [ring_index(place + size // 2, size)])


def ring_scatter(stacked, size, place):
    def part(offset):
        return lax.dynamic_index_in_dim(stacked, ring_index(place + offset, size), 0, False)

    far = part(size // 2)
    half = far.shape[0] // 2
    right = ring_shift(far[:half], 1, size)
    left = ring_shift(far[half:], -1, size)
    for t in range(size // 2 - 1, 0, -1):
        up, down = part(t).astype(f32), part(-t).astype(f32)
        if t == size // 2 - 1:
            up = jnp.concatenate([up[:half] + right.astype(f32), up[half:]], axis=0)
            down = jnp.concatenate([down[:half], down[half:] + left.astype(f32)], axis=0)
        else:
            up, down = up + right.astype(f32), down + left.astype(f32)
        right = ring_shift(up.astype(bf16), 1, size)
        left = ring_shift(down.astype(bf16), -1, size)
    return part(0).astype(f32) + right.astype(f32) + left.astype(f32)


def three_parts(value):
    high = value.astype(bf16).astype(f32)
    rest = value - high
    mid = rest.astype(bf16).astype(f32)
    return high, mid, rest - mid


def with_parts(base, value):
    high, mid, low = three_parts(value)
    lane = lax.broadcasted_iota(jnp.int32, base.shape, 1)
    filled = jnp.where(lane == HEAD_DIM, high, base)
    filled = jnp.where(lane == HEAD_DIM + 1, mid, filled)
    return jnp.where(lane == HEAD_DIM + 2, low, filled)


def first_kernel(heads, tile, qt_ref, qe_ref, k_ref, v_ref, ke_ref, qx_ref, acc_ref):
    ones = jnp.ones((EXT, k_ref.shape[1]), bf16)
    for h in range(heads):
        rows = slice(h * HEAD_DIM, (h + 1) * HEAD_DIM)
        keys = jnp.concatenate([k_ref[rows, :], ke_ref[...]], axis=0)
        vals = jnp.concatenate([v_ref[rows, :], ones], axis=0)
        for start in range(0, qt_ref.shape[1], tile):
            cut = slice(start, start + tile)
            natural = qt_ref[rows, cut].astype(f32).T
            queries = jnp.concatenate([natural, qe_ref[cut, :].astype(f32)], axis=1)
            scores = dot(queries.astype(bf16), keys, 1, 0)
            top = jnp.max(scores, axis=1, keepdims=True)
            weights = jnp.exp2(scores - top).astype(bf16)
            acc_ref[h, :, cut] = dot(vals, weights, 1, 1)
            qx_ref[h, cut, :] = with_parts(queries, top).astype(bf16)


def step_kernel(heads, tile, count, *refs):
    qx_ref, acc_in, acc_ref = refs[0], refs[1], refs[-1]
    blocks = refs[2:-1]
    ones = jnp.ones((EXT, blocks[0].shape[1]), bf16)
    for h in range(heads):
        rows = slice(h * HEAD_DIM, (h + 1) * HEAD_DIM)
        pairs = []
        for b in range(count):
            k_ref, v_ref, ke_ref = blocks[3 * b : 3 * b + 3]
            pairs.append(
                (
                    jnp.concatenate([k_ref[rows, :], ke_ref[...]], axis=0),
                    jnp.concatenate([v_ref[rows, :], ones], axis=0),
                )
            )
        for start in range(0, qx_ref.shape[1], tile):
            cut = slice(start, start + tile)
            total = acc_in[h, :, cut]
            for keys, vals in pairs:
                weights = jnp.exp2(dot(qx_ref[h, cut, :], keys, 1, 0)).astype(bf16)
                total = total + dot(vals, weights, 1, 1)
            acc_ref[h, :, cut] = total


def finish_kernel(heads, tile, count, *refs):
    qx_ref, acc_ref, ke_ref = refs[:3]
    blocks = refs[3 : 3 + 2 * count]
    ot_ref, on_ref, qx2_ref, k_buf, v_buf, acc, qx = refs[3 + 2 * count :]
    length = qx_ref.shape[1]
    sums = jnp.concatenate([acc_ref[h, HEAD_DIM : HEAD_DIM + 8, :] for h in range(heads)], axis=0)
    fine = jnp.logical_and(sums <= SAFE_SUM, sums >= 0.5)
    good = jnp.min(jnp.where(fine, 1.0, 0.0)) > 0.5
    acc[...] = acc_ref[...]
    qx[...] = qx_ref[...]

    @pl.when(jnp.logical_not(good))
    def _():
        ones = jnp.ones((EXT, k_buf.shape[1]), bf16)
        lane = lax.broadcasted_iota(jnp.int32, (tile, WIDE), 1)
        inside = jnp.logical_and(lane >= HEAD_DIM, lane < HEAD_DIM + 3)

        def each(body):
            for b in range(count):
                pltpu.sync_copy(blocks[2 * b], k_buf)
                pltpu.sync_copy(blocks[2 * b + 1], v_buf)

                def turn(step, carry):
                    h = step // (length // tile)
                    cut = pl.ds(pl.multiple_of(step % (length // tile) * tile, tile), tile)
                    rows = pl.ds(pl.multiple_of(h * HEAD_DIM, HEAD_DIM), HEAD_DIM)
                    keys = jnp.concatenate([k_buf[rows, :], ke_ref[b]], axis=0)
                    vals = jnp.concatenate([v_buf[rows, :], ones], axis=0)
                    body(b, h, cut, keys, vals)
                    return carry

                lax.fori_loop(0, heads * (length // tile), turn, 0)

        def raise_top(b, h, cut, keys, vals):
            base = qx[h, cut, :].astype(f32)
            old = jnp.sum(jnp.where(inside, base, 0.0), axis=1, keepdims=True)
            plain = jnp.where(inside, 0.0, base)
            scores = dot(plain.astype(bf16), keys, 1, 0)
            top = jnp.maximum(old, jnp.max(scores, axis=1, keepdims=True))
            qx[h, cut, :] = with_parts(plain, top).astype(bf16)

        def add_up(b, h, cut, keys, vals):
            weights = jnp.exp2(dot(qx[h, cut, :], keys, 1, 0)).astype(bf16)
            acc[h, :, cut] += dot(vals, weights, 1, 1)

        each(raise_top)
        acc[...] = jnp.zeros_like(acc)
        each(add_up)

    for h in range(heads):
        rows = slice(h * HEAD_DIM, (h + 1) * HEAD_DIM)
        for start in range(0, length, tile):
            cut = slice(start, start + tile)
            block = acc[h, :, cut]
            total = block[HEAD_DIM : HEAD_DIM + 1, :]
            ot_ref[rows, cut] = (block[:HEAD_DIM, :] / total).astype(bf16)
            natural = block.T
            sums = natural[:, HEAD_DIM : HEAD_DIM + 1]
            on_ref[h, cut, :] = natural[:, :HEAD_DIM] / sums
            base = qx[h, cut, :].astype(f32)
            lane = lax.broadcasted_iota(jnp.int32, base.shape, 1)
            inside = jnp.logical_and(lane >= HEAD_DIM, lane < HEAD_DIM + 3)
            top = jnp.sum(jnp.where(inside, base, 0.0), axis=1, keepdims=True)
            qx2_ref[h, cut, :] = with_parts(base, top + jnp.log2(sums)).astype(bf16)


def delta_kernel(heads, tile, dot_ref, on_ref, dox_ref):
    for h in range(heads):
        rows = slice(h * HEAD_DIM, (h + 1) * HEAD_DIM)
        for start in range(0, dot_ref.shape[1], tile):
            cut = slice(start, start + tile)
            natural = dot_ref[rows, cut].astype(f32).T
            delta = jnp.sum(natural * on_ref[h, cut, :], axis=1, keepdims=True)
            base = jnp.concatenate([natural, jnp.zeros((tile, EXT), f32)], axis=1)
            dox_ref[h, cut, :] = with_parts(base, delta).astype(bf16)


def back_kernel(
    heads,
    q_tile,
    k_tile,
    qx_ref,
    dox_ref,
    qt_ref,
    dot_ref,
    dq_in,
    k_ref,
    v_ref,
    ke_ref,
    dq_ref,
    dk_ref,
    dv_ref,
):
    for h in range(heads):
        rows = slice(h * HEAD_DIM, (h + 1) * HEAD_DIM)
        keys = jnp.concatenate([k_ref[rows, :], ke_ref[...]], axis=0)
        vals = jnp.concatenate([v_ref[rows, :], ke_ref[...]], axis=0)
        for k_start in range(0, k_ref.shape[1], k_tile):
            k_cut = slice(k_start, k_start + k_tile)
            d_key, d_value = 0.0, 0.0
            for start in range(0, qt_ref.shape[1], q_tile):
                cut = slice(start, start + q_tile)
                weights = jnp.exp2(dot(qx_ref[h, cut, :], keys[:, k_cut], 1, 0))
                shifted = dot(dox_ref[h, cut, :], vals[:, k_cut], 1, 0)
                d_scores = (weights * shifted).astype(bf16)
                d_value = d_value + dot(dot_ref[rows, cut], weights.astype(bf16), 1, 0)
                d_key = d_key + dot(qt_ref[rows, cut], d_scores, 1, 0)
                d_query = dot(keys[:HEAD_DIM, k_cut], d_scores, 1, 1)
                if k_start == 0:
                    dq_ref[rows, cut] = dq_in[rows, cut] + d_query
                else:
                    dq_ref[rows, cut] += d_query
            dk_ref[rows, k_cut] = d_key.astype(bf16)
            dv_ref[rows, k_cut] = d_value.astype(bf16)


def local_call(kernel, outs, ins, flops, name, scratch=(), spaces=None):
    spaces = spaces or [pltpu.VMEM] * len(ins)
    return pl.pallas_call(
        kernel,
        in_specs=[pl.BlockSpec(memory_space=space) for space in spaces],
        out_specs=[pl.BlockSpec(memory_space=pltpu.VMEM) for _ in outs],
        out_shape=[jax.ShapeDtypeStruct(shape, dtype) for shape, dtype in outs],
        scratch_shapes=list(scratch),
        compiler_params=pltpu.CompilerParams(vmem_limit_bytes=VMEM),
        cost_estimate=pl.CostEstimate(flops=flops, bytes_accessed=2**20, transcendentals=0),
        name=name,
    )(*ins)


def layer_norm(rows_in):
    centre = rows_in - jnp.mean(rows_in, axis=-1, keepdims=True)
    spread = jnp.mean(centre * centre, axis=-1, keepdims=True)
    rstd = lax.rsqrt(spread + norm_eps)
    return centre * rstd, rstd


def norm_back(normed, rstd, grad, gain):
    scaled = grad * gain
    return rstd * (
        scaled
        - jnp.mean(scaled, axis=-1, keepdims=True)
        - normed * jnp.mean(scaled * normed, axis=-1, keepdims=True)
    )


def turn(part, cosine, sine):
    heads = part.shape[0] // HEAD_DIM
    split = part.reshape(heads, 2, HEAD_DIM // 2, part.shape[1])
    lead, tail = split[:, 0], split[:, 1]
    return jnp.stack([lead * cosine - tail * sine, tail * cosine + lead * sine], 1).reshape(
        part.shape
    )


def local(
    layer_input,
    out_grad,
    doc_ids,
    w_qkv,
    w_out,
    norm1_gain,
    norm1_bias,
    w_up,
    w_gate,
    w_down,
    norm2_gain,
    norm2_bias,
):
    fsdp = lax.axis_size("fsdp")
    groups = lax.axis_size("seq")
    f = lax.axis_index("fsdp")
    s = lax.axis_index("seq")
    side, core = s // 2, s % 2
    tok_rows, width = layer_input.shape
    w_rows = w_qkv.shape[0]
    inner = width // groups
    heads = inner // HEAD_DIM
    group_rows = tok_rows * groups
    half_rows = group_rows // 2
    length = SPAN * group_rows
    place = ring_place(f, fsdp)
    spot = ring_place(f % SPAN, SPAN)
    base = f // SPAN * SPAN

    def quarter(matrix, start):
        return lax.dynamic_slice_in_dim(matrix, start + s * inner, inner, 1)

    qkv_own = jnp.concatenate([quarter(w_qkv, i * width) for i in range(3)], axis=1).astype(bf16)
    x_side = seq_swap(layer_input, 2)
    x_core = seq_swap(layer_input, 1)
    x_far = seq_swap(x_side, 1)
    qkv_full = ring_gather(qkv_own, fsdp, place).reshape(width, 3 * inner)

    def ff_quarter(matrix):
        split = matrix.reshape(w_rows, fsdp, groups, w_rows)
        return lax.dynamic_index_in_dim(split, s, 2, False).reshape(w_rows, width)

    gains = jnp.stack([norm1_gain, norm1_bias, norm2_gain, norm2_bias], axis=1)
    own = jnp.concatenate(
        [
            w_out,
            ff_quarter(w_up),
            ff_quarter(w_gate),
            lax.dynamic_slice_in_dim(w_down, s * w_rows, w_rows, 0),
            gains,
            jnp.zeros((w_rows, 124), f32),
        ],
        axis=1,
    ).astype(bf16)
    full = ring_gather(own, fsdp, place).reshape(width, own.shape[1])
    out_full = full[:, :width]
    up_own = full[:, width : 2 * width]
    gate_own = full[:, 2 * width : 3 * width]
    down_own = full[:, 3 * width : 4 * width]
    vectors = full[:, 4 * width : 4 * width + 4].astype(f32).T
    gain_one, bias_one, gain_two, bias_two = [vectors[i : i + 1] for i in range(4)]
    up_other = seq_swap(up_own, 2)
    gate_other = seq_swap(gate_own, 2)
    down_other = seq_swap(down_own, 2)

    x_all = arrange([layer_input, x_side, x_core, x_far], [s, s ^ 2, s ^ 1, s ^ 3]).reshape(
        group_rows, width
    )
    projected = dot(qkv_full, x_all, 0, 1)
    positions = f % SPAN * group_rows + jnp.arange(group_rows, dtype=jnp.int32)
    steps = jnp.arange(HEAD_DIM // 2, dtype=f32)
    freqs = jnp.exp(steps * (-2.0 * base_log / HEAD_DIM))
    angles = freqs[:, None] * positions.astype(f32)[None, :]
    cosine, sine = jnp.cos(angles), jnp.sin(angles)
    score_scale = HEAD_DIM ** (-0.5)
    queries = turn(projected[:inner] * (score_scale * log2e), cosine, sine).astype(bf16)
    own_kv = jnp.concatenate(
        [turn(projected[inner : 2 * inner], cosine, sine), projected[2 * inner :]], axis=0
    ).astype(bf16)

    seq_docs = lax.dynamic_slice_in_dim(doc_ids, f // SPAN * length, length) - f // SPAN * 3
    kinds = jnp.arange(3, dtype=jnp.int32)
    key_ext = jnp.concatenate(
        [
            jnp.full((3, length), -1.0, f32),
            jnp.where(seq_docs[None, :] == kinds[:, None], 0.0, -1.0),
            jnp.zeros((EXT - 6, length), f32),
        ],
        axis=0,
    ).astype(bf16)
    own_docs = lax.dynamic_slice_in_dim(seq_docs, f % SPAN * group_rows, group_rows)
    query_ext = jnp.concatenate(
        [
            jnp.zeros((group_rows, 3), f32),
            jnp.where(own_docs[:, None] == kinds[None, :], BIG, 0.0),
            jnp.zeros((group_rows, EXT - 6), f32),
        ],
        axis=1,
    ).astype(bf16)

    def ext_of(offset):
        return lax.dynamic_slice_in_dim(
            key_ext, ring_index(spot + offset, SPAN) * group_rows, group_rows, 1
        )

    block_flops = 4 * 256 * heads * group_rows * group_rows // 2
    acc_out = ((heads, WIDE, group_rows), f32)
    wide_out = ((heads, group_rows, WIDE), bf16)
    tile = min(512, group_rows)
    own_ext = ext_of(0)
    qx, acc = local_call(
        functools.partial(first_kernel, heads, tile),
        [wide_out, acc_out],
        [queries, query_ext, own_kv[:inner], own_kv[inner:], own_ext],
        block_flops,
        "attend_own",
    )
    blocks = {0: (own_kv[:inner], own_kv[inner:], own_ext)}
    right, left = own_kv, own_kv
    for t in range(1, SPAN // 2 + 1):
        if t < SPAN // 2:
            right, left = ring_shift(right, 1, SPAN), ring_shift(left, -1, SPAN)
            blocks[-t] = (right[:inner], right[inner:], ext_of(-t))
            blocks[t] = (left[:inner], left[inner:], ext_of(t))
            now = blocks[-t] + blocks[t]
        else:
            blocks[t] = (
                ring_shift(right[:inner], 1, SPAN),
                ring_shift(left[inner:], -1, SPAN),
                ext_of(t),
            )
            now = blocks[t]
        (acc,) = local_call(
            functools.partial(step_kernel, heads, tile, len(now) // 3),
            [acc_out],
            [qx, acc, *now],
            block_flops * (len(now) // 3),
            "attend_step",
        )
    offsets = sorted(blocks)
    heads_t, heads_n, qx = local_call(
        functools.partial(finish_kernel, heads, min(256, group_rows), SPAN),
        [((inner, group_rows), bf16), ((heads, group_rows, HEAD_DIM), f32), wide_out],
        [
            qx,
            acc,
            jnp.stack([blocks[o][2] for o in offsets]),
            *[ref for o in offsets for ref in blocks[o][:2]],
        ],
        block_flops // 16,
        "attend_finish",
        scratch=[
            pltpu.VMEM((inner, group_rows), bf16),
            pltpu.VMEM((inner, group_rows), bf16),
            pltpu.VMEM(*acc_out),
            pltpu.VMEM(*wide_out),
        ],
        spaces=[pltpu.VMEM] * 3 + [pl.ANY] * (2 * SPAN),
    )

    def my_half(value, axis):
        return lax.dynamic_slice_in_dim(value, side * half_rows, half_rows, axis)

    def other_half(value, axis):
        return lax.dynamic_slice_in_dim(value, (1 - side) * half_rows, half_rows, axis)

    heads_own = my_half(heads_t, 1)
    heads_side = seq_swap(other_half(heads_t, 1), 2)
    heads_pair = jnp.stack([heads_own, heads_side])
    heads_far = seq_swap(heads_pair, 1)
    heads_all = arrange(
        [heads_own, heads_side, heads_far[0], heads_far[1]], [s, s ^ 2, s ^ 1, s ^ 3]
    ).reshape(width, half_rows)
    x_half = my_half(x_all, 0).astype(f32)
    first_sum = x_half + dot(heads_all, out_full, 0, 0)
    normed_one, rstd_one = layer_norm(first_sum)
    hidden = normed_one * gain_one + bias_one
    hidden_low = hidden.astype(bf16)

    def my_rows(value):
        return lax.dynamic_slice_in_dim(value, core * tok_rows, tok_rows, 0)

    def other_rows(value):
        return lax.dynamic_slice_in_dim(value, (1 - core) * tok_rows, tok_rows, 0)

    def core_sum(value):
        got = seq_swap(other_rows(value).astype(bf16), 1)
        return my_rows(value) + got.astype(f32)

    def core_gather(value):
        got = seq_swap(value, 1)
        return arrange([value, got], [core, 1 - core]).reshape(half_rows, width)

    acts = []
    branch = 0.0
    for up_w, gate_w, down_w in ((up_own, gate_own, down_own), (up_other, gate_other, down_other)):
        up_act, gate_act = dot(hidden_low, up_w, 1, 0), dot(hidden_low, gate_w, 1, 0)
        gate_sig = lax.logistic(gate_act)
        inner_low = (gate_act * gate_sig * up_act).astype(bf16)
        acts.append((up_act, gate_act, gate_sig, inner_low))
        branch = branch + dot(inner_low, down_w, 1, 0)
    second_sum = my_rows(hidden) + core_sum(branch)
    normed_two, rstd_two = layer_norm(second_sum)
    result = normed_two * gain_two + bias_two
    cotangent = out_grad.astype(f32)
    d_second = norm_back(normed_two, rstd_two, cotangent, gain_two)
    d_branch_two = core_gather(d_second.astype(bf16))
    d_hidden = 0.0
    ff_grads = []
    for (up_act, gate_act, gate_sig, inner_low), (up_w, gate_w, down_w) in zip(
        acts, ((up_own, gate_own, down_own), (up_other, gate_other, down_other))
    ):
        d_inner = dot(d_branch_two, down_w, 1, 1)
        d_gate = (d_inner * up_act * gate_sig * (1.0 + gate_act * (1.0 - gate_sig))).astype(bf16)
        d_up = (d_inner * gate_act * gate_sig).astype(bf16)
        d_hidden = d_hidden + dot(d_up, up_w, 1, 1) + dot(d_gate, gate_w, 1, 1)
        ff_grads.append(
            (
                dot(hidden_low, d_up, 0, 0),
                dot(hidden_low, d_gate, 0, 0),
                dot(inner_low, d_branch_two, 0, 0),
            )
        )
    d_hidden = d_second + core_sum(d_hidden)
    normed_own = my_rows(normed_one)
    d_first = norm_back(normed_own, my_rows(rstd_one), d_hidden, gain_one)
    d_branch_one = core_gather(d_first.astype(bf16))

    def out_rows(which):
        return lax.dynamic_slice_in_dim(out_full, (2 * which + core) * inner, inner, 0)

    d_heads_own = dot(out_rows(side), d_branch_one, 1, 1).astype(bf16)
    d_heads_side = seq_swap(dot(out_rows(1 - side), d_branch_one, 1, 1).astype(bf16), 2)
    d_heads_t = jnp.concatenate(
        [
            jnp.where(side == 0, d_heads_own, d_heads_side),
            jnp.where(side == 0, d_heads_side, d_heads_own),
        ],
        axis=1,
    )
    (dox,) = local_call(
        functools.partial(delta_kernel, heads, tile),
        [wide_out],
        [d_heads_t, heads_n],
        block_flops // 16,
        "delta",
    )

    def out_columns(which):
        return lax.dynamic_slice_in_dim(d_branch_one, (2 * which + core) * inner, inner, 1)

    grad_vectors = jnp.stack(
        [
            jnp.sum(d_hidden * normed_own, axis=0),
            jnp.sum(d_hidden, axis=0),
            jnp.sum(cotangent * normed_two, axis=0),
            jnp.sum(cotangent, axis=0),
        ],
        axis=1,
    )
    own_grads = [*ff_grads[0], dot(heads_all, out_columns(side), 1, 0)]
    other_grads = [*ff_grads[1], dot(heads_all, out_columns(1 - side), 1, 0)]
    got_grads = [seq_swap(grad.astype(bf16), 2) for grad in other_grads]
    summed = [
        (mine + got.astype(f32)).astype(bf16).reshape(fsdp, w_rows, -1)
        for mine, got in zip(own_grads, got_grads)
    ]
    packed = jnp.concatenate(
        summed
        + [
            grad_vectors.astype(bf16).reshape(fsdp, w_rows, 4),
            jnp.zeros((fsdp, w_rows, 60), bf16),
        ],
        axis=2,
    )
    grads_own = ring_scatter(packed, fsdp, place).astype(bf16)

    d_query = jnp.zeros((inner, group_rows), f32)

    def back(offset, d_query):
        return local_call(
            functools.partial(back_kernel, heads, min(256, group_rows), group_rows),
            [((inner, group_rows), f32), ((inner, group_rows), bf16), ((inner, group_rows), bf16)],
            [qx, dox, queries, d_heads_t, d_query, *blocks[offset]],
            block_flops * 2,
            "attend_back",
        )

    far = SPAN // 2
    d_query, d_key, d_value = back(far, d_query)
    right, left = ring_shift(d_key, 1, SPAN), ring_shift(d_value, -1, SPAN)
    for t in range(far - 1, 0, -1):
        d_query, up_key, up_value = back(t, d_query)
        d_query, down_key, down_value = back(-t, d_query)
        if t == far - 1:
            up = jnp.concatenate([(up_key + right), up_value], axis=0)
            down = jnp.concatenate([down_key, (down_value + left)], axis=0)
        else:
            up = jnp.concatenate([up_key, up_value], axis=0) + right
            down = jnp.concatenate([down_key, down_value], axis=0) + left
        right, left = ring_shift(up, 1, SPAN), ring_shift(down, -1, SPAN)
    d_query, d_key, d_value = back(0, d_query)
    d_kv = (
        jnp.concatenate([d_key, d_value], axis=0).astype(f32) + right.astype(f32) + left.astype(f32)
    )
    d_raw_q = turn(d_query * score_scale, cosine, -sine)
    d_raw_k = turn(d_kv[:inner] * (1.0 / log2e), cosine, -sine)
    d_projected = jnp.concatenate([d_raw_q, d_raw_k, d_kv[inner:]], axis=0).astype(bf16)

    grad_qkv = dot(x_all, d_projected, 0, 1).astype(bf16).reshape(fsdp, w_rows, 3 * inner)
    qkv_own_grad = ring_scatter(grad_qkv, fsdp, place).astype(bf16)
    d_input = dot(d_projected, qkv_full, 0, 1).reshape(2, 2, tok_rows, width)
    sent = lax.dynamic_index_in_dim(d_input, 1 - core, 1, False).astype(bf16)
    kept = lax.dynamic_index_in_dim(d_input, core, 1, False)
    d_input = kept + seq_swap(sent, 1).astype(f32)
    sent = lax.dynamic_index_in_dim(d_input, 1 - side, 0, False).astype(bf16)
    kept = lax.dynamic_index_in_dim(d_input, side, 0, False)
    d_input = d_first + kept + seq_swap(sent, 2).astype(f32)

    def seq_gather(value):
        pair = jnp.stack([value, seq_swap(value, 2)])
        far_pair = seq_swap(pair, 1)
        return arrange([pair[0], pair[1], far_pair[0], far_pair[1]], [s, s ^ 2, s ^ 1, s ^ 3])

    qkv_parts = seq_gather(qkv_own_grad).astype(f32)
    parts = seq_gather(grads_own).astype(f32)
    final_qkv = qkv_parts.reshape(groups, w_rows, 3, inner).transpose(1, 2, 0, 3)
    final_up = parts[:, :, :width].reshape(groups, w_rows, fsdp, w_rows).transpose(1, 2, 0, 3)
    final_gate = (
        parts[:, :, width : 2 * width].reshape(groups, w_rows, fsdp, w_rows).transpose(1, 2, 0, 3)
    )
    final_down = parts[:, :, 2 * width : 3 * width].reshape(groups * w_rows, width)
    final_out = parts[:, :, 3 * width : 3 * width + inner].transpose(1, 0, 2)
    final_vectors = jnp.sum(
        parts[:, :, 3 * width + inner : 3 * width + inner + 4], axis=0
    ).T
    return (
        result.astype(bf16),
        d_input.astype(bf16),
        final_qkv.reshape(w_rows, 3 * width),
        final_out.reshape(w_rows, width),
        final_vectors[0],
        final_vectors[1],
        final_up.reshape(w_rows, -1),
        final_gate.reshape(w_rows, -1),
        final_down,
        final_vectors[2],
        final_vectors[3],
    )


def solution(mesh):
    rows = P(("fsdp", "seq"), None)
    param, vector = P("fsdp", None), P("fsdp")
    in_specs = (rows, rows, P(), param, param, vector, vector, param, param, param, vector, vector)
    out_specs = (rows, rows, param, param, vector, vector, param, param, param, vector, vector)
    return jax.shard_map(local, mesh=mesh, in_specs=in_specs, out_specs=out_specs, check_vma=False)
```

```python
import functools
import math

import jax
import jax.numpy as jnp
from jax import lax
from jax.experimental import pallas as pl
from jax.experimental.pallas import tpu as pltpu
from jax.sharding import PartitionSpec as P

HEADS = 12
HEAD_DIM = 64
SPAN = 8
EXT = 16
WIDE = HEAD_DIM + EXT
BIG = 2.0**30
SAFE_SUM = 2.0**100
VMEM = 48 * 2**20

bf16 = jnp.bfloat16
f32 = jnp.float32
norm_eps = 1e-12
base_log = math.log(1000.0)


def dot(left_op, right_op, left_dim, right_dim):
    return lax.dot_general(
        left_op, right_op, (((left_dim,), (right_dim,)), ((), ())), preferred_element_type=f32
    )


def ring_order(size):
    return list(range(0, size, 2)) + list(range(size - 1, 0, -2))


def ring_place(index, size):
    return jnp.where(index % 2 == 0, index // 2, size - 1 - index // 2)


def ring_index(place, size):
    place = place % size
    return jnp.where(place < size // 2, 2 * place, 2 * (size - 1 - place) + 1)


def ring_shift(value, step, size):
    order = ring_order(size)
    pairs = [
        (base + order[i], base + order[(i + step) % size])
        for base in range(0, lax.axis_size("fsdp"), size)
        for i in range(size)
    ]
    return lax.ppermute(value, "fsdp", pairs)


def seq_swap(value, mask):
    return lax.ppermute(value, "seq", [(i, i ^ mask) for i in range(lax.axis_size("seq"))])


def arrange_kernel(order, *refs):
    for i, ref in enumerate(refs[:-1]):
        refs[-1][order[i]] = ref[...]


def arrange(blocks, order):
    shape = blocks[0].shape
    return pl.pallas_call(
        arrange_kernel,
        in_specs=[pl.BlockSpec(memory_space=pltpu.SMEM)]
        + [pl.BlockSpec(memory_space=pltpu.VMEM)] * len(blocks),
        out_specs=pl.BlockSpec(memory_space=pltpu.VMEM),
        out_shape=jax.ShapeDtypeStruct((len(blocks),) + shape, blocks[0].dtype),
        compiler_params=pltpu.CompilerParams(vmem_limit_bytes=VMEM),
        name="arrange",
    )(jnp.stack(order).astype(jnp.int32), *blocks)


def ring_gather(block, size, place, each=None):
    half = block.shape[0] // 2
    each = each or (lambda value: None)
    right, left = block, block
    blocks, order, seen = [block], [ring_index(place, size)], [each(block)]
    for t in range(1, size // 2):
        right, left = ring_shift(right, 1, size), ring_shift(left, -1, size)
        blocks += [right, left]
        order += [ring_index(place - t, size), ring_index(place + t, size)]
        seen += [each(right), each(left)]
    last = jnp.concatenate(
        [ring_shift(right[:half], 1, size), ring_shift(left[half:], -1, size)], axis=0
    )
    return blocks + [last], order + [ring_index(place + size // 2, size)], seen + [each(last)]


def ring_scatter(part, size):
    half = part(size // 2).shape[0] // 2
    far = part(size // 2).astype(bf16)
    right = ring_shift(far[:half], 1, size)
    left = ring_shift(far[half:], -1, size)
    for t in range(size // 2 - 1, 0, -1):
        up, down = part(t), part(-t)
        if t == size // 2 - 1:
            up = jnp.concatenate([up[:half] + right.astype(f32), up[half:]], axis=0)
            down = jnp.concatenate([down[:half], down[half:] + left.astype(f32)], axis=0)
        else:
            up, down = up + right.astype(f32), down + left.astype(f32)
        right = ring_shift(up.astype(bf16), 1, size)
        left = ring_shift(down.astype(bf16), -1, size)
    return part(0) + right.astype(f32) + left.astype(f32)


def three_parts(value):
    high = value.astype(bf16).astype(f32)
    rest = value - high
    mid = rest.astype(bf16).astype(f32)
    return high, mid, rest - mid


def with_parts(base, value):
    high, mid, low = three_parts(value)
    lane = lax.broadcasted_iota(jnp.int32, base.shape, 1)
    filled = jnp.where(lane == HEAD_DIM, high, base)
    filled = jnp.where(lane == HEAD_DIM + 1, mid, filled)
    return jnp.where(lane == HEAD_DIM + 2, low, filled)


def first_kernel(heads, tile, where_ref, ext_ref, qt_ref, qe_ref, kv_ref, qx_ref, acc_ref):
    tokens = qt_ref.shape[1]
    ones = jnp.ones((EXT, tokens), bf16)
    ext = block_ext(ext_ref, where_ref, 0, tokens)
    for h in range(heads):
        rows = slice(h * HEAD_DIM, (h + 1) * HEAD_DIM)
        k_rows, v_rows = block_rows([kv_ref], h)
        keys = jnp.concatenate([k_rows, ext], axis=0)
        vals = jnp.concatenate([v_rows, ones], axis=0)
        for start in range(0, tokens, tile):
            cut = slice(start, start + tile)
            natural = qt_ref[rows, cut].astype(f32).T
            queries = jnp.concatenate([natural, qe_ref[cut, :].astype(f32)], axis=1)
            scores = dot(queries.astype(bf16), keys, 1, 0)
            top = jnp.max(scores, axis=1, keepdims=True)
            weights = jnp.exp(scores - top).astype(bf16)
            acc_ref[h, :, cut] = dot(vals, weights, 1, 1)
            qx_ref[h, cut, :] = with_parts(queries, top).astype(bf16)


def block_rows(refs, h):
    if len(refs) == 2:
        rows = slice(h * HEAD_DIM, (h + 1) * HEAD_DIM)
        return refs[0][rows, :], refs[1][rows, :]
    inner = refs[0].shape[0] // 2
    return (
        refs[0][h * HEAD_DIM : (h + 1) * HEAD_DIM, :],
        refs[0][inner + h * HEAD_DIM : inner + (h + 1) * HEAD_DIM, :],
    )


def block_ext(ext_ref, where_ref, index, tokens):
    return ext_ref[:, pl.ds(pl.multiple_of(where_ref[index] * tokens, tokens), tokens)]


def step_kernel(heads, tile, parts, where_ref, ext_ref, qx_ref, acc_in, *refs):
    acc_ref, tokens = refs[-1], qx_ref.shape[1]
    ones = jnp.ones((EXT, tokens), bf16)
    blocks, at = [], 0
    for b, part in enumerate(parts):
        blocks.append((refs[at : at + part], block_ext(ext_ref, where_ref, b, tokens)))
        at += part
    for h in range(heads):
        pairs = []
        for block, ext in blocks:
            k_rows, v_rows = block_rows(block, h)
            pairs.append(
                (jnp.concatenate([k_rows, ext], axis=0), jnp.concatenate([v_rows, ones], axis=0))
            )
        for start in range(0, tokens, tile):
            cut = slice(start, start + tile)
            total = acc_in[h, :, cut]
            for keys, vals in pairs:
                weights = jnp.exp(dot(qx_ref[h, cut, :], keys, 1, 0)).astype(bf16)
                total = total + dot(vals, weights, 1, 1)
            acc_ref[h, :, cut] = total


def finish_kernel(heads, tile, parts, where_ref, ext_ref, qx_ref, acc_ref, *refs):
    count = sum(parts)
    blocks = refs[:count]
    ot_ref, on_ref, qx2_ref, k_buf, v_buf, acc_new, qx_new = refs[count:]
    tokens = qx_ref.shape[1]
    inner = k_buf.shape[0]
    fine = True
    for h in range(heads):
        sums = acc_ref[h, HEAD_DIM : HEAD_DIM + 8, :]
        fine = jnp.logical_and(fine, jnp.logical_and(sums <= SAFE_SUM, sums >= 0.5))
    good = jnp.min(jnp.where(fine, 1.0, 0.0)) > 0.5

    def write(acc, qx):
        lane = lax.broadcasted_iota(jnp.int32, (tile, WIDE), 1)
        inside = jnp.logical_and(lane >= HEAD_DIM, lane < HEAD_DIM + 3)
        for h in range(heads):
            rows = slice(h * HEAD_DIM, (h + 1) * HEAD_DIM)
            for start in range(0, tokens, tile):
                cut = slice(start, start + tile)
                block = acc[h, :, cut]
                total = block[HEAD_DIM : HEAD_DIM + 1, :]
                normed = block[:HEAD_DIM, :] * (1.0 / total)
                ot_ref[rows, cut] = normed.astype(bf16)
                stacked = jnp.concatenate([normed, jnp.log(block[HEAD_DIM:, :])], axis=0).T
                on_ref[h, cut, :] = stacked[:, :HEAD_DIM]
                base = qx[h, cut, :].astype(f32)
                top = jnp.sum(jnp.where(inside, base, 0.0), axis=1, keepdims=True)
                shift = top + stacked[:, HEAD_DIM : HEAD_DIM + 1]
                qx2_ref[h, cut, :] = with_parts(base, shift).astype(bf16)

    @pl.when(good)
    def _():
        write(acc_ref, qx_ref)

    @pl.when(jnp.logical_not(good))
    def _():
        ones = jnp.ones((EXT, tokens), bf16)
        lane = lax.broadcasted_iota(jnp.int32, (tile, WIDE), 1)
        inside = jnp.logical_and(lane >= HEAD_DIM, lane < HEAD_DIM + 3)

        def each(body):
            at = 0
            for b, part in enumerate(parts):
                if part == 2:
                    pltpu.sync_copy(blocks[at], k_buf)
                    pltpu.sync_copy(blocks[at + 1], v_buf)
                else:
                    pltpu.sync_copy(blocks[at].at[pl.ds(0, inner)], k_buf)
                    pltpu.sync_copy(blocks[at].at[pl.ds(inner, inner)], v_buf)
                at += part
                ext = block_ext(ext_ref, where_ref, b, tokens)

                def turn(step, carry):
                    h = step // (tokens // tile)
                    cut = pl.ds(pl.multiple_of(step % (tokens // tile) * tile, tile), tile)
                    rows = pl.ds(pl.multiple_of(h * HEAD_DIM, HEAD_DIM), HEAD_DIM)
                    keys = jnp.concatenate([k_buf[rows, :], ext], axis=0)
                    vals = jnp.concatenate([v_buf[rows, :], ones], axis=0)
                    body(h, cut, keys, vals)
                    return carry

                lax.fori_loop(0, heads * (tokens // tile), turn, 0)

        def raise_top(h, cut, keys, vals):
            base = qx_new[h, cut, :].astype(f32)
            old = jnp.sum(jnp.where(inside, base, 0.0), axis=1, keepdims=True)
            plain = jnp.where(inside, 0.0, base)
            scores = dot(plain.astype(bf16), keys, 1, 0)
            top = jnp.maximum(old, jnp.max(scores, axis=1, keepdims=True))
            qx_new[h, cut, :] = with_parts(plain, top).astype(bf16)

        def add_up(h, cut, keys, vals):
            weights = jnp.exp(dot(qx_new[h, cut, :], keys, 1, 0)).astype(bf16)
            acc_new[h, :, cut] += dot(vals, weights, 1, 1)

        qx_new[...] = qx_ref[...]
        acc_new[...] = jnp.zeros_like(acc_new)
        each(raise_top)
        each(add_up)
        write(acc_new, qx_new)


def delta_kernel(heads, tile, dot_ref, on_ref, dox_ref):
    for h in range(heads):
        rows = slice(h * HEAD_DIM, (h + 1) * HEAD_DIM)
        for start in range(0, dot_ref.shape[1], tile):
            cut = slice(start, start + tile)
            natural = dot_ref[rows, cut].astype(f32).T
            delta = jnp.sum(natural * on_ref[h, cut, :], axis=1, keepdims=True)
            base = jnp.concatenate([natural, jnp.zeros((tile, EXT), f32)], axis=1)
            dox_ref[h, cut, :] = with_parts(base, delta).astype(bf16)


def back_kernel(heads, q_tile, where_ref, ext_ref, qx_ref, dox_ref, qt_ref, dot_ref, dq_in, *refs):
    block, (dq_ref, dkv_ref) = refs[:-2], refs[-2:]
    tokens, inner = qt_ref.shape[1], qt_ref.shape[0]
    ext = block_ext(ext_ref, where_ref, 0, tokens)
    for h in range(heads):
        rows = slice(h * HEAD_DIM, (h + 1) * HEAD_DIM)
        k_rows, v_rows = block_rows(block, h)
        keys = jnp.concatenate([k_rows, ext], axis=0)
        vals = jnp.concatenate([v_rows, ext], axis=0)
        d_key, d_value = 0.0, 0.0
        for start in range(0, tokens, q_tile):
            cut = slice(start, start + q_tile)
            weights = jnp.exp(dot(qx_ref[h, cut, :], keys, 1, 0))
            shifted = dot(dox_ref[h, cut, :], vals, 1, 0)
            d_scores = (weights * shifted).astype(bf16)
            d_value = d_value + dot(dot_ref[rows, cut], weights.astype(bf16), 1, 0)
            d_key = d_key + dot(qt_ref[rows, cut], d_scores, 1, 0)
            dq_ref[rows, cut] = dq_in[rows, cut] + dot(k_rows, d_scores, 1, 1)
        dkv_ref[rows, :] = d_key.astype(bf16)
        dkv_ref[inner + h * HEAD_DIM : inner + (h + 1) * HEAD_DIM, :] = d_value.astype(bf16)


def pack_kernel(parts, s_ref, up_ref, gate_ref, down_ref, out_ref):
    s = s_ref[0]
    rows = up_ref.shape[0]
    for i, ref in enumerate((up_ref, gate_ref)):
        pieces = []
        for k in range(parts):
            run = ref[:, 4 * rows * k : 4 * rows * (k + 1)]
            pieces.append(pltpu.roll(run, (4 * rows - s * rows) % (4 * rows), 1)[:, :rows])
        out_ref[:, i * parts * rows : (i + 1) * parts * rows] = jnp.concatenate(
            pieces, axis=1
        ).astype(bf16)
    own = down_ref[pl.ds(pl.multiple_of(s * rows, 8), rows), :]
    out_ref[:, 2 * parts * rows :] = own.astype(bf16)


def unpack_kernel(parts, width, *refs):
    quarters, (up_ref, gate_ref, down_ref, out_ref, vec_ref) = refs[:4], refs[4:]
    rows = up_ref.shape[0]
    inner = width // 4
    for i, ref in enumerate((up_ref, gate_ref)):
        for k in range(parts):
            at = i * width + k * rows
            ref[:, 4 * rows * k : 4 * rows * (k + 1)] = jnp.concatenate(
                [q[:, at : at + rows].astype(f32) for q in quarters], axis=1
            )
    for g, q in enumerate(quarters):
        down_ref[g * rows : (g + 1) * rows, :] = q[:, 2 * width : 3 * width].astype(f32)
    at = 3 * width
    out_ref[...] = jnp.concatenate([q[:, at : at + inner].astype(f32) for q in quarters], axis=1)
    vec_ref[...] = sum(q[:, at + inner :].astype(f32) for q in quarters)


def ordered_kernel(kernel, count, order, *refs):
    buffer = refs[-1]
    for i in range(count):
        buffer[order[i]] = refs[i][...]
    kernel(*[buffer.at[i] for i in range(count)], *refs[count:-1])


def grads_kernel(slot, hidden_ref, branch_ref, heads_ref, vec_ref, *refs):
    sides, outs = (refs[:4], refs[4:8]), refs[8:]
    count, rows = outs[0].shape[0], outs[0].shape[1]
    width = hidden_ref.shape[1]
    hidden_t = hidden_ref[...].T
    for which, ((up_ref, gate_ref, inner_ref, cols_ref), out_ref) in enumerate(zip(sides, outs)):

        def put(value, at):
            for k in range(count):
                out_ref[slot[k], :, at : at + value.shape[1]] = value[k * rows : (k + 1) * rows]

        put(dot(hidden_t, up_ref[...], 1, 0).astype(bf16), 0)
        put(dot(hidden_t, gate_ref[...], 1, 0).astype(bf16), width)
        put(dot(inner_ref[...].T, branch_ref[...], 1, 0).astype(bf16), 2 * width)
        tail = dot(heads_ref[...], cols_ref[...], 1, 0).astype(bf16)
        rest = vec_ref[...] if which == 0 else jnp.zeros_like(vec_ref[...])
        put(jnp.concatenate([tail, rest], axis=1), 3 * width)


def local_call(kernel, outs, ins, flops, name, scratch=(), spaces=None, after=()):
    spaces = list(spaces or [pltpu.VMEM] * len(ins))
    count = len(ins)

    def body(*refs):
        kernel(*refs[:count], *refs[count + len(after) :])

    return pl.pallas_call(
        body,
        in_specs=[pl.BlockSpec(memory_space=space) for space in spaces + [pl.ANY] * len(after)],
        out_specs=[pl.BlockSpec(memory_space=pltpu.VMEM) for _ in outs],
        out_shape=[jax.ShapeDtypeStruct(shape, dtype) for shape, dtype in outs],
        scratch_shapes=list(scratch),
        compiler_params=pltpu.CompilerParams(vmem_limit_bytes=VMEM),
        cost_estimate=pl.CostEstimate(flops=flops * 5, bytes_accessed=2**20, transcendentals=0),
        name=name,
    )(*ins, *after)


def layer_norm(rows_in):
    centre = rows_in - jnp.mean(rows_in, axis=-1, keepdims=True)
    spread = jnp.mean(centre * centre, axis=-1, keepdims=True)
    rstd = lax.rsqrt(spread + norm_eps)
    return centre * rstd, rstd


def norm_back(normed, rstd, grad, gain):
    scaled = grad * gain
    return rstd * (
        scaled
        - jnp.mean(scaled, axis=-1, keepdims=True)
        - normed * jnp.mean(scaled * normed, axis=-1, keepdims=True)
    )


def turn(part, cosine, sine):
    heads = part.shape[0] // HEAD_DIM
    split = part.reshape(heads, 2, HEAD_DIM // 2, part.shape[1])
    lead, tail = split[:, 0], split[:, 1]
    return jnp.stack([lead * cosine - tail * sine, tail * cosine + lead * sine], 1).reshape(
        part.shape
    )


def local(
    layer_input,
    out_grad,
    doc_ids,
    w_qkv,
    w_out,
    norm1_gain,
    norm1_bias,
    w_up,
    w_gate,
    w_down,
    norm2_gain,
    norm2_bias,
):
    fsdp = lax.axis_size("fsdp")
    groups = lax.axis_size("seq")
    f = lax.axis_index("fsdp")
    s = lax.axis_index("seq")
    side, core = s // 2, s % 2
    tok_rows, width = layer_input.shape
    w_rows = w_qkv.shape[0]
    inner = width // groups
    heads = inner // HEAD_DIM
    group_rows = tok_rows * groups
    half_rows = group_rows // 2
    length = SPAN * group_rows
    place = ring_place(f, fsdp)
    spot = ring_place(f % SPAN, SPAN)
    base = f // SPAN * SPAN

    seq_order = [s, s ^ 2, s ^ 1, s ^ 3]
    smem, vmem = pltpu.SMEM, pltpu.VMEM

    def quarter(matrix, start):
        return lax.dynamic_slice_in_dim(matrix, start + s * inner, inner, 1)

    qkv_own = jnp.concatenate([quarter(w_qkv, i * width) for i in range(3)], axis=1).astype(bf16)
    x_side = seq_swap(layer_input, 2)
    x_core = seq_swap(layer_input, 1)
    x_far = seq_swap(x_side, 1)
    qkv_blocks, order, _ = ring_gather(qkv_own, fsdp, place)
    qkv_full = arrange(qkv_blocks, order).reshape(width, 3 * inner)

    def ff_quarter(matrix):
        split = matrix.reshape(w_rows, fsdp, groups, w_rows)
        return lax.dynamic_index_in_dim(split, s, 2, False).reshape(w_rows, width)

    if w_rows * groups % 128 == 0:
        (ff_own,) = local_call(
            functools.partial(pack_kernel, fsdp),
            [((w_rows, 3 * width), bf16)],
            [s.reshape(1), w_up, w_gate, w_down],
            2**20,
            "pack",
            spaces=[smem, vmem, vmem, vmem],
            after=[qkv_blocks[2 * 2]],
        )
    else:
        down_rows = lax.dynamic_slice_in_dim(w_down, s * w_rows, w_rows, 0)
        ff_own = jnp.concatenate([ff_quarter(w_up), ff_quarter(w_gate), down_rows], 1).astype(bf16)
    gains = jnp.stack([norm1_gain, norm1_bias, norm2_gain, norm2_bias], axis=1)
    spare = 256 - inner % 256
    own = jnp.concatenate(
        [
            ff_own,
            quarter(w_out, 0).astype(bf16),
            gains.astype(bf16),
            jnp.zeros((w_rows, spare - 4), bf16),
        ],
        axis=1,
    )
    mine, order, others = ring_gather(own, fsdp, place, lambda value: seq_swap(value, 2))
    mine = arrange(mine, order).reshape(width, own.shape[1])
    others = arrange(others, order).reshape(width, own.shape[1])
    up_own, gate_own, down_own = [mine[:, i * width : (i + 1) * width] for i in range(3)]
    up_other, gate_other, down_other = [others[:, i * width : (i + 1) * width] for i in range(3)]
    out_own = mine[:, 3 * width : 3 * width + 256]
    out_side = others[:, 3 * width : 3 * width + 256]
    out_core, out_far = seq_swap(out_own, 1), seq_swap(out_side, 1)
    out_parts = arrange([out_own, out_side, out_core, out_far], seq_order)
    out_full = jnp.concatenate([out_parts[i, :, :inner] for i in range(groups)], axis=1)
    vectors = out_own[:, inner : inner + 4].astype(f32).T
    gain_one, bias_one, gain_two, bias_two = [vectors[i : i + 1] for i in range(4)]

    x_all = arrange([layer_input, x_side, x_core, x_far], [s, s ^ 2, s ^ 1, s ^ 3]).reshape(
        group_rows, width
    )
    projected = dot(qkv_full, x_all, 0, 1)
    positions = f % SPAN * group_rows + jnp.arange(group_rows, dtype=jnp.int32)
    steps = jnp.arange(HEAD_DIM // 2, dtype=f32)
    freqs = jnp.exp(steps * (-2.0 * base_log / HEAD_DIM))
    angles = freqs[:, None] * positions.astype(f32)[None, :]
    cosine, sine = jnp.cos(angles), jnp.sin(angles)
    score_scale = HEAD_DIM ** (-0.5)
    queries = turn(projected[:inner], cosine, sine).astype(bf16) * bf16(score_scale)
    own_kv = jnp.concatenate(
        [turn(projected[inner : 2 * inner], cosine, sine), projected[2 * inner :]], axis=0
    ).astype(bf16)

    seq_docs = lax.dynamic_slice_in_dim(doc_ids, f // SPAN * length, length) - f // SPAN * 3
    kinds = jnp.arange(3, dtype=jnp.int32)
    key_ext = jnp.concatenate(
        [
            jnp.full((3, length), -1.0, f32),
            jnp.where(seq_docs[None, :] == kinds[:, None], 0.0, -1.0),
            jnp.zeros((EXT - 6, length), f32),
        ],
        axis=0,
    ).astype(bf16)
    own_docs = lax.dynamic_slice_in_dim(seq_docs, f % SPAN * group_rows, group_rows)
    query_ext = jnp.concatenate(
        [
            jnp.zeros((group_rows, 3), f32),
            jnp.where(own_docs[:, None] == kinds[None, :], BIG, 0.0),
            jnp.zeros((group_rows, EXT - 6), f32),
        ],
        axis=1,
    ).astype(bf16)

    def spots(*offsets):
        return jnp.stack([ring_index(spot + o, SPAN) for o in offsets]).astype(jnp.int32)

    block_flops = 8 * 256 * heads * group_rows * group_rows
    acc_out = ((heads, WIDE, group_rows), f32)
    wide_out = ((heads, group_rows, WIDE), bf16)
    tile = min(512, group_rows)
    qx, acc = local_call(
        functools.partial(first_kernel, heads, tile),
        [wide_out, acc_out],
        [spots(0), key_ext, queries, query_ext, own_kv],
        block_flops,
        "attend_own",
        spaces=[smem] + [vmem] * 4,
    )
    far = SPAN // 2
    blocks = {0: (own_kv,)}
    right, left = own_kv, own_kv
    for t in range(1, far + 1):
        if t < far:
            right, left = ring_shift(right, 1, SPAN), ring_shift(left, -1, SPAN)
            blocks[-t], blocks[t] = (right,), (left,)
            now = [-t, t]
        else:
            blocks[t] = (ring_shift(right[:inner], 1, SPAN), ring_shift(left[inner:], -1, SPAN))
            now = [t]
        refs = [ref for o in now for ref in blocks[o]]
        (acc,) = local_call(
            functools.partial(step_kernel, heads, tile, [len(blocks[o]) for o in now]),
            [acc_out],
            [spots(*now), key_ext, qx, acc, *refs],
            block_flops * len(now),
            "attend_step",
            spaces=[smem] + [vmem] * (3 + len(refs)),
        )
    offsets = sorted(blocks)
    refs = [ref for o in offsets for ref in blocks[o]]
    heads_t, heads_n, qx = local_call(
        functools.partial(
            finish_kernel, heads, min(512, group_rows), [len(blocks[o]) for o in offsets]
        ),
        [((inner, group_rows), bf16), ((heads, group_rows, HEAD_DIM), f32), wide_out],
        [spots(*offsets), key_ext, qx, acc, *refs],
        block_flops // 4,
        "attend_finish",
        scratch=[
            pltpu.VMEM((inner, group_rows), bf16),
            pltpu.VMEM((inner, group_rows), bf16),
            pltpu.VMEM(*acc_out),
            pltpu.VMEM(*wide_out),
        ],
        spaces=[smem] + [vmem] * 3 + [pl.ANY] * len(refs),
    )

    def my_half(value, axis):
        return lax.dynamic_slice_in_dim(value, side * half_rows, half_rows, axis)

    def other_half(value, axis):
        return lax.dynamic_slice_in_dim(value, (1 - side) * half_rows, half_rows, axis)

    heads_own = my_half(heads_t, 1)
    heads_side = seq_swap(other_half(heads_t, 1), 2)
    heads_pair = jnp.stack([heads_own, heads_side])
    heads_far = seq_swap(heads_pair, 1)
    heads_all = arrange(
        [heads_own, heads_side, heads_far[0], heads_far[1]], [s, s ^ 2, s ^ 1, s ^ 3]
    ).reshape(width, half_rows)
    x_half = my_half(x_all, 0).astype(f32)
    first_sum = x_half + dot(heads_all, out_full, 0, 0)
    normed_one, rstd_one = layer_norm(first_sum)
    hidden = normed_one * gain_one + bias_one
    hidden_low = hidden.astype(bf16)

    def my_rows(value):
        return lax.dynamic_slice_in_dim(value, core * tok_rows, tok_rows, 0)

    def other_rows(value):
        return lax.dynamic_slice_in_dim(value, (1 - core) * tok_rows, tok_rows, 0)

    def core_sum(value):
        got = seq_swap(other_rows(value).astype(bf16), 1)
        return my_rows(value) + got.astype(f32)

    def core_gather(value):
        got = seq_swap(value, 1)
        return arrange([value, got], [core, 1 - core]).reshape(half_rows, width)

    acts = []
    branch = 0.0
    for up_w, gate_w, down_w in ((up_own, gate_own, down_own), (up_other, gate_other, down_other)):
        up_act, gate_act = dot(hidden_low, up_w, 1, 0), dot(hidden_low, gate_w, 1, 0)
        gate_sig = lax.logistic(gate_act)
        inner_low = (gate_act * gate_sig * up_act).astype(bf16)
        acts.append((up_act, gate_act, gate_sig, inner_low))
        branch = branch + dot(inner_low, down_w, 1, 0)
    second_sum = my_rows(hidden) + core_sum(branch)
    normed_two, rstd_two = layer_norm(second_sum)
    result = normed_two * gain_two + bias_two
    cotangent = out_grad.astype(f32)
    d_second = norm_back(normed_two, rstd_two, cotangent, gain_two)
    d_branch_two = core_gather(d_second.astype(bf16))
    d_hidden = 0.0
    ff_terms = []
    for (up_act, gate_act, gate_sig, inner_low), (up_w, gate_w, down_w) in zip(
        acts, ((up_own, gate_own, down_own), (up_other, gate_other, down_other))
    ):
        d_inner = dot(d_branch_two, down_w, 1, 1)
        d_gate = (d_inner * up_act * gate_sig * (1.0 + gate_act * (1.0 - gate_sig))).astype(bf16)
        d_up = (d_inner * gate_act * gate_sig).astype(bf16)
        d_hidden = d_hidden + dot(d_up, up_w, 1, 1) + dot(d_gate, gate_w, 1, 1)
        ff_terms.append((d_up, d_gate, inner_low))
    d_hidden = d_second + core_sum(d_hidden)
    normed_own = my_rows(normed_one)
    d_first = norm_back(normed_own, my_rows(rstd_one), d_hidden, gain_one)
    d_branch_one = core_gather(d_first.astype(bf16))

    def out_rows(which):
        return lax.dynamic_slice_in_dim(out_full, (2 * which + core) * inner, inner, 0)

    d_heads_sent = dot(out_rows(1 - side), d_branch_one, 1, 1).astype(bf16)
    d_heads_side = seq_swap(d_heads_sent, 2)
    d_heads_own = dot(out_rows(side), d_branch_one, 1, 1).astype(bf16)
    d_heads_t = jnp.concatenate(
        [
            jnp.where(side == 0, d_heads_own, d_heads_side),
            jnp.where(side == 0, d_heads_side, d_heads_own),
        ],
        axis=1,
    )
    (dox,) = local_call(
        functools.partial(delta_kernel, heads, tile),
        [wide_out],
        [d_heads_t, heads_n],
        block_flops // 4,
        "delta",
    )

    def out_columns(which):
        return lax.dynamic_slice_in_dim(d_branch_one, (2 * which + core) * inner, inner, 1)

    grad_vectors = jnp.stack(
        [
            jnp.sum(d_hidden * normed_own, axis=0),
            jnp.sum(d_hidden, axis=0),
            jnp.sum(cotangent * normed_two, axis=0),
            jnp.sum(cotangent, axis=0),
        ],
        axis=1,
    )
    grad_vectors = jnp.pad(grad_vectors, ((0, 0), (0, spare - 4))).astype(bf16)
    steps_out = [fsdp // 2] + [o for t in range(fsdp // 2 - 1, 0, -1) for o in (t, -t)] + [0]
    step_of = {o: i for i, o in enumerate(steps_out)}
    table = jnp.asarray([step_of[(o + fsdp // 2 - 1) % fsdp - (fsdp // 2 - 1)] for o in range(fsdp)])
    slots = table[(ring_place(jnp.arange(fsdp), fsdp) - place) % fsdp].astype(jnp.int32)
    packed = ((fsdp, w_rows, own.shape[1]), bf16)
    grads_mine, grads_other = local_call(
        grads_kernel,
        [packed, packed],
        [
            slots,
            hidden_low,
            d_branch_two,
            heads_all,
            grad_vectors,
            *ff_terms[0],
            out_columns(side),
            *ff_terms[1],
            out_columns(1 - side),
        ],
        2**32,
        "grads",
        spaces=[smem] + [vmem] * 12,
        after=[d_heads_sent],
    )
    cuts = [0, 3 * fsdp // 8, 5 * fsdp // 8, fsdp]
    got = [seq_swap(grads_other[a:b], 2) for a, b in zip(cuts, cuts[1:])]

    def grads_part(offset):
        i = step_of[offset]
        which = sum(i >= cut for cut in cuts[1:])
        return grads_mine[i].astype(f32) + got[which][i - cuts[which]].astype(f32)

    grads_own = ring_scatter(grads_part, fsdp).astype(bf16)

    d_query = jnp.zeros((inner, group_rows), f32)

    def back(offset, d_query, after):
        return local_call(
            functools.partial(back_kernel, heads, min(256, group_rows)),
            [((inner, group_rows), f32), ((2 * inner, group_rows), bf16)],
            [spots(offset), key_ext, qx, dox, queries, d_heads_t, d_query, *blocks[offset]],
            block_flops * 2,
            "attend_back",
            spaces=[smem] + [vmem] * (6 + len(blocks[offset])),
            after=after,
        )

    d_query, d_far = back(far, d_query, [])
    d_query, up = back(far - 1, d_query, [])
    d_query, down = back(1 - far, d_query, [])
    right, left = ring_shift(d_far[:inner], 1, SPAN), ring_shift(d_far[inner:], -1, SPAN)
    up = jnp.concatenate([up[:inner] + right, up[inner:]], axis=0)
    down = jnp.concatenate([down[:inner], down[inner:] + left], axis=0)
    after = [right, left]
    for t in range(far - 2, 0, -1):
        d_query, next_up = back(t, d_query, after)
        right, left = ring_shift(up, 1, SPAN), ring_shift(down, -1, SPAN)
        d_query, next_down = back(-t, d_query, [])
        up, down = next_up + right, next_down + left
        after = [right, left]
    right, left = ring_shift(up, 1, SPAN), ring_shift(down, -1, SPAN)
    d_query, d_kv = back(0, d_query, after)
    d_kv = d_kv.astype(f32) + right.astype(f32) + left.astype(f32)
    d_raw_q = turn(d_query * score_scale, cosine, -sine)
    d_raw_k = turn(d_kv[:inner], cosine, -sine)
    d_projected = jnp.concatenate([d_raw_q, d_raw_k, d_kv[inner:]], axis=0).astype(bf16)

    grad_qkv = dot(x_all, d_projected, 0, 1).astype(bf16).reshape(fsdp, w_rows, 3 * inner)

    def qkv_part(offset):
        index = ring_index(place + offset, fsdp)
        return lax.dynamic_index_in_dim(grad_qkv, index, 0, False).astype(f32)

    qkv_own_grad = ring_scatter(qkv_part, fsdp).astype(bf16)
    d_input = dot(d_projected, qkv_full, 0, 1).reshape(2, 2, tok_rows, width)
    sent = lax.dynamic_index_in_dim(d_input, 1 - core, 1, False).astype(bf16)
    kept = lax.dynamic_index_in_dim(d_input, core, 1, False)
    d_input = kept + seq_swap(sent, 1).astype(f32)
    sent = lax.dynamic_index_in_dim(d_input, 1 - side, 0, False).astype(bf16)
    kept = lax.dynamic_index_in_dim(d_input, side, 0, False)
    d_input = d_first + kept + seq_swap(sent, 2).astype(f32)

    def seq_gather(value):
        other = seq_swap(value, 2)
        return [value, other, seq_swap(value, 1), seq_swap(other, 1)]

    qkv_parts = arrange(seq_gather(qkv_own_grad), seq_order).astype(f32)
    final_qkv = qkv_parts.reshape(groups, w_rows, 3, inner).transpose(1, 2, 0, 3)
    final_qkv = final_qkv.reshape(w_rows, 3 * width)
    parts = seq_gather(grads_own)
    if w_rows * groups % 128 == 0:
        final_up, final_gate, final_down, final_out, final_vectors = local_call(
            functools.partial(ordered_kernel, functools.partial(unpack_kernel, fsdp, width), 4),
            [
                (w_up.shape, f32),
                (w_gate.shape, f32),
                (w_down.shape, f32),
                (w_out.shape, f32),
                ((w_rows, spare), f32),
            ],
            [jnp.stack(seq_order).astype(jnp.int32), *parts],
            2**20,
            "unpack",
            scratch=[pltpu.VMEM((groups,) + parts[0].shape, bf16)],
            spaces=[smem] + [vmem] * 4,
        )
    else:
        parts = arrange(parts, seq_order).astype(f32)

        def columns(at):
            value = parts[:, :, at : at + width].reshape(groups, w_rows, fsdp, w_rows)
            return value.transpose(1, 2, 0, 3).reshape(w_rows, groups * width)

        final_up, final_gate = columns(0), columns(width)
        final_down = parts[:, :, 2 * width : 3 * width].reshape(groups * w_rows, width)
        final_out = parts[:, :, 3 * width : 3 * width + inner].transpose(1, 0, 2)
        final_out = final_out.reshape(w_rows, width)
        final_vectors = jnp.sum(parts[:, :, 3 * width + inner :], axis=0)
    final_vectors = final_vectors[:, :4].T
    return (
        result.astype(bf16),
        d_input.astype(bf16),
        final_qkv,
        final_out,
        final_vectors[0],
        final_vectors[1],
        final_up,
        final_gate,
        final_down,
        final_vectors[2],
        final_vectors[3],
    )


def solution(mesh):
    rows = P(("fsdp", "seq"), None)
    param, vector = P("fsdp", None), P("fsdp")
    in_specs = (rows, rows, P(), param, param, vector, vector, param, param, param, vector, vector)
    out_specs = (rows, rows, param, param, vector, vector, param, param, param, vector, vector)
    return jax.shard_map(local, mesh=mesh, in_specs=in_specs, out_specs=out_specs, check_vma=False)
```

```python
import functools
import math

import jax
import jax.numpy as jnp
from jax import lax
from jax.experimental import pallas as pl
from jax.experimental.pallas import tpu as pltpu
from jax.sharding import PartitionSpec as P

HEADS = 12
HEAD_DIM = 64
SPAN = 8
EXT = 16
WIDE = HEAD_DIM + EXT
BIG = 2.0**30
SAFE_SUM = 2.0**100
VMEM = 48 * 2**20

bf16 = jnp.bfloat16
f32 = jnp.float32
norm_eps = 1e-12
base_log = math.log(1000.0)


def dot(left_op, right_op, left_dim, right_dim):
    return lax.dot_general(
        left_op, right_op, (((left_dim,), (right_dim,)), ((), ())), preferred_element_type=f32
    )


def ring_order(size):
    return list(range(0, size, 2)) + list(range(size - 1, 0, -2))


def ring_place(index, size):
    return jnp.where(index % 2 == 0, index // 2, size - 1 - index // 2)


def ring_index(place, size):
    place = place % size
    return jnp.where(place < size // 2, 2 * place, 2 * (size - 1 - place) + 1)


def ring_shift(value, step, size):
    order = ring_order(size)
    pairs = [
        (base + order[i], base + order[(i + step) % size])
        for base in range(0, lax.axis_size("fsdp"), size)
        for i in range(size)
    ]
    return lax.ppermute(value, "fsdp", pairs)


def seq_swap(value, mask):
    return lax.ppermute(value, "seq", [(i, i ^ mask) for i in range(lax.axis_size("seq"))])


def arrange_kernel(order, *refs):
    for i, ref in enumerate(refs[:-1]):
        refs[-1][order[i]] = ref[...]


def arrange(blocks, order):
    shape = blocks[0].shape
    return pl.pallas_call(
        arrange_kernel,
        in_specs=[pl.BlockSpec(memory_space=pltpu.SMEM)]
        + [pl.BlockSpec(memory_space=pltpu.VMEM)] * len(blocks),
        out_specs=pl.BlockSpec(memory_space=pltpu.VMEM),
        out_shape=jax.ShapeDtypeStruct((len(blocks),) + shape, blocks[0].dtype),
        compiler_params=pltpu.CompilerParams(vmem_limit_bytes=VMEM),
        name="arrange",
    )(jnp.stack(order).astype(jnp.int32), *blocks)


def arrange_runs_kernel(order, *refs):
    at = 0
    for ref in refs[:-1]:
        for k in range(ref.shape[0]):
            refs[-1][order[at]] = ref[k]
            at += 1


def arrange_runs(runs, order):
    return pl.pallas_call(
        arrange_runs_kernel,
        in_specs=[pl.BlockSpec(memory_space=pltpu.SMEM)]
        + [pl.BlockSpec(memory_space=pltpu.VMEM)] * len(runs),
        out_specs=pl.BlockSpec(memory_space=pltpu.VMEM),
        out_shape=jax.ShapeDtypeStruct((len(order),) + runs[0].shape[1:], runs[0].dtype),
        compiler_params=pltpu.CompilerParams(vmem_limit_bytes=VMEM),
        name="arrange_runs",
    )(jnp.stack(order).astype(jnp.int32), *runs)


def ring_gather(block, size, place):
    half = block.shape[0] // 2
    right, left = block, block
    blocks, order = [block], [ring_index(place, size)]
    for t in range(1, size // 2):
        right, left = ring_shift(right, 1, size), ring_shift(left, -1, size)
        blocks += [right, left]
        order += [ring_index(place - t, size), ring_index(place + t, size)]
    last = jnp.concatenate(
        [ring_shift(right[:half], 1, size), ring_shift(left[half:], -1, size)], axis=0
    )
    return blocks + [last], order + [ring_index(place + size // 2, size)]


def ring_scatter(part, size, far=None):
    far = part(size // 2).astype(bf16) if far is None else far
    half = far.shape[0] // 2
    right = ring_shift(far[:half], 1, size)
    left = ring_shift(far[half:], -1, size)
    for t in range(size // 2 - 1, 0, -1):
        up, down = part(t), part(-t)
        if t == size // 2 - 1:
            up = jnp.concatenate([up[:half] + right.astype(f32), up[half:]], axis=0)
            down = jnp.concatenate([down[:half], down[half:] + left.astype(f32)], axis=0)
        else:
            up, down = up + right.astype(f32), down + left.astype(f32)
        right = ring_shift(up.astype(bf16), 1, size)
        left = ring_shift(down.astype(bf16), -1, size)
    return part(0) + right.astype(f32) + left.astype(f32)


def three_parts(value):
    high = value.astype(bf16).astype(f32)
    rest = value - high
    mid = rest.astype(bf16).astype(f32)
    return high, mid, rest - mid


def with_parts(base, value):
    high, mid, low = three_parts(value)
    lane = lax.broadcasted_iota(jnp.int32, base.shape, 1)
    filled = jnp.where(lane == HEAD_DIM, high, base)
    filled = jnp.where(lane == HEAD_DIM + 1, mid, filled)
    return jnp.where(lane == HEAD_DIM + 2, low, filled)


def first_kernel(heads, tile, where_ref, ext_ref, qt_ref, qe_ref, kv_ref, qx_ref, acc_ref):
    tokens = qt_ref.shape[1]
    ones = jnp.ones((EXT, tokens), bf16)
    ext = block_ext(ext_ref, where_ref, 0, tokens)
    for h in range(heads):
        rows = slice(h * HEAD_DIM, (h + 1) * HEAD_DIM)
        k_rows, v_rows = block_rows([kv_ref], h)
        keys = jnp.concatenate([k_rows, ext], axis=0)
        vals = jnp.concatenate([v_rows, ones], axis=0)
        for start in range(0, tokens, tile):
            cut = slice(start, start + tile)
            natural = qt_ref[rows, cut].astype(f32).T
            queries = jnp.concatenate([natural, qe_ref[cut, :].astype(f32)], axis=1)
            scores = dot(queries.astype(bf16), keys, 1, 0)
            top = jnp.max(scores, axis=1, keepdims=True)
            weights = jnp.exp(scores - top).astype(bf16)
            acc_ref[h, :, cut] = dot(vals, weights, 1, 1)
            qx_ref[h, cut, :] = with_parts(queries, top).astype(bf16)


def block_rows(refs, h):
    if len(refs) == 2:
        rows = slice(h * HEAD_DIM, (h + 1) * HEAD_DIM)
        return refs[0][rows, :], refs[1][rows, :]
    inner = refs[0].shape[0] // 2
    return (
        refs[0][h * HEAD_DIM : (h + 1) * HEAD_DIM, :],
        refs[0][inner + h * HEAD_DIM : inner + (h + 1) * HEAD_DIM, :],
    )


def block_ext(ext_ref, where_ref, index, tokens):
    return ext_ref[:, pl.ds(pl.multiple_of(where_ref[index] * tokens, tokens), tokens)]


def step_kernel(heads, tile, parts, where_ref, ext_ref, qx_ref, acc_in, *refs):
    acc_ref, tokens = refs[-1], qx_ref.shape[1]
    ones = jnp.ones((EXT, tokens), bf16)
    blocks, at = [], 0
    for b, part in enumerate(parts):
        blocks.append((refs[at : at + part], block_ext(ext_ref, where_ref, b, tokens)))
        at += part
    for h in range(heads):
        pairs = []
        for block, ext in blocks:
            k_rows, v_rows = block_rows(block, h)
            pairs.append(
                (jnp.concatenate([k_rows, ext], axis=0), jnp.concatenate([v_rows, ones], axis=0))
            )
        for start in range(0, tokens, tile):
            cut = slice(start, start + tile)
            total = acc_in[h, :, cut]
            for keys, vals in pairs:
                weights = jnp.exp(dot(qx_ref[h, cut, :], keys, 1, 0)).astype(bf16)
                total = total + dot(vals, weights, 1, 1)
            acc_ref[h, :, cut] = total


def finish_kernel(heads, tile, parts, where_ref, ext_ref, qx_ref, acc_ref, *refs):
    count = sum(parts)
    blocks = refs[:count]
    ot_ref, on_ref, qx2_ref, buf, acc, qx = refs[count:]
    tokens = qx_ref.shape[1]
    inner = buf.shape[1] // 2
    fine = True
    for h in range(heads):
        sums = acc_ref[h, HEAD_DIM : HEAD_DIM + 8, :]
        fine = jnp.logical_and(fine, jnp.logical_and(sums <= SAFE_SUM, sums >= 0.5))
    good = jnp.min(jnp.where(fine, 1.0, 0.0)) > 0.5
    acc[...] = acc_ref[...]
    qx[...] = qx_ref[...]

    @pl.when(jnp.logical_not(good))
    def _():
        small = tile // 2
        ones = jnp.ones((EXT, tokens), bf16)
        lane = lax.broadcasted_iota(jnp.int32, (small, WIDE), 1)
        inside = jnp.logical_and(lane >= HEAD_DIM, lane < HEAD_DIM + 3)
        at = 0
        for b, part in enumerate(parts):
            if part == 2:
                pltpu.sync_copy(blocks[at], buf.at[b, pl.ds(0, inner)])
                pltpu.sync_copy(blocks[at + 1], buf.at[b, pl.ds(inner, inner)])
            else:
                pltpu.sync_copy(blocks[at], buf.at[b])
            at += part

        def each(body):
            cuts = tokens // small

            def turn(step, carry):
                b, rest = step // (heads * cuts), step % (heads * cuts)
                h = rest // cuts
                cut = pl.ds(pl.multiple_of(rest % cuts * small, small), small)
                rows = pl.multiple_of(h * HEAD_DIM, HEAD_DIM)
                ext = block_ext(ext_ref, where_ref, b, tokens)
                keys = jnp.concatenate([buf[b, pl.ds(rows, HEAD_DIM), :], ext], axis=0)
                vals = buf[b, pl.ds(pl.multiple_of(inner + rows, HEAD_DIM), HEAD_DIM), :]
                body(h, cut, keys, jnp.concatenate([vals, ones], axis=0))
                return carry

            lax.fori_loop(0, len(parts) * heads * cuts, turn, 0)

        def raise_top(h, cut, keys, vals):
            base = qx[h, cut, :].astype(f32)
            old = jnp.sum(jnp.where(inside, base, 0.0), axis=1, keepdims=True)
            plain = jnp.where(inside, 0.0, base)
            scores = dot(plain.astype(bf16), keys, 1, 0)
            top = jnp.maximum(old, jnp.max(scores, axis=1, keepdims=True))
            qx[h, cut, :] = with_parts(plain, top).astype(bf16)

        def add_up(h, cut, keys, vals):
            weights = jnp.exp(dot(qx[h, cut, :], keys, 1, 0)).astype(bf16)
            acc[h, :, cut] += dot(vals, weights, 1, 1)

        each(raise_top)
        acc[...] = jnp.zeros_like(acc)
        each(add_up)

    lane = lax.broadcasted_iota(jnp.int32, (tile, WIDE), 1)
    inside = jnp.logical_and(lane >= HEAD_DIM, lane < HEAD_DIM + 3)
    for h in range(heads):
        rows = slice(h * HEAD_DIM, (h + 1) * HEAD_DIM)
        for start in range(0, tokens, tile):
            cut = slice(start, start + tile)
            block = acc[h, :, cut]
            normed = block[:HEAD_DIM, :] * (1.0 / block[HEAD_DIM : HEAD_DIM + 1, :])
            ot_ref[rows, cut] = normed.astype(bf16)
            stacked = jnp.concatenate([normed, jnp.log(block[HEAD_DIM:, :])], axis=0).T
            on_ref[h, cut, :] = stacked[:, :HEAD_DIM]
            base = qx[h, cut, :].astype(f32)
            top = jnp.sum(jnp.where(inside, base, 0.0), axis=1, keepdims=True)
            shift = top + stacked[:, HEAD_DIM : HEAD_DIM + 1]
            qx2_ref[h, cut, :] = with_parts(base, shift).astype(bf16)


def delta_kernel(heads, where, own_ref, got_ref, on_ref, dox_ref, dot_ref):
    tokens = own_ref.shape[1]
    for tile in range(2):
        cut = slice(tile * tokens, (tile + 1) * tokens)

        @pl.when(where[0] == tile)
        def _():
            dot_ref[:, cut] = own_ref[...]

        @pl.when(where[0] != tile)
        def _():
            dot_ref[:, cut] = got_ref[...]

        for h in range(heads):
            rows = slice(h * HEAD_DIM, (h + 1) * HEAD_DIM)
            natural = dot_ref[rows, cut].astype(f32).T
            delta = jnp.sum(natural * on_ref[h, cut, :], axis=1, keepdims=True)
            base = jnp.concatenate([natural, jnp.zeros((tokens, EXT), f32)], axis=1)
            dox_ref[h, cut, :] = with_parts(base, delta).astype(bf16)


def back_kernel(heads, q_tile, where_ref, ext_ref, qx_ref, dox_ref, qt_ref, dot_ref, dq_in, *refs):
    block, (dq_ref, dkv_ref) = refs[:-2], refs[-2:]
    tokens, inner = qt_ref.shape[1], qt_ref.shape[0]
    ext = block_ext(ext_ref, where_ref, 0, tokens)
    for h in range(heads):
        rows = slice(h * HEAD_DIM, (h + 1) * HEAD_DIM)
        k_rows, v_rows = block_rows(block, h)
        keys = jnp.concatenate([k_rows, ext], axis=0)
        vals = jnp.concatenate([v_rows, ext], axis=0)
        d_key, d_value = 0.0, 0.0
        for start in range(0, tokens, q_tile):
            cut = slice(start, start + q_tile)
            weights = jnp.exp(dot(qx_ref[h, cut, :], keys, 1, 0))
            shifted = dot(dox_ref[h, cut, :], vals, 1, 0)
            d_scores = (weights * shifted).astype(bf16)
            d_value = d_value + dot(dot_ref[rows, cut], weights.astype(bf16), 1, 0)
            d_key = d_key + dot(qt_ref[rows, cut], d_scores, 1, 0)
            dq_ref[rows, cut] = dq_in[rows, cut] + dot(k_rows, d_scores, 1, 1)
        dkv_ref[rows, :] = d_key.astype(bf16)
        dkv_ref[inner + h * HEAD_DIM : inner + (h + 1) * HEAD_DIM, :] = d_value.astype(bf16)


def pack_kernel(parts, s_ref, up_ref, gate_ref, down_ref, out_ref):
    s = s_ref[0]
    rows = up_ref.shape[0]
    for i, ref in enumerate((up_ref, gate_ref)):
        pieces = []
        for k in range(parts):
            run = ref[:, 4 * rows * k : 4 * rows * (k + 1)]
            pieces.append(pltpu.roll(run, (4 * rows - s * rows) % (4 * rows), 1)[:, :rows])
        out_ref[:, i * parts * rows : (i + 1) * parts * rows] = jnp.concatenate(
            pieces, axis=1
        ).astype(bf16)
    own = down_ref[pl.ds(pl.multiple_of(s * rows, 8), rows), :]
    out_ref[:, 2 * parts * rows :] = own.astype(bf16)


def unpack_kernel(parts, width, *refs):
    quarters, (up_ref, gate_ref, down_ref, out_ref, vec_ref) = refs[:4], refs[4:]
    rows = up_ref.shape[0]
    inner = width // 4
    for i, ref in enumerate((up_ref, gate_ref)):
        for k in range(parts):
            at = i * width + k * rows
            ref[:, 4 * rows * k : 4 * rows * (k + 1)] = jnp.concatenate(
                [q[:, at : at + rows].astype(f32) for q in quarters], axis=1
            )
    for g, q in enumerate(quarters):
        down_ref[g * rows : (g + 1) * rows, :] = q[:, 2 * width : 3 * width].astype(f32)
    at = 3 * width
    out_ref[...] = jnp.concatenate([q[:, at : at + inner].astype(f32) for q in quarters], axis=1)
    vec_ref[...] = sum(q[:, at + inner :].astype(f32) for q in quarters)


def ordered_kernel(kernel, count, order, *refs):
    buffer = refs[-1]
    for i in range(count):
        buffer[order[i]] = refs[i][...]
    kernel(*[buffer.at[i] for i in range(count)], *refs[count:-1])


def grads_kernel(order, hidden_ref, branch_ref, heads_ref, first_sums, second_sums, *refs):
    sides, mine_ref, runs, buffer = (refs[:4], refs[4:8]), refs[8], refs[9:-1], refs[-1]
    count, rows = mine_ref.shape[0], mine_ref.shape[1]
    width = hidden_ref.shape[1]
    hidden_t = hidden_ref[...].T
    heads = heads_ref[...].reshape(width, heads_ref.shape[2])
    vectors = (first_sums[...] + second_sums[...]).T
    vectors = jnp.concatenate(
        [vectors, jnp.zeros((width, mine_ref.shape[2] - 3 * width - width // 4 - 8), f32)], axis=1
    ).astype(bf16)
    for which, (up_ref, gate_ref, inner_ref, cols_ref) in enumerate(sides):

        def put(value, at):
            for k in range(count):
                buffer[k, :, at : at + value.shape[1]] = value[k * rows : (k + 1) * rows]

        put(dot(hidden_t, up_ref[...], 1, 0).astype(bf16), 0)
        put(dot(hidden_t, gate_ref[...], 1, 0).astype(bf16), width)
        put(dot(inner_ref[...].T, branch_ref[...], 1, 0).astype(bf16), 2 * width)
        tail = dot(heads, cols_ref[...], 1, 0).astype(bf16)
        rest = vectors if which == 0 else jnp.zeros_like(vectors)
        put(jnp.concatenate([tail, rest], axis=1), 3 * width)
        if which == 0:
            for i in range(count):
                mine_ref[i] = buffer[order[i]]
        else:
            at = 0
            for run in runs:
                for k in range(run.shape[0]):
                    run[k] = buffer[order[at]]
                    at += 1


def tail_kernel(
    order, where, dq_ref, dkv_ref, right_ref, left_ref, cos_ref, sin_ref, x_ref, w_ref, *refs
):
    grad_ref, sent_ref, kept_ref, raw, buffer = refs
    inner = dq_ref.shape[0]
    cosine, sine = cos_ref[...], sin_ref[...]
    d_kv = dkv_ref[...].astype(f32) + right_ref[...].astype(f32) + left_ref[...].astype(f32)

    def put(base):
        def at_base(at, value):
            raw[base + at : base + at + value.shape[0], :] = value.astype(bf16)

        return at_base

    turn_rows(dq_ref[...] * HEAD_DIM**-0.5, cosine, -sine, put(0))
    turn_rows(d_kv[:inner], cosine, -sine, put(inner))
    raw[2 * inner :, :] = d_kv[inner:].astype(bf16)
    projected = raw[...].T
    count, rows = grad_ref.shape[0], grad_ref.shape[1]
    width, quarter = x_ref.shape[2], x_ref.shape[1]
    terms = dot(projected, w_ref[...].reshape(width, 3 * inner), 1, 1)
    for core in range(2):
        side = [terms[(2 * y + core) * quarter : (2 * y + core + 1) * quarter] for y in range(2)]

        @pl.when(where[1] == core)
        def _():
            for y in range(2):
                kept_ref[y] = side[y]

        @pl.when(where[1] != core)
        def _():
            for y in range(2):
                sent_ref[y] = side[y].astype(bf16)

    grad = dot(x_ref[...].reshape(4 * quarter, width).T, projected, 1, 0).astype(bf16)
    for k in range(count):
        buffer[k] = grad[k * rows : (k + 1) * rows]
    for i in range(count):
        grad_ref[i] = buffer[order[i]]


def unpack_qkv_kernel(*refs):
    quarters, out_ref = refs[:4], refs[4]
    inner = quarters[0].shape[1] // 3
    out_ref[...] = jnp.concatenate(
        [q[:, i * inner : (i + 1) * inner].astype(f32) for i in range(3) for q in quarters], axis=1
    )


def tables_kernel(at_ref, docs_ref, key_ref, query_ref):
    length, tokens = key_ref.shape[1], query_ref.shape[0]

    def kinds(start, count):
        docs = docs_ref[:, pl.ds(pl.multiple_of(start, count), count)] - at_ref[1]
        docs = jnp.broadcast_to(docs, (EXT, count))
        row = lax.broadcasted_iota(jnp.int32, (EXT, count), 0)
        return row, docs == row - 3

    row, same = kinds(at_ref[0], length)
    mark = jnp.where(jnp.logical_or(row < 3, jnp.logical_not(same)), -1.0, 0.0)
    key_ref[...] = jnp.where(row < 6, mark, 0.0).astype(bf16)
    row, same = kinds(at_ref[2], tokens)
    inside = jnp.logical_and(same, jnp.logical_and(row >= 3, row < 6))
    query_ref[...] = jnp.where(inside, BIG, 0.0).T.astype(bf16)


def turn_rows(value, cosine, sine, put):
    half = HEAD_DIM // 2
    for at in range(0, value.shape[0], HEAD_DIM):
        lead, last = value[at : at + half], value[at + half : at + HEAD_DIM]
        put(at, lead * cosine - last * sine)
        put(at + half, last * cosine + lead * sine)


def project_kernel(count, order, places, cos_ref, sin_ref, *refs):
    weights, tokens = refs[:count], refs[count : count + 4]
    q_ref, kv_ref, x_ref, w_ref = refs[count + 4 :]
    inner = q_ref.shape[0]
    for i, ref in enumerate(weights):
        w_ref[order[i]] = ref[...]
    for i, ref in enumerate(tokens):
        x_ref[places[i]] = ref[...]
    cosine, sine = cos_ref[...], sin_ref[...]
    width = x_ref.shape[2]
    matrix = w_ref[...].reshape(width, 3 * inner).T
    rows = x_ref[...].reshape(-1, width)

    def put_q(at, value):
        q_ref[at : at + value.shape[0], :] = value.astype(bf16) * bf16(HEAD_DIM**-0.5)

    def put_k(at, value):
        kv_ref[at : at + value.shape[0], :] = value.astype(bf16)

    turn_rows(dot(matrix[:inner], rows, 1, 1), cosine, sine, put_q)
    turn_rows(dot(matrix[inner : 2 * inner], rows, 1, 1), cosine, sine, put_k)
    kv_ref[inner:, :] = dot(matrix[2 * inner :], rows, 1, 1).astype(bf16)


def outer_kernel(places, *refs):
    parts, (out_ref, vec_ref, buffer) = refs[:4], refs[4:]
    inner = out_ref.shape[1] // 4
    for i, ref in enumerate(parts):
        buffer[places[i]] = ref[...]
    out_ref[...] = jnp.concatenate([buffer[g, :, :inner] for g in range(4)], axis=1)
    vec_ref[...] = parts[0][:, inner:].astype(f32).T[:8]


def norm_parts(rows_in):
    centre = rows_in - jnp.mean(rows_in, axis=-1, keepdims=True)
    rstd = lax.rsqrt(jnp.mean(centre * centre, axis=-1, keepdims=True) + norm_eps)
    return centre * rstd, rstd


def norm_grad(normed, rstd, grad, gain):
    scaled = grad * gain
    mean = jnp.mean(scaled, axis=-1, keepdims=True)
    return rstd * (scaled - mean - normed * jnp.mean(scaled * normed, axis=-1, keepdims=True))


def ff_weights(ref):
    width = ref.shape[0]
    return ref[:, :width], ref[:, width : 2 * width], ref[:, 2 * width : 3 * width]


def forward_kernel(places, where, *refs):
    parts, (x_ref, out_ref, vec_ref, mine_ref, other_ref) = refs[:4], refs[4:9]
    heads_ref, hidden_ref, kept_ref, sent_ref, normed_ref, rstd_ref = refs[9:15]
    acts = (refs[15:18], refs[18:21])
    width, rows = hidden_ref.shape[1], kept_ref.shape[0]
    side, core = where[0], where[1]
    for i, ref in enumerate(parts):
        heads_ref[places[i]] = ref[...]
    for tile in range(2):
        cut = slice(tile * rows, (tile + 1) * rows)
        start = pl.multiple_of((2 * side + tile) * rows, rows)
        heads = heads_ref[:, :, cut].reshape(width, rows).T
        first = x_ref[pl.ds(start, rows), :].astype(f32) + dot(heads, out_ref[...], 1, 0)
        normed, rstd = norm_parts(first)
        hidden = normed * vec_ref[0:1] + vec_ref[1:2]
        low = hidden.astype(bf16)
        hidden_ref[cut, :] = low
        branch = 0.0
        for w_ref, (up_ref, gate_ref, inner_ref) in zip((mine_ref, other_ref), acts):
            up_w, gate_w, down_w = ff_weights(w_ref)
            up, gate = dot(low, up_w, 1, 0), dot(low, gate_w, 1, 0)
            inner = (gate * lax.logistic(gate) * up).astype(bf16)
            up_ref[cut, :], gate_ref[cut, :], inner_ref[cut, :] = up, gate, inner
            branch = branch + dot(inner, down_w, 1, 0)

        @pl.when(core == tile)
        def _():
            kept_ref[...] = hidden + branch
            normed_ref[...] = normed
            rstd_ref[...] = jnp.broadcast_to(rstd, rstd_ref.shape)

        @pl.when(core != tile)
        def _():
            sent_ref[...] = branch.astype(bf16)


def second_kernel(kept_ref, got_ref, grad_ref, vec_ref, result_ref, d_ref, low_ref, sums_ref):
    normed, rstd = norm_parts(kept_ref[...] + got_ref[...].astype(f32))
    gain = vec_ref[2:3]
    result_ref[...] = (normed * gain + vec_ref[3:4]).astype(bf16)
    grad = grad_ref[...].astype(f32)
    d_second = norm_grad(normed, rstd, grad, gain)
    d_ref[...] = d_second
    low_ref[...] = d_second.astype(bf16)
    sums_ref[...] = jnp.zeros_like(sums_ref)
    sums_ref[2:3] = jnp.sum(grad * normed, axis=0, keepdims=True)
    sums_ref[3:4] = jnp.sum(grad, axis=0, keepdims=True)


def backward_kernel(where, own_ref, got_ref, mine_ref, other_ref, *refs):
    acts = (refs[:2], refs[2:4])
    branch_ref, kept_ref, sent_ref = refs[4:7]
    outs = (refs[7:9], refs[9:11])
    rows, core = kept_ref.shape[0], where[1]
    branch_ref[pl.ds(pl.multiple_of(core * rows, rows), rows), :] = own_ref[...]
    branch_ref[pl.ds(pl.multiple_of((1 - core) * rows, rows), rows), :] = got_ref[...]
    for tile in range(2):
        cut = slice(tile * rows, (tile + 1) * rows)
        branch = branch_ref[cut, :]
        total = 0.0
        for w_ref, (up_ref, gate_ref), (d_up_ref, d_gate_ref) in zip(
            (mine_ref, other_ref), acts, outs
        ):
            up_w, gate_w, down_w = ff_weights(w_ref)
            d_inner = dot(branch, down_w, 1, 1)
            up, gate = up_ref[cut, :], gate_ref[cut, :]
            sig = lax.logistic(gate)
            d_gate = (d_inner * up * sig * (1.0 + gate * (1.0 - sig))).astype(bf16)
            d_up = (d_inner * gate * sig).astype(bf16)
            d_up_ref[cut, :], d_gate_ref[cut, :] = d_up, d_gate
            total = total + dot(d_up, up_w, 1, 1) + dot(d_gate, gate_w, 1, 1)

        @pl.when(core == tile)
        def _():
            kept_ref[...] = total

        @pl.when(core != tile)
        def _():
            sent_ref[...] = total.astype(bf16)


def first_back_kernel(
    kept_ref, got_ref, d_second_ref, normed_ref, rstd_ref, vec_ref, d_ref, low_ref, sums_ref
):
    d_hidden = d_second_ref[...] + kept_ref[...] + got_ref[...].astype(f32)
    normed = normed_ref[...]
    d_first = norm_grad(normed, rstd_ref[:, 0:1], d_hidden, vec_ref[0:1])
    d_ref[...] = d_first
    low_ref[...] = d_first.astype(bf16)
    sums_ref[...] = jnp.zeros_like(sums_ref)
    sums_ref[0:1] = jnp.sum(d_hidden * normed, axis=0, keepdims=True)
    sums_ref[1:2] = jnp.sum(d_hidden, axis=0, keepdims=True)


def heads_back_kernel(
    where, own_ref, got_ref, out_ref, own_heads_ref, sent_ref, own_cols_ref, other_cols_ref, branch
):
    side, core = where[0], where[1]
    rows, inner = own_ref.shape[0], sent_ref.shape[0]
    branch[pl.ds(pl.multiple_of(core * rows, rows), rows), :] = own_ref[...]
    branch[pl.ds(pl.multiple_of((1 - core) * rows, rows), rows), :] = got_ref[...]
    for which, ref in ((1 - side, sent_ref), (side, own_heads_ref)):
        at = pl.multiple_of((2 * which + core) * inner, inner)
        ref[...] = dot(out_ref[pl.ds(at, inner), :], branch[...], 1, 1).astype(bf16)
    for group in range(4):
        value = branch[:, group * inner : (group + 1) * inner]

        @pl.when(2 * side + core == group)
        def _():
            own_cols_ref[...] = value

        @pl.when(2 * (1 - side) + core == group)
        def _():
            other_cols_ref[...] = value


def input_mid_kernel(where, kept_ref, got_ref, kept_out, sent_out):
    for y in range(2):
        value = kept_ref[y] + got_ref[y].astype(f32)

        @pl.when(where[0] == y)
        def _():
            kept_out[...] = value

        @pl.when(where[0] != y)
        def _():
            sent_out[...] = value.astype(bf16)


def input_end_kernel(first_ref, kept_ref, got_ref, out_ref):
    out_ref[...] = (first_ref[...] + kept_ref[...] + got_ref[...].astype(f32)).astype(bf16)


def far_kernel(mine_ref, got_ref, out_ref):
    out_ref[...] = (mine_ref[0].astype(f32) + got_ref[0].astype(f32)).astype(bf16)


def local_call(kernel, outs, ins, flops, name, scratch=(), spaces=None, after=()):
    spaces = list(spaces or [pltpu.VMEM] * len(ins))
    count = len(ins)

    def body(*refs):
        kernel(*refs[:count], *refs[count + len(after) :])

    return pl.pallas_call(
        body,
        in_specs=[pl.BlockSpec(memory_space=space) for space in spaces + [pl.ANY] * len(after)],
        out_specs=[pl.BlockSpec(memory_space=pltpu.VMEM) for _ in outs],
        out_shape=[jax.ShapeDtypeStruct(shape, dtype) for shape, dtype in outs],
        scratch_shapes=list(scratch),
        compiler_params=pltpu.CompilerParams(vmem_limit_bytes=VMEM),
        cost_estimate=pl.CostEstimate(flops=flops * 5, bytes_accessed=2**20, transcendentals=0),
        name=name,
    )(*ins, *after)


def local(
    layer_input,
    out_grad,
    doc_ids,
    w_qkv,
    w_out,
    norm1_gain,
    norm1_bias,
    w_up,
    w_gate,
    w_down,
    norm2_gain,
    norm2_bias,
):
    fsdp = lax.axis_size("fsdp")
    groups = lax.axis_size("seq")
    f = lax.axis_index("fsdp")
    s = lax.axis_index("seq")
    side, core = s // 2, s % 2
    tok_rows, width = layer_input.shape
    w_rows = w_qkv.shape[0]
    inner = width // groups
    heads = inner // HEAD_DIM
    group_rows = tok_rows * groups
    half_rows = group_rows // 2
    length = SPAN * group_rows
    place = ring_place(f, fsdp)
    spot = ring_place(f % SPAN, SPAN)
    base = f // SPAN * SPAN

    seq_order = [s, s ^ 2, s ^ 1, s ^ 3]
    seq_places = jnp.stack(seq_order).astype(jnp.int32)
    where = jnp.stack([side, core]).astype(jnp.int32)
    smem, vmem = pltpu.SMEM, pltpu.VMEM
    aligned = w_rows * groups % 128 == 0 and w_rows % 16 == 0

    def quarter(matrix, start):
        return lax.dynamic_slice_in_dim(matrix, start + s * inner, inner, 1)

    qkv_own = jnp.concatenate([quarter(w_qkv, i * width) for i in range(3)], axis=1).astype(bf16)
    x_side = seq_swap(layer_input, 2)
    x_core = seq_swap(layer_input, 1)
    x_far = seq_swap(x_side, 1)
    qkv_blocks, order = ring_gather(qkv_own, fsdp, place)
    early = qkv_blocks[-3:-1]
    ring_order_now = jnp.stack(order).astype(jnp.int32)
    if not aligned:
        qkv_blocks = [arrange(qkv_blocks, order).reshape(width, 3 * inner)]
        ring_order_now = jnp.zeros((1,), jnp.int32)
    key_ext, query_ext = local_call(
        tables_kernel,
        [((EXT, length), bf16), ((group_rows, EXT), bf16)],
        [
            jnp.stack([f // SPAN * length, f // SPAN * 3, f * group_rows]).astype(jnp.int32),
            doc_ids[None, :],
        ],
        2**20,
        "tables",
        spaces=[smem, vmem],
        after=early,
    )
    positions = f % SPAN * group_rows + jnp.arange(group_rows, dtype=jnp.int32)
    steps = jnp.arange(HEAD_DIM // 2, dtype=f32)
    freqs = jnp.exp(steps * (-2.0 * base_log / HEAD_DIM))
    angles = freqs[:, None] * positions.astype(f32)[None, :]
    cosine, sine = jnp.cos(angles), jnp.sin(angles)

    queries, own_kv, x_all, qkv_full = local_call(
        functools.partial(project_kernel, len(qkv_blocks)),
        [
            ((inner, group_rows), bf16),
            ((2 * inner, group_rows), bf16),
            ((groups, tok_rows, width), bf16),
            ((len(qkv_blocks),) + qkv_blocks[0].shape, bf16),
        ],
        [
            ring_order_now,
            seq_places,
            cosine,
            sine,
            *qkv_blocks,
            layer_input,
            x_side,
            x_core,
            x_far,
        ],
        2**32,
        "project",
        spaces=[smem, smem] + [vmem] * (len(qkv_blocks) + 6),
    )

    def ff_quarter(matrix):
        split = matrix.reshape(w_rows, fsdp, groups, w_rows)
        return lax.dynamic_index_in_dim(split, s, 2, False).reshape(w_rows, width)

    if aligned:
        (ff_own,) = local_call(
            functools.partial(pack_kernel, fsdp),
            [((w_rows, 3 * width), bf16)],
            [s.reshape(1), w_up, w_gate, w_down],
            2**20,
            "pack",
            spaces=[smem, vmem, vmem, vmem],
            after=early,
        )
    else:
        down_rows = lax.dynamic_slice_in_dim(w_down, s * w_rows, w_rows, 0)
        ff_own = jnp.concatenate([ff_quarter(w_up), ff_quarter(w_gate), down_rows], 1).astype(bf16)
    gains = jnp.stack([norm1_gain, norm1_bias, norm2_gain, norm2_bias], axis=1)
    spare = 256 - inner % 256
    own = jnp.concatenate(
        [
            ff_own,
            quarter(w_out, 0).astype(bf16),
            gains.astype(bf16),
            jnp.zeros((w_rows, spare - 4), bf16),
        ],
        axis=1,
    )
    mine, order = ring_gather(own, fsdp, place)
    steady = [jnp.int32(i) for i in range(fsdp)]
    runs = [mine[: fsdp // 2 - 1], mine[fsdp // 2 - 1 : -3], mine[-3:]]
    others = [seq_swap(arrange(run, steady[: len(run)]), 2) for run in runs]
    others = arrange_runs(others, order).reshape(width, own.shape[1])
    mine = arrange(mine, order).reshape(width, own.shape[1])
    out_own, out_side = mine[:, 3 * width :], others[:, 3 * width :]
    out_core, out_far = seq_swap(out_own, 1), seq_swap(out_side, 1)
    out_full, vectors = local_call(
        outer_kernel,
        [((width, width), bf16), ((8, width), f32)],
        [seq_places, out_own, out_side, out_core, out_far],
        2**20,
        "outer",
        scratch=[pltpu.VMEM((groups,) + out_own.shape, bf16)],
        spaces=[smem] + [vmem] * 4,
    )

    def spots(*offsets):
        return jnp.stack([ring_index(spot + o, SPAN) for o in offsets]).astype(jnp.int32)

    block_flops = 8 * 256 * heads * group_rows * group_rows
    acc_out = ((heads, WIDE, group_rows), f32)
    wide_out = ((heads, group_rows, WIDE), bf16)
    tile = min(512, group_rows)
    qx, acc = local_call(
        functools.partial(first_kernel, heads, tile),
        [wide_out, acc_out],
        [spots(0), key_ext, queries, query_ext, own_kv],
        block_flops,
        "attend_own",
        spaces=[smem] + [vmem] * 4,
    )
    far = SPAN // 2
    blocks = {0: (own_kv,)}
    right, left = own_kv, own_kv
    for t in range(1, far + 1):
        if t < far:
            right, left = ring_shift(right, 1, SPAN), ring_shift(left, -1, SPAN)
            blocks[-t], blocks[t] = (right,), (left,)
            now = [-t, t]
        else:
            blocks[t] = (ring_shift(right[:inner], 1, SPAN), ring_shift(left[inner:], -1, SPAN))
            now = [t]
        refs = [ref for o in now for ref in blocks[o]]
        (acc,) = local_call(
            functools.partial(step_kernel, heads, tile, [len(blocks[o]) for o in now]),
            [acc_out],
            [spots(*now), key_ext, qx, acc, *refs],
            block_flops * len(now),
            "attend_step",
            spaces=[smem] + [vmem] * (3 + len(refs)),
            after=[mine] if t == far - 1 else [],
        )
    offsets = sorted(blocks)
    refs = [ref for o in offsets for ref in blocks[o]]
    heads_t, heads_n, qx = local_call(
        functools.partial(
            finish_kernel, heads, min(512, group_rows), [len(blocks[o]) for o in offsets]
        ),
        [((inner, group_rows), bf16), ((heads, group_rows, HEAD_DIM), f32), wide_out],
        [spots(*offsets), key_ext, qx, acc, *refs],
        block_flops // 4,
        "attend_finish",
        scratch=[
            pltpu.VMEM((SPAN, 2 * inner, group_rows), bf16),
            pltpu.VMEM(*acc_out),
            pltpu.VMEM(*wide_out),
        ],
        spaces=[smem] + [vmem] * 3 + [pl.ANY] * len(refs),
        after=[out_full],
    )

    def my_half(value, axis):
        return lax.dynamic_slice_in_dim(value, side * half_rows, half_rows, axis)

    def other_half(value, axis):
        return lax.dynamic_slice_in_dim(value, (1 - side) * half_rows, half_rows, axis)

    heads_own = my_half(heads_t, 1)
    heads_side = seq_swap(other_half(heads_t, 1), 2)
    heads_core = seq_swap(heads_own, 1)
    heads_far = seq_swap(heads_side, 1)
    half_low = ((half_rows, width), bf16)
    half_acts = [((half_rows, width), f32)] * 2 + [half_low]
    own_low, own_full = ((tok_rows, width), bf16), ((tok_rows, width), f32)
    sums_out = ((8, width), f32)
    heads_all, hidden_low, kept, sent, normed_one, rstd_one, *acts = local_call(
        forward_kernel,
        [
            ((groups, inner, half_rows), bf16),
            half_low,
            own_full,
            own_low,
            own_full,
            ((tok_rows, 128), f32),
            *half_acts,
            *half_acts,
        ],
        [
            seq_places,
            where,
            heads_own,
            heads_side,
            heads_core,
            heads_far,
            x_all.reshape(group_rows, width),
            out_full,
            vectors,
            mine,
            others,
        ],
        2**33,
        "feed_forward",
        spaces=[smem, smem] + [vmem] * 9,
    )
    result, d_second, d_branch_two, sums_two = local_call(
        second_kernel,
        [own_low, own_full, own_low, sums_out],
        [kept, seq_swap(sent, 1), out_grad, vectors],
        2**20,
        "second_norm",
    )
    d_branch_two, kept, sent, d_up, d_gate, d_up_other, d_gate_other = local_call(
        backward_kernel,
        [half_low, own_full, own_low] + [half_low] * 4,
        [
            where,
            d_branch_two,
            seq_swap(d_branch_two, 1),
            mine,
            others,
            acts[0],
            acts[1],
            acts[3],
            acts[4],
        ],
        2**33,
        "feed_back",
        spaces=[smem] + [vmem] * 8,
    )
    d_first, d_branch_one, sums_one = local_call(
        first_back_kernel,
        [own_full, own_low, sums_out],
        [kept, seq_swap(sent, 1), d_second, normed_one, rstd_one, vectors],
        2**20,
        "first_norm_back",
    )

    part = ((inner, half_rows), bf16)
    columns = ((half_rows, inner), bf16)
    d_heads_own, d_heads_sent, cols_own, cols_other = local_call(
        heads_back_kernel,
        [part, part, columns, columns],
        [where, d_branch_one, seq_swap(d_branch_one, 1), out_full],
        2**30,
        "heads_back",
        scratch=[pltpu.VMEM(*half_low)],
        spaces=[smem] + [vmem] * 3,
    )
    dox, d_heads_t = local_call(
        functools.partial(delta_kernel, heads),
        [wide_out, ((inner, group_rows), bf16)],
        [where, d_heads_own, seq_swap(d_heads_sent, 2), heads_n],
        block_flops // 4,
        "delta",
        spaces=[smem] + [vmem] * 3,
    )

    steps_out = [fsdp // 2] + [o for t in range(fsdp // 2 - 1, 0, -1) for o in (t, -t)] + [0]
    step_of = {o: i for i, o in enumerate(steps_out)}
    ring_rows = jnp.stack([ring_index(place + o, fsdp) for o in steps_out]).astype(jnp.int32)
    packed = ((fsdp, w_rows, own.shape[1]), bf16)
    cuts = [0, 3 * fsdp // 8, fsdp]
    grads_mine, *grads_other = local_call(
        grads_kernel,
        [packed] + [((b - a,) + packed[0][1:], bf16) for a, b in zip(cuts, cuts[1:])],
        [
            ring_rows,
            hidden_low,
            d_branch_two,
            heads_all,
            sums_one,
            sums_two,
            d_up,
            d_gate,
            acts[2],
            cols_own,
            d_up_other,
            d_gate_other,
            acts[5],
            cols_other,
        ],
        2**32,
        "grads",
        scratch=[pltpu.VMEM(*packed)],
        spaces=[smem] + [vmem] * 13,
    )
    got = [seq_swap(run, 2) for run in grads_other]

    def grads_part(offset):
        i = step_of[offset]
        which = sum(i >= cut for cut in cuts[1:])
        return grads_mine[i].astype(f32) + got[which][i - cuts[which]].astype(f32)


    d_query = jnp.zeros((inner, group_rows), f32)

    def back(offset, d_query, after):
        return local_call(
            functools.partial(back_kernel, heads, min(256, group_rows)),
            [((inner, group_rows), f32), ((2 * inner, group_rows), bf16)],
            [spots(offset), key_ext, qx, dox, queries, d_heads_t, d_query, *blocks[offset]],
            block_flops * 2,
            "attend_back",
            spaces=[smem] + [vmem] * (6 + len(blocks[offset])),
            after=after,
        )

    d_query, d_far = back(far, d_query, [])
    d_query, up = back(far - 1, d_query, [])
    d_query, down = back(1 - far, d_query, [])
    right, left = ring_shift(d_far[:inner], 1, SPAN), ring_shift(d_far[inner:], -1, SPAN)
    up = jnp.concatenate([up[:inner] + right, up[inner:]], axis=0)
    down = jnp.concatenate([down[:inner], down[inner:] + left], axis=0)
    after = [right, left]
    for t in range(far - 2, 0, -1):
        d_query, next_up = back(t, d_query, after)
        right, left = ring_shift(up, 1, SPAN), ring_shift(down, -1, SPAN)
        d_query, next_down = back(-t, d_query, [])
        up, down = next_up + right, next_down + left
        after = [right, left]
    last_up, last_down = up, down
    right, left = ring_shift(up, 1, SPAN), ring_shift(down, -1, SPAN)
    d_query, d_kv = back(0, d_query, after)
    (grads_far,) = local_call(
        far_kernel,
        [((w_rows, own.shape[1]), bf16)],
        [grads_mine[:1], got[0][:1]],
        2**20,
        "grads_far",
        after=[last_up, last_down],
    )
    grads_own = ring_scatter(grads_part, fsdp, grads_far).astype(bf16)
    grad_qkv, sent, kept = local_call(
        tail_kernel,
        [
            ((fsdp, w_rows, 3 * inner), bf16),
            ((2, tok_rows, width), bf16),
            ((2, tok_rows, width), f32),
        ],
        [
            ring_rows,
            where,
            d_query,
            d_kv,
            right,
            left,
            cosine,
            sine,
            x_all,
            qkv_full,
        ],
        2**32,
        "tail",
        scratch=[
            pltpu.VMEM((3 * inner, group_rows), bf16),
            pltpu.VMEM((fsdp, w_rows, 3 * inner), bf16),
        ],
        spaces=[smem, smem] + [vmem] * 8,
    )
    kept, sent = local_call(
        input_mid_kernel,
        [own_full, own_low],
        [where, kept, seq_swap(sent, 1)],
        2**20,
        "input_mid",
        spaces=[smem, vmem, vmem],
    )
    (d_input,) = local_call(
        input_end_kernel, [own_low], [d_first, kept, seq_swap(sent, 2)], 2**20, "input_end"
    )
    qkv_own_grad = ring_scatter(
        lambda offset: grad_qkv[step_of[offset]].astype(f32), fsdp
    ).astype(bf16)

    def seq_gather(value):
        other = seq_swap(value, 2)
        return [value, other, seq_swap(value, 1), seq_swap(other, 1)]

    (final_qkv,) = local_call(
        functools.partial(ordered_kernel, unpack_qkv_kernel, 4),
        [(w_qkv.shape, f32)],
        [seq_places, *seq_gather(qkv_own_grad)],
        2**20,
        "unpack_qkv",
        scratch=[pltpu.VMEM((groups, w_rows, 3 * inner), bf16)],
        spaces=[smem] + [vmem] * 4,
    )
    parts = seq_gather(grads_own)
    if aligned:
        final_up, final_gate, final_down, final_out, final_vectors = local_call(
            functools.partial(ordered_kernel, functools.partial(unpack_kernel, fsdp, width), 4),
            [
                (w_up.shape, f32),
                (w_gate.shape, f32),
                (w_down.shape, f32),
                (w_out.shape, f32),
                ((w_rows, spare), f32),
            ],
            [seq_places, *parts],
            2**20,
            "unpack",
            scratch=[pltpu.VMEM((groups,) + parts[0].shape, bf16)],
            spaces=[smem] + [vmem] * 4,
        )
    else:
        parts = arrange(parts, seq_order).astype(f32)

        def columns(at):
            value = parts[:, :, at : at + width].reshape(groups, w_rows, fsdp, w_rows)
            return value.transpose(1, 2, 0, 3).reshape(w_rows, groups * width)

        final_up, final_gate = columns(0), columns(width)
        final_down = parts[:, :, 2 * width : 3 * width].reshape(groups * w_rows, width)
        final_out = parts[:, :, 3 * width : 3 * width + inner].transpose(1, 0, 2)
        final_out = final_out.reshape(w_rows, width)
        final_vectors = jnp.sum(parts[:, :, 3 * width + inner :], axis=0)
    final_vectors = final_vectors[:, :4].T
    return (
        result,
        d_input,
        final_qkv,
        final_out,
        final_vectors[0],
        final_vectors[1],
        final_up,
        final_gate,
        final_down,
        final_vectors[2],
        final_vectors[3],
    )


def solution(mesh):
    rows = P(("fsdp", "seq"), None)
    param, vector = P("fsdp", None), P("fsdp")
    in_specs = (rows, rows, P(), param, param, vector, vector, param, param, param, vector, vector)
    out_specs = (rows, rows, param, param, vector, vector, param, param, param, vector, vector)
    return jax.shard_map(local, mesh=mesh, in_specs=in_specs, out_specs=out_specs, check_vma=False)
```

```python
import functools
import math

import jax
import jax.numpy as jnp
from jax import lax
from jax.experimental import pallas as pl
from jax.experimental.pallas import tpu as pltpu
from jax.sharding import PartitionSpec as P

HEADS = 12
HEAD_DIM = 64
SPAN = 8
EXT = 16
WIDE = HEAD_DIM + EXT
BIG = 2.0**30
SAFE_SUM = 2.0**100
VMEM = 40 * 2**20
SMALL = 16 * 2**20

bf16 = jnp.bfloat16
f32 = jnp.float32
norm_eps = 1e-12
base_log = math.log(1000.0)


def dot(left_op, right_op, left_dim, right_dim):
    return lax.dot_general(
        left_op, right_op, (((left_dim,), (right_dim,)), ((), ())), preferred_element_type=f32
    )


def ring_order(size):
    return list(range(0, size, 2)) + list(range(size - 1, 0, -2))


def ring_place(index, size):
    return jnp.where(index % 2 == 0, index // 2, size - 1 - index // 2)


def ring_index(place, size):
    place = place % size
    return jnp.where(place < size // 2, 2 * place, 2 * (size - 1 - place) + 1)


def ring_shift(value, step, size):
    order = ring_order(size)
    pairs = [
        (base + order[i], base + order[(i + step) % size])
        for base in range(0, lax.axis_size("fsdp"), size)
        for i in range(size)
    ]
    return lax.ppermute(value, "fsdp", pairs)


def seq_swap(value, mask):
    return lax.ppermute(value, "seq", [(i, i ^ mask) for i in range(lax.axis_size("seq"))])


def arrange_kernel(count, order, *refs):
    for i, ref in enumerate(refs[:count]):
        refs[-1][order[i]] = ref[...]


def arrange(blocks, order, after=()):
    return pl.pallas_call(
        functools.partial(arrange_kernel, len(blocks)),
        in_specs=[pl.BlockSpec(memory_space=pltpu.SMEM)]
        + [pl.BlockSpec(memory_space=pltpu.VMEM)] * len(blocks)
        + [pl.BlockSpec(memory_space=pl.ANY)] * len(after),
        out_specs=pl.BlockSpec(memory_space=pltpu.VMEM),
        out_shape=jax.ShapeDtypeStruct((len(blocks),) + blocks[0].shape, blocks[0].dtype),
        compiler_params=pltpu.CompilerParams(vmem_limit_bytes=SMALL),
        name="arrange",
    )(jnp.stack(order).astype(jnp.int32), *blocks, *after)


def arrange_runs_kernel(order, *refs):
    at = 0
    for ref in refs[:-1]:
        for k in range(ref.shape[0]):
            refs[-1][order[at]] = ref[k]
            at += 1


def arrange_runs(runs, order):
    return pl.pallas_call(
        arrange_runs_kernel,
        in_specs=[pl.BlockSpec(memory_space=pltpu.SMEM)]
        + [pl.BlockSpec(memory_space=pltpu.VMEM)] * len(runs),
        out_specs=pl.BlockSpec(memory_space=pltpu.VMEM),
        out_shape=jax.ShapeDtypeStruct((len(order),) + runs[0].shape[1:], runs[0].dtype),
        compiler_params=pltpu.CompilerParams(vmem_limit_bytes=VMEM),
        name="arrange_runs",
    )(jnp.stack(order).astype(jnp.int32), *runs)


def ring_gather(block, size, place):
    half = block.shape[0] // 2
    right, left = block, block
    blocks, order = [block], [ring_index(place, size)]
    for t in range(1, size // 2):
        right, left = ring_shift(right, 1, size), ring_shift(left, -1, size)
        blocks += [right, left]
        order += [ring_index(place - t, size), ring_index(place + t, size)]
    last = jnp.concatenate(
        [ring_shift(right[:half], 1, size), ring_shift(left[half:], -1, size)], axis=0
    )
    return blocks + [last], order + [ring_index(place + size // 2, size)]


def sum_kernel(counts, split, *refs):
    outs = refs[-len(counts) :]
    at = 0
    for which, (count, arrived) in enumerate(counts):
        blocks, got = refs[at : at + count], refs[at + count : at + count + arrived]
        at += count + arrived
        total = sum(ref[0].astype(f32) for ref in blocks)
        if split and arrived:
            half = total.shape[0] // 2
            cut = slice(0, half) if which == 0 else slice(half, 2 * half)
            other = slice(half, 2 * half) if which == 0 else slice(0, half)
            outs[which][cut, :] = (total[cut] + got[0][...].astype(f32)).astype(bf16)
            outs[which][other, :] = total[other].astype(bf16)
        else:
            total = total + sum(ref[...].astype(f32) for ref in got)
            outs[which][...] = total.astype(bf16)


def block_sums(directions, split, after):
    specs, ins = [], []
    for blocks, got in directions:
        for stacked, index in blocks:
            shape = (1,) + stacked.shape[1:]
            specs.append(pl.BlockSpec(shape, lambda _, index=index: (index, 0, 0)))
            ins.append(stacked)
        for value in got:
            specs.append(pl.BlockSpec(value.shape, lambda _: (0, 0)))
            ins.append(value)
    shape = directions[0][0][0][0].shape[1:]
    counts = [(len(blocks), len(got)) for blocks, got in directions]
    used = len(ins)

    def body(*refs):
        sum_kernel(counts, split, *refs[:used], *refs[used + len(after) :])

    return pl.pallas_call(
        body,
        grid=(1,),
        in_specs=specs + [pl.BlockSpec(memory_space=pl.ANY)] * len(after),
        out_specs=[pl.BlockSpec(shape, lambda _: (0, 0)) for _ in counts],
        out_shape=[jax.ShapeDtypeStruct(shape, bf16) for _ in counts],
        compiler_params=pltpu.CompilerParams(vmem_limit_bytes=SMALL),
        name="sums",
    )(*ins, *after)


def block_ref(ref):
    return ref[0].astype(f32)


def pair_kernel(split, *refs):
    directions, outs = (refs[:5], refs[5:10]), refs[10:]
    for which, (mine_ref, other_ref, got_ref, qkv_ref, qkv_got_ref) in enumerate(directions):
        out_ref = outs[which]
        rows, width = mine_ref.shape[1], mine_ref.shape[2]
        got = got_ref[:, :width].astype(f32)
        out_ref[:, :width] = (block_ref(mine_ref) + block_ref(other_ref) + got).astype(bf16)
        total = block_ref(qkv_ref)
        if split:
            half = rows // 2
            cut = slice(0, half) if which == 0 else slice(half, rows)
            rest = slice(half, rows) if which == 0 else slice(0, half)
            out_ref[cut, width:] = (total[cut] + qkv_got_ref[...].astype(f32)).astype(bf16)
            out_ref[rest, width:] = total[rest].astype(bf16)
        else:
            out_ref[:, width:] = (total + qkv_got_ref[:, width:].astype(f32)).astype(bf16)


def final_kernel(
    mine_ref, other_ref, right_ref, left_ref, up_ref, down_ref, out_ref, right_out, left_out
):
    width = mine_ref.shape[2]
    right, left = right_ref[...].astype(f32), left_ref[...].astype(f32)
    total = block_ref(mine_ref) + block_ref(other_ref) + right[:, :width] + left[:, :width]
    out_ref[...] = total.astype(bf16)
    right_out[...] = (block_ref(up_ref) + right[:, width:]).astype(bf16)
    left_out[...] = (block_ref(down_ref) + left[:, width:]).astype(bf16)


def block_call(kernel, outs, ins, name, after=()):
    specs, arrays = [], []
    for item in ins:
        if isinstance(item, tuple):
            stacked, index = item
            shape = (1,) + stacked.shape[1:]
            specs.append(pl.BlockSpec(shape, lambda _, index=index: (index, 0, 0)))
            arrays.append(stacked)
        else:
            specs.append(pl.BlockSpec(item.shape, lambda _: (0, 0)))
            arrays.append(item)
    used = len(arrays)

    def body(*refs):
        kernel(*refs[:used], *refs[used + len(after) :])

    return pl.pallas_call(
        body,
        grid=(1,),
        in_specs=specs + [pl.BlockSpec(memory_space=pl.ANY)] * len(after),
        out_specs=[pl.BlockSpec(shape, lambda _: (0, 0)) for shape in outs],
        out_shape=[jax.ShapeDtypeStruct(shape, bf16) for shape in outs],
        compiler_params=pltpu.CompilerParams(vmem_limit_bytes=SMALL),
        name=name,
    )(*arrays, *after)


def ring_scatter(blocks, size, after):
    after = {i: list(values) for i, values in enumerate(after)}
    (far,) = block_sums([(blocks(size // 2), [])], False, after.get(0, []))
    half = far.shape[0] // 2
    sent = [far]
    right = ring_shift(far[:half], 1, size)
    left = ring_shift(far[half:], -1, size)
    for hop, t in enumerate(range(size // 2 - 1, 0, -1)):
        up, down = block_sums(
            [(blocks(t), [right]), (blocks(-t), [left])], hop == 0, after.get(hop + 1, [])
        )
        right, left = ring_shift(up, 1, size), ring_shift(down, -1, size)
        sent.append(up)
    (total,) = block_sums([(blocks(0), [right, left])], False, after.get(size // 2, []))
    return total, sent


def three_parts(value):
    high = value.astype(bf16).astype(f32)
    rest = value - high
    mid = rest.astype(bf16).astype(f32)
    return high, mid, rest - mid


def with_parts(base, value):
    high, mid, low = three_parts(value)
    lane = lax.broadcasted_iota(jnp.int32, base.shape, 1)
    filled = jnp.where(lane == HEAD_DIM, high, base)
    filled = jnp.where(lane == HEAD_DIM + 1, mid, filled)
    return jnp.where(lane == HEAD_DIM + 2, low, filled)


def first_kernel(heads, tile, where_ref, ext_ref, qt_ref, qe_ref, kv_ref, qx_ref, acc_ref):
    tokens = qt_ref.shape[1]
    ones = jnp.ones((EXT, tokens), bf16)
    ext = block_ext(ext_ref, where_ref, 0, tokens)
    for h in range(heads):
        rows = slice(h * HEAD_DIM, (h + 1) * HEAD_DIM)
        k_rows, v_rows = block_rows([kv_ref], h)
        keys = jnp.concatenate([k_rows, ext], axis=0)
        vals = jnp.concatenate([v_rows, ones], axis=0)
        for start in range(0, tokens, tile):
            cut = slice(start, start + tile)
            natural = qt_ref[rows, cut].astype(f32).T
            queries = jnp.concatenate([natural, qe_ref[cut, :].astype(f32)], axis=1)
            scores = dot(queries.astype(bf16), keys, 1, 0)
            top = jnp.max(scores, axis=1, keepdims=True)
            weights = jnp.exp(scores - top).astype(bf16)
            acc_ref[h, :, cut] = dot(vals, weights, 1, 1)
            qx_ref[h, cut, :] = with_parts(queries, top).astype(bf16)


def block_rows(refs, h):
    if len(refs) == 2:
        rows = slice(h * HEAD_DIM, (h + 1) * HEAD_DIM)
        return refs[0][rows, :], refs[1][rows, :]
    inner = refs[0].shape[0] // 2
    return (
        refs[0][h * HEAD_DIM : (h + 1) * HEAD_DIM, :],
        refs[0][inner + h * HEAD_DIM : inner + (h + 1) * HEAD_DIM, :],
    )


def block_ext(ext_ref, where_ref, index, tokens):
    return ext_ref[:, pl.ds(pl.multiple_of(where_ref[index] * tokens, tokens), tokens)]


def step_kernel(heads, tile, parts, where_ref, ext_ref, qx_ref, acc_in, *refs):
    acc_ref, tokens = refs[-1], qx_ref.shape[1]
    ones = jnp.ones((EXT, tokens), bf16)
    blocks, at = [], 0
    for b, part in enumerate(parts):
        blocks.append((refs[at : at + part], block_ext(ext_ref, where_ref, b, tokens)))
        at += part
    for h in range(heads):
        pairs = []
        for block, ext in blocks:
            k_rows, v_rows = block_rows(block, h)
            pairs.append(
                (jnp.concatenate([k_rows, ext], axis=0), jnp.concatenate([v_rows, ones], axis=0))
            )
        for start in range(0, tokens, tile):
            cut = slice(start, start + tile)
            total = acc_in[h, :, cut]
            for keys, vals in pairs:
                weights = jnp.exp(dot(qx_ref[h, cut, :], keys, 1, 0)).astype(bf16)
                total = total + dot(vals, weights, 1, 1)
            acc_ref[h, :, cut] = total


def finish_kernel(heads, tile, parts, where_ref, ext_ref, qx_ref, acc_ref, *refs):
    count = sum(parts)
    blocks = refs[:count]
    ot_ref, on_ref, qx2_ref, buf, acc, qx = refs[count:]
    tokens = qx_ref.shape[1]
    inner = buf.shape[1] // 2
    fine = True
    for h in range(heads):
        sums = acc_ref[h, HEAD_DIM : HEAD_DIM + 8, :]
        fine = jnp.logical_and(fine, jnp.logical_and(sums <= SAFE_SUM, sums >= 0.5))
    good = jnp.min(jnp.where(fine, 1.0, 0.0)) > 0.5
    acc[...] = acc_ref[...]
    qx[...] = qx_ref[...]

    @pl.when(jnp.logical_not(good))
    def _():
        small = tile // 2
        ones = jnp.ones((EXT, tokens), bf16)
        lane = lax.broadcasted_iota(jnp.int32, (small, WIDE), 1)
        inside = jnp.logical_and(lane >= HEAD_DIM, lane < HEAD_DIM + 3)
        at = 0
        for b, part in enumerate(parts):
            if part == 2:
                pltpu.sync_copy(blocks[at], buf.at[b, pl.ds(0, inner)])
                pltpu.sync_copy(blocks[at + 1], buf.at[b, pl.ds(inner, inner)])
            else:
                pltpu.sync_copy(blocks[at], buf.at[b])
            at += part

        def each(body):
            cuts = tokens // small

            def turn(step, carry):
                b, rest = step // (heads * cuts), step % (heads * cuts)
                h = rest // cuts
                cut = pl.ds(pl.multiple_of(rest % cuts * small, small), small)
                rows = pl.multiple_of(h * HEAD_DIM, HEAD_DIM)
                ext = block_ext(ext_ref, where_ref, b, tokens)
                keys = jnp.concatenate([buf[b, pl.ds(rows, HEAD_DIM), :], ext], axis=0)
                vals = buf[b, pl.ds(pl.multiple_of(inner + rows, HEAD_DIM), HEAD_DIM), :]
                body(h, cut, keys, jnp.concatenate([vals, ones], axis=0))
                return carry

            lax.fori_loop(0, len(parts) * heads * cuts, turn, 0)

        def raise_top(h, cut, keys, vals):
            base = qx[h, cut, :].astype(f32)
            old = jnp.sum(jnp.where(inside, base, 0.0), axis=1, keepdims=True)
            plain = jnp.where(inside, 0.0, base)
            scores = dot(plain.astype(bf16), keys, 1, 0)
            top = jnp.maximum(old, jnp.max(scores, axis=1, keepdims=True))
            qx[h, cut, :] = with_parts(plain, top).astype(bf16)

        def add_up(h, cut, keys, vals):
            weights = jnp.exp(dot(qx[h, cut, :], keys, 1, 0)).astype(bf16)
            acc[h, :, cut] += dot(vals, weights, 1, 1)

        each(raise_top)
        acc[...] = jnp.zeros_like(acc)
        each(add_up)

    lane = lax.broadcasted_iota(jnp.int32, (tile, WIDE), 1)
    inside = jnp.logical_and(lane >= HEAD_DIM, lane < HEAD_DIM + 3)
    for h in range(heads):
        rows = slice(h * HEAD_DIM, (h + 1) * HEAD_DIM)
        for start in range(0, tokens, tile):
            cut = slice(start, start + tile)
            block = acc[h, :, cut]
            normed = block[:HEAD_DIM, :] * (1.0 / block[HEAD_DIM : HEAD_DIM + 1, :])
            ot_ref[rows, cut] = normed.astype(bf16)
            stacked = jnp.concatenate([normed, jnp.log(block[HEAD_DIM:, :])], axis=0).T
            on_ref[h, cut, :] = stacked[:, :HEAD_DIM]
            base = qx[h, cut, :].astype(f32)
            top = jnp.sum(jnp.where(inside, base, 0.0), axis=1, keepdims=True)
            shift = top + stacked[:, HEAD_DIM : HEAD_DIM + 1]
            qx2_ref[h, cut, :] = with_parts(base, shift).astype(bf16)


def delta_kernel(heads, where, own_ref, got_ref, on_ref, dox_ref, dot_ref):
    tokens = own_ref.shape[1]
    for tile in range(2):
        cut = slice(tile * tokens, (tile + 1) * tokens)

        @pl.when(where[0] == tile)
        def _():
            dot_ref[:, cut] = own_ref[...]

        @pl.when(where[0] != tile)
        def _():
            dot_ref[:, cut] = got_ref[...]

        for h in range(heads):
            rows = slice(h * HEAD_DIM, (h + 1) * HEAD_DIM)
            natural = dot_ref[rows, cut].astype(f32).T
            delta = jnp.sum(natural * on_ref[h, cut, :], axis=1, keepdims=True)
            base = jnp.concatenate([natural, jnp.zeros((tokens, EXT), f32)], axis=1)
            dox_ref[h, cut, :] = with_parts(base, delta).astype(bf16)


def back_kernel(heads, q_tile, where_ref, ext_ref, qx_ref, dox_ref, qt_ref, dot_ref, dq_in, *refs):
    block, (dq_ref, dkv_ref) = refs[:-2], refs[-2:]
    tokens, inner = qt_ref.shape[1], qt_ref.shape[0]
    ext = block_ext(ext_ref, where_ref, 0, tokens)
    for h in range(heads):
        rows = slice(h * HEAD_DIM, (h + 1) * HEAD_DIM)
        k_rows, v_rows = block_rows(block, h)
        keys = jnp.concatenate([k_rows, ext], axis=0)
        vals = jnp.concatenate([v_rows, ext], axis=0)
        d_key, d_value = 0.0, 0.0
        for start in range(0, tokens, q_tile):
            cut = slice(start, start + q_tile)
            weights = jnp.exp(dot(qx_ref[h, cut, :], keys, 1, 0))
            shifted = dot(dox_ref[h, cut, :], vals, 1, 0)
            d_scores = (weights * shifted).astype(bf16)
            d_value = d_value + dot(dot_ref[rows, cut], weights.astype(bf16), 1, 0)
            d_key = d_key + dot(qt_ref[rows, cut], d_scores, 1, 0)
            dq_ref[rows, cut] = dq_in[rows, cut] + dot(k_rows, d_scores, 1, 1)
        dkv_ref[rows, :] = d_key.astype(bf16)
        dkv_ref[inner + h * HEAD_DIM : inner + (h + 1) * HEAD_DIM, :] = d_value.astype(bf16)


def pack_kernel(parts, s_ref, up_ref, gate_ref, down_ref, last_ref, *refs):
    vectors, out_ref = refs[:4], refs[4]
    s = s_ref[0]
    rows = up_ref.shape[0]
    width = parts * rows
    for i, ref in enumerate((up_ref, gate_ref)):
        pieces = []
        for k in range(parts):
            run = ref[:, 4 * rows * k : 4 * rows * (k + 1)]
            pieces.append(pltpu.roll(run, (4 * rows - s * rows) % (4 * rows), 1)[:, :rows])
        out_ref[:, i * width : (i + 1) * width] = jnp.concatenate(pieces, axis=1).astype(bf16)
    own = down_ref[pl.ds(pl.multiple_of(s * rows, 8), rows), :]
    out_ref[:, 2 * width : 3 * width] = own.astype(bf16)
    inner = width // 4
    columns = pltpu.roll(last_ref[...], (width - s * inner) % width, 1)[:, :inner]
    spare = out_ref.shape[1] - 3 * width - inner
    side = jnp.concatenate([ref[...] for ref in vectors] + [jnp.zeros((4, rows), f32)], axis=0).T
    out_ref[:, 3 * width :] = jnp.concatenate(
        [columns, side, jnp.zeros((rows, spare - 8), f32)], axis=1
    ).astype(bf16)


def unpack_kernel(parts, width, *refs):
    quarters, (up_ref, gate_ref, down_ref, out_ref, vec_ref) = refs[:4], refs[4:]
    rows = up_ref.shape[0]
    inner = width // 4
    for i, ref in enumerate((up_ref, gate_ref)):
        for k in range(parts):
            at = i * width + k * rows
            ref[:, 4 * rows * k : 4 * rows * (k + 1)] = jnp.concatenate(
                [q[:, at : at + rows].astype(f32) for q in quarters], axis=1
            )
    for g, q in enumerate(quarters):
        down_ref[g * rows : (g + 1) * rows, :] = q[:, 2 * width : 3 * width].astype(f32)
    at = 3 * width
    out_ref[...] = jnp.concatenate([q[:, at : at + inner].astype(f32) for q in quarters], axis=1)
    vec_ref[...] = sum(q[:, at + inner :].astype(f32) for q in quarters)


def ordered_kernel(kernel, count, order, *refs):
    buffer = refs[-1]
    for i in range(count):
        buffer[order[i]] = refs[i][...]
    kernel(*[buffer.at[i] for i in range(count)], *refs[count:-1])


def grads_kernel(order, hidden_ref, branch_ref, heads_ref, first_sums, second_sums, *refs):
    sides, mine_ref, runs, buffer = (refs[:4], refs[4:8]), refs[8], refs[9:-1], refs[-1]
    count, rows = mine_ref.shape[0], mine_ref.shape[1]
    width = hidden_ref.shape[1]
    hidden_t = hidden_ref[...].T
    heads = heads_ref[...].reshape(width, heads_ref.shape[2])
    vectors = (first_sums[...] + second_sums[...]).T
    vectors = jnp.concatenate(
        [vectors, jnp.zeros((width, mine_ref.shape[2] - 3 * width - width // 4 - 8), f32)], axis=1
    ).astype(bf16)
    for which, (up_ref, gate_ref, inner_ref, cols_ref) in enumerate(sides):

        def put(value, at):
            for k in range(count):
                buffer[k, :, at : at + value.shape[1]] = value[k * rows : (k + 1) * rows]

        put(dot(hidden_t, up_ref[...], 1, 0).astype(bf16), 0)
        put(dot(hidden_t, gate_ref[...], 1, 0).astype(bf16), width)
        put(dot(inner_ref[...].T, branch_ref[...], 1, 0).astype(bf16), 2 * width)
        tail = dot(heads, cols_ref[...], 1, 0).astype(bf16)
        rest = vectors if which == 0 else jnp.zeros_like(vectors)
        put(jnp.concatenate([tail, rest], axis=1), 3 * width)
        if which == 0:
            for i in range(count):
                mine_ref[i] = buffer[order[i]]
        else:
            at = 0
            for run in runs:
                for k in range(run.shape[0]):
                    run[k] = buffer[order[at]]
                    at += 1


def tail_kernel(
    order, where, dq_ref, dkv_ref, right_ref, left_ref, cos_ref, sin_ref, x_ref, w_ref, *refs
):
    grad_ref, sent_ref, kept_ref, raw, buffer = refs
    inner = dq_ref.shape[0]
    cosine, sine = cos_ref[...], sin_ref[...]
    d_kv = dkv_ref[...].astype(f32) + right_ref[...].astype(f32) + left_ref[...].astype(f32)

    def put(base):
        def at_base(at, value):
            raw[base + at : base + at + value.shape[0], :] = value.astype(bf16)

        return at_base

    turn_rows(dq_ref[...] * HEAD_DIM**-0.5, cosine, -sine, put(0))
    turn_rows(d_kv[:inner], cosine, -sine, put(inner))
    raw[2 * inner :, :] = d_kv[inner:].astype(bf16)
    projected = raw[...].T
    count, rows = grad_ref.shape[0], grad_ref.shape[1]
    width, quarter = x_ref.shape[2], x_ref.shape[1]
    terms = dot(projected, w_ref[...].reshape(width, 3 * inner), 1, 1)
    for core in range(2):
        side = [terms[(2 * y + core) * quarter : (2 * y + core + 1) * quarter] for y in range(2)]

        @pl.when(where[1] == core)
        def _():
            for y in range(2):
                kept_ref[y] = side[y]

        @pl.when(where[1] != core)
        def _():
            for y in range(2):
                sent_ref[y] = side[y].astype(bf16)

    grad = dot(x_ref[...].reshape(4 * quarter, width).T, projected, 1, 0).astype(bf16)
    for k in range(count):
        buffer[k] = grad[k * rows : (k + 1) * rows]
    for i in range(count):
        grad_ref[i] = buffer[order[i]]


def unpack_qkv_kernel(*refs):
    quarters, out_ref = refs[:4], refs[4]
    inner = quarters[0].shape[1] // 3
    out_ref[...] = jnp.concatenate(
        [q[:, i * inner : (i + 1) * inner].astype(f32) for i in range(3) for q in quarters], axis=1
    )


def tables_kernel(at_ref, docs_ref, key_ref, query_ref):
    length, tokens = key_ref.shape[1], query_ref.shape[0]

    def kinds(start, count):
        docs = docs_ref[:, pl.ds(pl.multiple_of(start, count), count)] - at_ref[1]
        docs = jnp.broadcast_to(docs, (EXT, count))
        row = lax.broadcasted_iota(jnp.int32, (EXT, count), 0)
        return row, docs == row - 3

    row, same = kinds(at_ref[0], length)
    mark = jnp.where(jnp.logical_or(row < 3, jnp.logical_not(same)), -1.0, 0.0)
    key_ref[...] = jnp.where(row < 6, mark, 0.0).astype(bf16)
    row, same = kinds(at_ref[2], tokens)
    inside = jnp.logical_and(same, jnp.logical_and(row >= 3, row < 6))
    query_ref[...] = jnp.where(inside, BIG, 0.0).T.astype(bf16)


def turn_rows(value, cosine, sine, put):
    half = HEAD_DIM // 2
    for at in range(0, value.shape[0], HEAD_DIM):
        lead, last = value[at : at + half], value[at + half : at + HEAD_DIM]
        put(at, lead * cosine - last * sine)
        put(at + half, last * cosine + lead * sine)


def project_kernel(count, order, places, cos_ref, sin_ref, *refs):
    weights, tokens = refs[:count], refs[count : count + 4]
    q_ref, kv_ref, x_ref, w_ref = refs[count + 4 :]
    inner = q_ref.shape[0]
    for i, ref in enumerate(weights):
        w_ref[order[i]] = ref[...]
    for i, ref in enumerate(tokens):
        x_ref[places[i]] = ref[...]
    cosine, sine = cos_ref[...], sin_ref[...]
    width = x_ref.shape[2]
    matrix = w_ref[...].reshape(width, 3 * inner).T
    rows = x_ref[...].reshape(-1, width)

    def put_q(at, value):
        q_ref[at : at + value.shape[0], :] = value.astype(bf16) * bf16(HEAD_DIM**-0.5)

    def put_k(at, value):
        kv_ref[at : at + value.shape[0], :] = value.astype(bf16)

    turn_rows(dot(matrix[:inner], rows, 1, 1), cosine, sine, put_q)
    turn_rows(dot(matrix[inner : 2 * inner], rows, 1, 1), cosine, sine, put_k)
    kv_ref[inner:, :] = dot(matrix[2 * inner :], rows, 1, 1).astype(bf16)


def outer_kernel(places, *refs):
    parts, (out_ref, vec_ref, buffer) = refs[:4], refs[4:]
    inner = out_ref.shape[1] // 4
    for i, ref in enumerate(parts):
        buffer[places[i]] = ref[...]
    out_ref[...] = jnp.concatenate([buffer[g, :, :inner] for g in range(4)], axis=1)
    vec_ref[...] = parts[0][:, inner:].astype(f32).T[:8]


def gate(value, after):
    return pl.pallas_call(
        lambda *refs: None,
        in_specs=[pl.BlockSpec(memory_space=pl.ANY)] * (1 + len(after)),
        out_specs=pl.BlockSpec(memory_space=pl.ANY),
        out_shape=jax.ShapeDtypeStruct(value.shape, value.dtype),
        input_output_aliases={0: 0},
        name="gate",
    )(value, *after)


def norm_parts(rows_in):
    centre = rows_in - jnp.mean(rows_in, axis=-1, keepdims=True)
    rstd = lax.rsqrt(jnp.mean(centre * centre, axis=-1, keepdims=True) + norm_eps)
    return centre * rstd, rstd


def norm_grad(normed, rstd, grad, gain):
    scaled = grad * gain
    mean = jnp.mean(scaled, axis=-1, keepdims=True)
    return rstd * (scaled - mean - normed * jnp.mean(scaled * normed, axis=-1, keepdims=True))


def ff_weights(ref):
    width = ref.shape[0]
    return ref[:, :width], ref[:, width : 2 * width], ref[:, 2 * width : 3 * width]


def forward_kernel(places, where, *refs):
    parts, (x_ref, out_ref, vec_ref, mine_ref, other_ref) = refs[:4], refs[4:9]
    heads_ref, hidden_ref, kept_ref, sent_ref, normed_ref, rstd_ref = refs[9:15]
    acts = (refs[15:18], refs[18:21])
    width, rows = hidden_ref.shape[1], kept_ref.shape[0]
    side, core = where[0], where[1]
    for i, ref in enumerate(parts):
        heads_ref[places[i]] = ref[...]
    for tile in range(2):
        cut = slice(tile * rows, (tile + 1) * rows)
        start = pl.multiple_of((2 * side + tile) * rows, rows)
        heads = heads_ref[:, :, cut].reshape(width, rows).T
        first = x_ref[pl.ds(start, rows), :].astype(f32) + dot(heads, out_ref[...], 1, 0)
        normed, rstd = norm_parts(first)
        hidden = normed * vec_ref[0:1] + vec_ref[1:2]
        low = hidden.astype(bf16)
        hidden_ref[cut, :] = low
        branch = 0.0
        for w_ref, (up_ref, gate_ref, inner_ref) in zip((mine_ref, other_ref), acts):
            up_w, gate_w, down_w = ff_weights(w_ref)
            up, gate = dot(low, up_w, 1, 0), dot(low, gate_w, 1, 0)
            inner = (gate * lax.logistic(gate) * up).astype(bf16)
            up_ref[cut, :], gate_ref[cut, :], inner_ref[cut, :] = up, gate, inner
            branch = branch + dot(inner, down_w, 1, 0)

        @pl.when(core == tile)
        def _():
            kept_ref[...] = hidden + branch
            normed_ref[...] = normed
            rstd_ref[...] = jnp.broadcast_to(rstd, rstd_ref.shape)

        @pl.when(core != tile)
        def _():
            sent_ref[...] = branch.astype(bf16)


def second_kernel(kept_ref, got_ref, grad_ref, vec_ref, result_ref, d_ref, low_ref, sums_ref):
    normed, rstd = norm_parts(kept_ref[...] + got_ref[...].astype(f32))
    gain = vec_ref[2:3]
    result_ref[...] = (normed * gain + vec_ref[3:4]).astype(bf16)
    grad = grad_ref[...].astype(f32)
    d_second = norm_grad(normed, rstd, grad, gain)
    d_ref[...] = d_second
    low_ref[...] = d_second.astype(bf16)
    sums_ref[...] = jnp.zeros_like(sums_ref)
    sums_ref[2:3] = jnp.sum(grad * normed, axis=0, keepdims=True)
    sums_ref[3:4] = jnp.sum(grad, axis=0, keepdims=True)


def backward_kernel(where, own_ref, got_ref, mine_ref, other_ref, *refs):
    acts = (refs[:2], refs[2:4])
    branch_ref, kept_ref, sent_ref = refs[4:7]
    outs = (refs[7:9], refs[9:11])
    rows, core = kept_ref.shape[0], where[1]
    branch_ref[pl.ds(pl.multiple_of(core * rows, rows), rows), :] = own_ref[...]
    branch_ref[pl.ds(pl.multiple_of((1 - core) * rows, rows), rows), :] = got_ref[...]
    for tile in range(2):
        cut = slice(tile * rows, (tile + 1) * rows)
        branch = branch_ref[cut, :]
        total = 0.0
        for w_ref, (up_ref, gate_ref), (d_up_ref, d_gate_ref) in zip(
            (mine_ref, other_ref), acts, outs
        ):
            up_w, gate_w, down_w = ff_weights(w_ref)
            d_inner = dot(branch, down_w, 1, 1)
            up, gate = up_ref[cut, :], gate_ref[cut, :]
            sig = lax.logistic(gate)
            d_gate = (d_inner * up * sig * (1.0 + gate * (1.0 - sig))).astype(bf16)
            d_up = (d_inner * gate * sig).astype(bf16)
            d_up_ref[cut, :], d_gate_ref[cut, :] = d_up, d_gate
            total = total + dot(d_up, up_w, 1, 1) + dot(d_gate, gate_w, 1, 1)

        @pl.when(core == tile)
        def _():
            kept_ref[...] = total

        @pl.when(core != tile)
        def _():
            sent_ref[...] = total.astype(bf16)


def first_back_kernel(
    kept_ref, got_ref, d_second_ref, normed_ref, rstd_ref, vec_ref, d_ref, low_ref, sums_ref
):
    d_hidden = d_second_ref[...] + kept_ref[...] + got_ref[...].astype(f32)
    normed = normed_ref[...]
    d_first = norm_grad(normed, rstd_ref[:, 0:1], d_hidden, vec_ref[0:1])
    d_ref[...] = d_first
    low_ref[...] = d_first.astype(bf16)
    sums_ref[...] = jnp.zeros_like(sums_ref)
    sums_ref[0:1] = jnp.sum(d_hidden * normed, axis=0, keepdims=True)
    sums_ref[1:2] = jnp.sum(d_hidden, axis=0, keepdims=True)


def heads_back_kernel(
    where, own_ref, got_ref, out_ref, own_heads_ref, sent_ref, own_cols_ref, other_cols_ref, branch
):
    side, core = where[0], where[1]
    rows, inner = own_ref.shape[0], sent_ref.shape[0]
    branch[pl.ds(pl.multiple_of(core * rows, rows), rows), :] = own_ref[...]
    branch[pl.ds(pl.multiple_of((1 - core) * rows, rows), rows), :] = got_ref[...]
    for which, ref in ((1 - side, sent_ref), (side, own_heads_ref)):
        at = pl.multiple_of((2 * which + core) * inner, inner)
        ref[...] = dot(out_ref[pl.ds(at, inner), :], branch[...], 1, 1).astype(bf16)
    for group in range(4):
        value = branch[:, group * inner : (group + 1) * inner]

        @pl.when(2 * side + core == group)
        def _():
            own_cols_ref[...] = value

        @pl.when(2 * (1 - side) + core == group)
        def _():
            other_cols_ref[...] = value


def input_mid_kernel(where, kept_ref, got_ref, kept_out, sent_out):
    for y in range(2):
        value = kept_ref[y] + got_ref[y].astype(f32)

        @pl.when(where[0] == y)
        def _():
            kept_out[...] = value

        @pl.when(where[0] != y)
        def _():
            sent_out[...] = value.astype(bf16)


def input_end_kernel(first_ref, kept_ref, got_ref, out_ref):
    out_ref[...] = (first_ref[...] + kept_ref[...] + got_ref[...].astype(f32)).astype(bf16)


def local_call(kernel, outs, ins, flops, name, scratch=(), spaces=None, after=()):
    spaces = list(spaces or [pltpu.VMEM] * len(ins))
    count = len(ins)

    def body(*refs):
        kernel(*refs[:count], *refs[count + len(after) :])

    return pl.pallas_call(
        body,
        in_specs=[pl.BlockSpec(memory_space=space) for space in spaces + [pl.ANY] * len(after)],
        out_specs=[pl.BlockSpec(memory_space=pltpu.VMEM) for _ in outs],
        out_shape=[jax.ShapeDtypeStruct(shape, dtype) for shape, dtype in outs],
        scratch_shapes=list(scratch),
        compiler_params=pltpu.CompilerParams(vmem_limit_bytes=VMEM),
        cost_estimate=pl.CostEstimate(flops=flops * 5, bytes_accessed=2**20, transcendentals=0),
        name=name,
    )(*ins, *after)


def local(
    layer_input,
    out_grad,
    doc_ids,
    w_qkv,
    w_out,
    norm1_gain,
    norm1_bias,
    w_up,
    w_gate,
    w_down,
    norm2_gain,
    norm2_bias,
):
    fsdp = lax.axis_size("fsdp")
    groups = lax.axis_size("seq")
    f = lax.axis_index("fsdp")
    s = lax.axis_index("seq")
    side, core = s // 2, s % 2
    tok_rows, width = layer_input.shape
    w_rows = w_qkv.shape[0]
    inner = width // groups
    heads = inner // HEAD_DIM
    group_rows = tok_rows * groups
    half_rows = group_rows // 2
    length = SPAN * group_rows
    place = ring_place(f, fsdp)
    spot = ring_place(f % SPAN, SPAN)
    base = f // SPAN * SPAN

    seq_order = [s, s ^ 2, s ^ 1, s ^ 3]
    seq_places = jnp.stack(seq_order).astype(jnp.int32)
    where = jnp.stack([side, core]).astype(jnp.int32)
    smem, vmem = pltpu.SMEM, pltpu.VMEM
    aligned = w_rows * groups % 128 == 0 and w_rows % 16 == 0

    def quarter(matrix, start):
        return lax.dynamic_slice_in_dim(matrix, start + s * inner, inner, 1)

    qkv_own = jnp.concatenate([quarter(w_qkv, i * width) for i in range(3)], axis=1).astype(bf16)
    x_side = seq_swap(layer_input, 2)
    x_core = seq_swap(layer_input, 1)
    x_far = seq_swap(x_side, 1)
    qkv_blocks, order = ring_gather(qkv_own, fsdp, place)
    early, qkv_second = qkv_blocks[-3:-1], qkv_blocks[3:5]
    ring_order_now = jnp.stack(order).astype(jnp.int32)
    if not aligned:
        qkv_blocks = [arrange(qkv_blocks, order).reshape(width, 3 * inner)]
        ring_order_now = jnp.zeros((1,), jnp.int32)
    key_ext, query_ext = local_call(
        tables_kernel,
        [((EXT, length), bf16), ((group_rows, EXT), bf16)],
        [
            jnp.stack([f // SPAN * length, f // SPAN * 3, f * group_rows]).astype(jnp.int32),
            doc_ids[None, :],
        ],
        2**20,
        "tables",
        spaces=[smem, vmem],
        after=[*early, x_core, x_far],
    )
    positions = f % SPAN * group_rows + jnp.arange(group_rows, dtype=jnp.int32)
    steps = jnp.arange(HEAD_DIM // 2, dtype=f32)
    freqs = jnp.exp(steps * (-2.0 * base_log / HEAD_DIM))
    angles = freqs[:, None] * positions.astype(f32)[None, :]
    cosine, sine = jnp.cos(angles), jnp.sin(angles)

    queries, own_kv, x_all, qkv_full = local_call(
        functools.partial(project_kernel, len(qkv_blocks)),
        [
            ((inner, group_rows), bf16),
            ((2 * inner, group_rows), bf16),
            ((groups, tok_rows, width), bf16),
            ((len(qkv_blocks),) + qkv_blocks[0].shape, bf16),
        ],
        [
            ring_order_now,
            seq_places,
            cosine,
            sine,
            *qkv_blocks,
            layer_input,
            x_side,
            x_core,
            x_far,
        ],
        2**32,
        "project",
        spaces=[smem, smem] + [vmem] * (len(qkv_blocks) + 6),
    )

    def ff_quarter(matrix):
        split = matrix.reshape(w_rows, fsdp, groups, w_rows)
        return lax.dynamic_index_in_dim(split, s, 2, False).reshape(w_rows, width)

    spare = 256 - inner % 256
    packed_width = 3 * width + inner + spare
    if aligned:
        (own,) = local_call(
            functools.partial(pack_kernel, fsdp),
            [((w_rows, packed_width), bf16)],
            [
                s.reshape(1),
                w_up,
                w_gate,
                w_down,
                w_out,
                *[v[None, :] for v in (norm1_gain, norm1_bias, norm2_gain, norm2_bias)],
            ],
            2**20,
            "pack",
            spaces=[smem] + [vmem] * 8,
            after=[*qkv_second, x_core, x_far],
        )
    else:
        down_rows = lax.dynamic_slice_in_dim(w_down, s * w_rows, w_rows, 0)
        gains = jnp.stack([norm1_gain, norm1_bias, norm2_gain, norm2_bias], axis=1)
        own = jnp.concatenate(
            [
                ff_quarter(w_up),
                ff_quarter(w_gate),
                down_rows,
                quarter(w_out, 0),
                gains,
                jnp.zeros((w_rows, spare - 4), f32),
            ],
            axis=1,
        ).astype(bf16)
    mine, order = ring_gather(own, fsdp, place)
    steady = [jnp.int32(i) for i in range(fsdp)]
    others = [seq_swap(own, 2)[None]]
    for start in range(1, fsdp, 2):
        run = mine[start : start + 2]
        others.append(seq_swap(arrange(run, steady[: len(run)], others[-1:]), 2))
    others = arrange_runs(others, order).reshape(width, own.shape[1])
    mine = arrange(mine, order).reshape(width, own.shape[1])
    out_own, out_side = mine[:, 3 * width :], others[:, 3 * width :]
    out_core, out_far = seq_swap(out_own, 1), seq_swap(out_side, 1)
    out_full, vectors = local_call(
        outer_kernel,
        [((width, width), bf16), ((8, width), f32)],
        [seq_places, out_own, out_side, out_core, out_far],
        2**20,
        "outer",
        scratch=[pltpu.VMEM((groups,) + out_own.shape, bf16)],
        spaces=[smem] + [vmem] * 4,
    )

    def spots(*offsets):
        return jnp.stack([ring_index(spot + o, SPAN) for o in offsets]).astype(jnp.int32)

    block_flops = 8 * 256 * heads * group_rows * group_rows
    acc_out = ((heads, WIDE, group_rows), f32)
    wide_out = ((heads, group_rows, WIDE), bf16)
    tile = min(512, group_rows)
    qx, acc = local_call(
        functools.partial(first_kernel, heads, tile),
        [wide_out, acc_out],
        [spots(0), key_ext, queries, query_ext, own_kv],
        block_flops,
        "attend_own",
        spaces=[smem] + [vmem] * 4,
    )
    far = SPAN // 2
    blocks = {0: (own_kv,)}
    right, left = own_kv, own_kv
    for t in range(1, far + 1):
        if t < far:
            right, left = ring_shift(right, 1, SPAN), ring_shift(left, -1, SPAN)
            blocks[-t], blocks[t] = (right,), (left,)
            now = [-t, t]
        else:
            blocks[t] = (ring_shift(right[:inner], 1, SPAN), ring_shift(left[inner:], -1, SPAN))
            now = [t]
        refs = [ref for o in now for ref in blocks[o]]
        (acc,) = local_call(
            functools.partial(step_kernel, heads, tile, [len(blocks[o]) for o in now]),
            [acc_out],
            [spots(*now), key_ext, qx, acc, *refs],
            block_flops * len(now),
            "attend_step",
            spaces=[smem] + [vmem] * (3 + len(refs)),
            after=[mine] if t == far - 1 else [],
        )
    offsets = sorted(blocks)
    refs = [ref for o in offsets for ref in blocks[o]]
    heads_t, heads_n, qx = local_call(
        functools.partial(
            finish_kernel, heads, min(512, group_rows), [len(blocks[o]) for o in offsets]
        ),
        [((inner, group_rows), bf16), ((heads, group_rows, HEAD_DIM), f32), wide_out],
        [spots(*offsets), key_ext, qx, acc, *refs],
        block_flops // 4,
        "attend_finish",
        scratch=[
            pltpu.VMEM((SPAN, 2 * inner, group_rows), bf16),
            pltpu.VMEM(*acc_out),
            pltpu.VMEM(*wide_out),
        ],
        spaces=[smem] + [vmem] * 3 + [pl.ANY] * len(refs),
        after=[out_full],
    )

    def my_half(value, axis):
        return lax.dynamic_slice_in_dim(value, side * half_rows, half_rows, axis)

    def other_half(value, axis):
        return lax.dynamic_slice_in_dim(value, (1 - side) * half_rows, half_rows, axis)

    heads_own = my_half(heads_t, 1)
    heads_side = seq_swap(other_half(heads_t, 1), 2)
    heads_core = seq_swap(heads_own, 1)
    heads_far = seq_swap(heads_side, 1)
    half_low = ((half_rows, width), bf16)
    half_acts = [((half_rows, width), f32)] * 2 + [half_low]
    own_low, own_full = ((tok_rows, width), bf16), ((tok_rows, width), f32)
    sums_out = ((8, width), f32)
    heads_all, hidden_low, kept, sent, normed_one, rstd_one, *acts = local_call(
        forward_kernel,
        [
            ((groups, inner, half_rows), bf16),
            half_low,
            own_full,
            own_low,
            own_full,
            ((tok_rows, 128), f32),
            *half_acts,
            *half_acts,
        ],
        [
            seq_places,
            where,
            heads_own,
            heads_side,
            heads_core,
            heads_far,
            x_all.reshape(group_rows, width),
            out_full,
            vectors,
            mine,
            others,
        ],
        2**33,
        "feed_forward",
        spaces=[smem, smem] + [vmem] * 9,
    )
    result, d_second, d_branch_two, sums_two = local_call(
        second_kernel,
        [own_low, own_full, own_low, sums_out],
        [kept, seq_swap(sent, 1), out_grad, vectors],
        2**20,
        "second_norm",
    )
    d_branch_two, kept, sent, d_up, d_gate, d_up_other, d_gate_other = local_call(
        backward_kernel,
        [half_low, own_full, own_low] + [half_low] * 4,
        [
            where,
            d_branch_two,
            seq_swap(d_branch_two, 1),
            mine,
            others,
            acts[0],
            acts[1],
            acts[3],
            acts[4],
        ],
        2**33,
        "feed_back",
        spaces=[smem] + [vmem] * 8,
    )
    d_first, d_branch_one, sums_one = local_call(
        first_back_kernel,
        [own_full, own_low, sums_out],
        [kept, seq_swap(sent, 1), d_second, normed_one, rstd_one, vectors],
        2**20,
        "first_norm_back",
    )

    part = ((inner, half_rows), bf16)
    columns = ((half_rows, inner), bf16)
    d_heads_own, d_heads_sent, cols_own, cols_other = local_call(
        heads_back_kernel,
        [part, part, columns, columns],
        [where, d_branch_one, seq_swap(d_branch_one, 1), out_full],
        2**30,
        "heads_back",
        scratch=[pltpu.VMEM(*half_low)],
        spaces=[smem] + [vmem] * 3,
    )
    dox, d_heads_t = local_call(
        functools.partial(delta_kernel, heads),
        [wide_out, ((inner, group_rows), bf16)],
        [where, d_heads_own, seq_swap(d_heads_sent, 2), heads_n],
        block_flops // 4,
        "delta",
        spaces=[smem] + [vmem] * 3,
    )

    steps_out = [fsdp // 2] + [o for t in range(fsdp // 2 - 1, 0, -1) for o in (t, -t)] + [0]
    step_of = {o: i for i, o in enumerate(steps_out)}
    ring_rows = jnp.stack([ring_index(place + o, fsdp) for o in steps_out]).astype(jnp.int32)
    packed = ((fsdp, w_rows, own.shape[1]), bf16)
    cuts = [0, 3 * fsdp // 8, fsdp]
    grads_mine, *grads_other = local_call(
        grads_kernel,
        [packed] + [((b - a,) + packed[0][1:], bf16) for a, b in zip(cuts, cuts[1:])],
        [
            ring_rows,
            hidden_low,
            d_branch_two,
            heads_all,
            sums_one,
            sums_two,
            d_up,
            d_gate,
            acts[2],
            cols_own,
            d_up_other,
            d_gate_other,
            acts[5],
            cols_other,
        ],
        2**32,
        "grads",
        scratch=[pltpu.VMEM(*packed)],
        spaces=[smem] + [vmem] * 13,
    )

    got = [seq_swap(run, 2) for run in grads_other]

    def grads_part(offset):
        i = step_of[offset]
        which = sum(i >= cut for cut in cuts[1:])
        return [(grads_mine, i), (got[which], i - cuts[which])]

    d_query = jnp.zeros((inner, group_rows), f32)

    def back(offset, d_query, after):
        return local_call(
            functools.partial(back_kernel, heads, min(256, group_rows)),
            [((inner, group_rows), f32), ((2 * inner, group_rows), bf16)],
            [spots(offset), key_ext, qx, dox, queries, d_heads_t, d_query, *blocks[offset]],
            block_flops * 2,
            "attend_back",
            spaces=[smem] + [vmem] * (6 + len(blocks[offset])),
            after=after,
        )

    d_query, d_far = back(far, d_query, [])
    d_query, up = back(far - 1, d_query, [])
    d_query, down = back(1 - far, d_query, [])
    right, left = ring_shift(d_far[:inner], 1, SPAN), ring_shift(d_far[inner:], -1, SPAN)
    up = jnp.concatenate([up[:inner] + right, up[inner:]], axis=0)
    down = jnp.concatenate([down[:inner], down[inner:] + left], axis=0)
    after = [right, left]
    for t in range(far - 2, 0, -1):
        d_query, next_up = back(t, d_query, after)
        right, left = ring_shift(up, 1, SPAN), ring_shift(down, -1, SPAN)
        d_query, next_down = back(-t, d_query, [])
        after = [right, left]
        up, down = next_up + right, next_down + left
    right, left = ring_shift(up, 1, SPAN), ring_shift(down, -1, SPAN)
    d_query, d_kv = back(0, d_query, after)
    grads_sent = []
    if fsdp == SPAN:
        half = w_rows // 2
        (grads_far,) = block_sums([(grads_part(far), [])], False, [])
        up, down = block_sums(
            [
                (grads_part(far - 1), [ring_shift(grads_far[:half], 1, fsdp)]),
                (grads_part(1 - far), [ring_shift(grads_far[half:], -1, fsdp)]),
            ],
            True,
            [d_kv],
        )
        grads_sent = [up, down]
    grad_qkv, sent, kept = local_call(
        tail_kernel,
        [
            ((fsdp, w_rows, 3 * inner), bf16),
            ((2, tok_rows, width), bf16),
            ((2, tok_rows, width), f32),
        ],
        [
            ring_rows,
            where,
            d_query,
            d_kv,
            right,
            left,
            cosine,
            sine,
            x_all,
            qkv_full,
        ],
        2**32,
        "tail",
        scratch=[
            pltpu.VMEM((3 * inner, group_rows), bf16),
            pltpu.VMEM((fsdp, w_rows, 3 * inner), bf16),
        ],
        spaces=[smem, smem] + [vmem] * 8,
        after=grads_sent,
    )
    kept, sent = local_call(
        input_mid_kernel,
        [own_full, own_low],
        [where, kept, seq_swap(sent, 1)],
        2**20,
        "input_mid",
        spaces=[smem, vmem, vmem],
    )
    (d_input,) = local_call(
        input_end_kernel, [own_low], [d_first, kept, seq_swap(sent, 2)], 2**20, "input_end"
    )

    def qkv_part(offset):
        return [(grad_qkv, step_of[offset])]

    if fsdp == SPAN:
        grads_right = ring_shift(grads_sent[0], 1, fsdp)
        grads_left = ring_shift(grads_sent[1], -1, fsdp)
        right, left = grads_right, grads_left
        (qkv_far,) = block_sums([(qkv_part(far), [])], False, [])
        arrived = [ring_shift(qkv_far[:half], 1, fsdp), ring_shift(qkv_far[half:], -1, fsdp)]
        pair = [(w_rows, packed_width + 3 * inner)] * 2
        for t in range(far - 1, 1, -1):
            up, down = block_call(
                functools.partial(pair_kernel, t == far - 1),
                pair,
                [
                    *grads_part(t - 1),
                    right,
                    *qkv_part(t),
                    arrived[0],
                    *grads_part(1 - t),
                    left,
                    *qkv_part(-t),
                    arrived[1],
                ],
                "pair",
                after=[kept] if t == far - 1 else [],
            )
            right, left = ring_shift(up, 1, fsdp), ring_shift(down, -1, fsdp)
            arrived = [right, left]
        grads_own, up, down = block_call(
            final_kernel,
            [(w_rows, packed_width)] + [(w_rows, 3 * inner)] * 2,
            [*grads_part(0), right, left, *qkv_part(1), *qkv_part(-1)],
            "final",
            after=[d_input],
        )
        right, left = ring_shift(up, 1, fsdp), ring_shift(down, -1, fsdp)
        (qkv_own_grad,) = block_sums([(qkv_part(0), [right, left])], False, [])
    else:
        qkv_own_grad, _ = ring_scatter(qkv_part, fsdp, [])
        grads_own, _ = ring_scatter(grads_part, fsdp, [])

    def seq_gather(value, after):
        other = gate(seq_swap(value, 2), after) if after else seq_swap(value, 2)
        return [value, other, seq_swap(value, 1), seq_swap(other, 1)]

    (final_qkv,) = local_call(
        functools.partial(ordered_kernel, unpack_qkv_kernel, 4),
        [(w_qkv.shape, f32)],
        [seq_places, *seq_gather(qkv_own_grad, [])],
        2**20,
        "unpack_qkv",
        scratch=[pltpu.VMEM((groups, w_rows, 3 * inner), bf16)],
        spaces=[smem] + [vmem] * 4,
    )
    parts = seq_gather(grads_own, [qkv_own_grad])
    if aligned:
        final_up, final_gate, final_down, final_out, final_vectors = local_call(
            functools.partial(ordered_kernel, functools.partial(unpack_kernel, fsdp, width), 4),
            [
                (w_up.shape, f32),
                (w_gate.shape, f32),
                (w_down.shape, f32),
                (w_out.shape, f32),
                ((w_rows, spare), f32),
            ],
            [seq_places, *parts],
            2**20,
            "unpack",
            scratch=[pltpu.VMEM((groups,) + parts[0].shape, bf16)],
            spaces=[smem] + [vmem] * 4,
        )
    else:
        parts = arrange(parts, seq_order).astype(f32)

        def columns(at):
            value = parts[:, :, at : at + width].reshape(groups, w_rows, fsdp, w_rows)
            return value.transpose(1, 2, 0, 3).reshape(w_rows, groups * width)

        final_up, final_gate = columns(0), columns(width)
        final_down = parts[:, :, 2 * width : 3 * width].reshape(groups * w_rows, width)
        final_out = parts[:, :, 3 * width : 3 * width + inner].transpose(1, 0, 2)
        final_out = final_out.reshape(w_rows, width)
        final_vectors = jnp.sum(parts[:, :, 3 * width + inner :], axis=0)
    final_vectors = final_vectors[:, :4].T
    return (
        result,
        d_input,
        final_qkv,
        final_out,
        final_vectors[0],
        final_vectors[1],
        final_up,
        final_gate,
        final_down,
        final_vectors[2],
        final_vectors[3],
    )


def solution(mesh):
    rows = P(("fsdp", "seq"), None)
    param, vector = P("fsdp", None), P("fsdp")
    in_specs = (rows, rows, P(), param, param, vector, vector, param, param, param, vector, vector)
    out_specs = (rows, rows, param, param, vector, vector, param, param, param, vector, vector)
    return jax.shard_map(local, mesh=mesh, in_specs=in_specs, out_specs=out_specs, check_vma=False)
```

```python
import functools
import math

import jax
import jax.numpy as jnp
from jax import lax
from jax.experimental import pallas as pl
from jax.experimental.pallas import tpu as pltpu
from jax.sharding import PartitionSpec as P

HEADS = 12
HEAD_DIM = 64
SPAN = 8
EXT = 16
WIDE = HEAD_DIM + EXT
BIG = 2.0**30
SAFE_SUM = 2.0**100
VMEM = 40 * 2**20
SMALL = 16 * 2**20

bf16 = jnp.bfloat16
f32 = jnp.float32
norm_eps = 1e-12
base_log = math.log(1000.0)


def dot(left_op, right_op, left_dim, right_dim):
    return lax.dot_general(
        left_op, right_op, (((left_dim,), (right_dim,)), ((), ())), preferred_element_type=f32
    )


def ring_order(size):
    return list(range(0, size, 2)) + list(range(size - 1, 0, -2))


def ring_place(index, size):
    return jnp.where(index % 2 == 0, index // 2, size - 1 - index // 2)


def ring_index(place, size):
    place = place % size
    return jnp.where(place < size // 2, 2 * place, 2 * (size - 1 - place) + 1)


def ring_shift(value, step, size):
    order = ring_order(size)
    pairs = [
        (base + order[i], base + order[(i + step) % size])
        for base in range(0, lax.axis_size("fsdp"), size)
        for i in range(size)
    ]
    return lax.ppermute(value, "fsdp", pairs)


def seq_swap(value, mask):
    return lax.ppermute(value, "seq", [(i, i ^ mask) for i in range(lax.axis_size("seq"))])


def arrange_kernel(count, order, *refs):
    for i, ref in enumerate(refs[:count]):
        refs[-1][order[i]] = ref[...]


def arrange(blocks, order, after=()):
    return pl.pallas_call(
        functools.partial(arrange_kernel, len(blocks)),
        in_specs=[pl.BlockSpec(memory_space=pltpu.SMEM)]
        + [pl.BlockSpec(memory_space=pltpu.VMEM)] * len(blocks)
        + [pl.BlockSpec(memory_space=pl.ANY)] * len(after),
        out_specs=pl.BlockSpec(memory_space=pltpu.VMEM),
        out_shape=jax.ShapeDtypeStruct((len(blocks),) + blocks[0].shape, blocks[0].dtype),
        compiler_params=pltpu.CompilerParams(vmem_limit_bytes=SMALL),
        name="arrange",
    )(jnp.stack(order).astype(jnp.int32), *blocks, *after)


def arrange_runs_kernel(order, *refs):
    at = 0
    for ref in refs[:-1]:
        for k in range(ref.shape[0]):
            refs[-1][order[at]] = ref[k]
            at += 1


def arrange_runs(runs, order):
    return pl.pallas_call(
        arrange_runs_kernel,
        in_specs=[pl.BlockSpec(memory_space=pltpu.SMEM)]
        + [pl.BlockSpec(memory_space=pltpu.VMEM)] * len(runs),
        out_specs=pl.BlockSpec(memory_space=pltpu.VMEM),
        out_shape=jax.ShapeDtypeStruct((len(order),) + runs[0].shape[1:], runs[0].dtype),
        compiler_params=pltpu.CompilerParams(vmem_limit_bytes=VMEM),
        name="arrange_runs",
    )(jnp.stack(order).astype(jnp.int32), *runs)


def ring_gather(block, size, place):
    half = block.shape[0] // 2
    right, left = block, block
    blocks, order = [block], [ring_index(place, size)]
    for t in range(1, size // 2):
        right, left = ring_shift(right, 1, size), ring_shift(left, -1, size)
        blocks += [right, left]
        order += [ring_index(place - t, size), ring_index(place + t, size)]
    last = jnp.concatenate(
        [ring_shift(right[:half], 1, size), ring_shift(left[half:], -1, size)], axis=0
    )
    return blocks + [last], order + [ring_index(place + size // 2, size)]


def sum_kernel(counts, split, *refs):
    outs = refs[-len(counts) :]
    at = 0
    for which, (count, arrived) in enumerate(counts):
        blocks, got = refs[at : at + count], refs[at + count : at + count + arrived]
        at += count + arrived
        total = sum(ref[0].astype(f32) for ref in blocks)
        if split and arrived:
            half = total.shape[0] // 2
            cut = slice(0, half) if which == 0 else slice(half, 2 * half)
            other = slice(half, 2 * half) if which == 0 else slice(0, half)
            outs[which][cut, :] = (total[cut] + got[0][...].astype(f32)).astype(bf16)
            outs[which][other, :] = total[other].astype(bf16)
        else:
            total = total + sum(ref[...].astype(f32) for ref in got)
            outs[which][...] = total.astype(bf16)


def block_sums(directions, split, after):
    specs, ins = [], []
    for blocks, got in directions:
        for stacked, index in blocks:
            shape = (1,) + stacked.shape[1:]
            specs.append(pl.BlockSpec(shape, lambda _, index=index: (index, 0, 0)))
            ins.append(stacked)
        for value in got:
            specs.append(pl.BlockSpec(value.shape, lambda _: (0, 0)))
            ins.append(value)
    shape = directions[0][0][0][0].shape[1:]
    counts = [(len(blocks), len(got)) for blocks, got in directions]
    used = len(ins)

    def body(*refs):
        sum_kernel(counts, split, *refs[:used], *refs[used + len(after) :])

    return pl.pallas_call(
        body,
        grid=(1,),
        in_specs=specs + [pl.BlockSpec(memory_space=pl.ANY)] * len(after),
        out_specs=[pl.BlockSpec(shape, lambda _: (0, 0)) for _ in counts],
        out_shape=[jax.ShapeDtypeStruct(shape, bf16) for _ in counts],
        compiler_params=pltpu.CompilerParams(vmem_limit_bytes=SMALL),
        name="sums",
    )(*ins, *after)


def ring_scatter(blocks, size, after):
    after = {i: list(values) for i, values in enumerate(after)}
    (far,) = block_sums([(blocks(size // 2), [])], False, after.get(0, []))
    half = far.shape[0] // 2
    sent = [far]
    right = ring_shift(far[:half], 1, size)
    left = ring_shift(far[half:], -1, size)
    for hop, t in enumerate(range(size // 2 - 1, 0, -1)):
        up, down = block_sums(
            [(blocks(t), [right]), (blocks(-t), [left])], hop == 0, after.get(hop + 1, [])
        )
        right, left = ring_shift(up, 1, size), ring_shift(down, -1, size)
        sent.append(up)
    (total,) = block_sums([(blocks(0), [right, left])], False, after.get(size // 2, []))
    return total, sent


def three_parts(value):
    high = value.astype(bf16).astype(f32)
    rest = value - high
    mid = rest.astype(bf16).astype(f32)
    return high, mid, rest - mid


def with_parts(base, value):
    high, mid, low = three_parts(value)
    lane = lax.broadcasted_iota(jnp.int32, base.shape, 1)
    filled = jnp.where(lane == HEAD_DIM, high, base)
    filled = jnp.where(lane == HEAD_DIM + 1, mid, filled)
    return jnp.where(lane == HEAD_DIM + 2, low, filled)


def first_kernel(heads, tile, where_ref, ext_ref, qt_ref, qe_ref, kv_ref, qx_ref, acc_ref):
    tokens = qt_ref.shape[1]
    ones = jnp.ones((EXT, tokens), bf16)
    ext = block_ext(ext_ref, where_ref, 0, tokens)
    for h in range(heads):
        rows = slice(h * HEAD_DIM, (h + 1) * HEAD_DIM)
        k_rows, v_rows = block_rows([kv_ref], h)
        keys = jnp.concatenate([k_rows, ext], axis=0)
        vals = jnp.concatenate([v_rows, ones], axis=0)
        for start in range(0, tokens, tile):
            cut = slice(start, start + tile)
            natural = qt_ref[rows, cut].astype(f32).T
            queries = jnp.concatenate([natural, qe_ref[cut, :].astype(f32)], axis=1)
            scores = dot(queries.astype(bf16), keys, 1, 0)
            top = jnp.max(scores, axis=1, keepdims=True)
            weights = jnp.exp(scores - top).astype(bf16)
            acc_ref[h, :, cut] = dot(vals, weights, 1, 1)
            qx_ref[h, cut, :] = with_parts(queries, top).astype(bf16)


def block_rows(refs, h):
    if len(refs) == 2:
        rows = slice(h * HEAD_DIM, (h + 1) * HEAD_DIM)
        return refs[0][rows, :], refs[1][rows, :]
    inner = refs[0].shape[0] // 2
    return (
        refs[0][h * HEAD_DIM : (h + 1) * HEAD_DIM, :],
        refs[0][inner + h * HEAD_DIM : inner + (h + 1) * HEAD_DIM, :],
    )


def block_ext(ext_ref, where_ref, index, tokens):
    return ext_ref[:, pl.ds(pl.multiple_of(where_ref[index] * tokens, tokens), tokens)]


def step_kernel(heads, tile, parts, where_ref, ext_ref, qx_ref, acc_in, *refs):
    acc_ref, tokens = refs[-1], qx_ref.shape[1]
    ones = jnp.ones((EXT, tokens), bf16)
    blocks, at = [], 0
    for b, part in enumerate(parts):
        blocks.append((refs[at : at + part], block_ext(ext_ref, where_ref, b, tokens)))
        at += part
    for h in range(heads):
        pairs = []
        for block, ext in blocks:
            k_rows, v_rows = block_rows(block, h)
            pairs.append(
                (jnp.concatenate([k_rows, ext], axis=0), jnp.concatenate([v_rows, ones], axis=0))
            )
        for start in range(0, tokens, tile):
            cut = slice(start, start + tile)
            total = acc_in[h, :, cut]
            for keys, vals in pairs:
                weights = jnp.exp(dot(qx_ref[h, cut, :], keys, 1, 0)).astype(bf16)
                total = total + dot(vals, weights, 1, 1)
            acc_ref[h, :, cut] = total


def finish_kernel(heads, tile, parts, where_ref, ext_ref, qx_ref, acc_ref, *refs):
    count = sum(parts)
    blocks = refs[:count]
    ot_ref, on_ref, qx2_ref, buf, acc, qx = refs[count:]
    tokens = qx_ref.shape[1]
    inner = buf.shape[1] // 2
    fine = True
    for h in range(heads):
        sums = acc_ref[h, HEAD_DIM : HEAD_DIM + 8, :]
        fine = jnp.logical_and(fine, jnp.logical_and(sums <= SAFE_SUM, sums >= 0.5))
    good = jnp.min(jnp.where(fine, 1.0, 0.0)) > 0.5
    acc[...] = acc_ref[...]
    qx[...] = qx_ref[...]

    @pl.when(jnp.logical_not(good))
    def _():
        small = tile // 2
        ones = jnp.ones((EXT, tokens), bf16)
        lane = lax.broadcasted_iota(jnp.int32, (small, WIDE), 1)
        inside = jnp.logical_and(lane >= HEAD_DIM, lane < HEAD_DIM + 3)
        at = 0
        for b, part in enumerate(parts):
            if part == 2:
                pltpu.sync_copy(blocks[at], buf.at[b, pl.ds(0, inner)])
                pltpu.sync_copy(blocks[at + 1], buf.at[b, pl.ds(inner, inner)])
            else:
                pltpu.sync_copy(blocks[at], buf.at[b])
            at += part

        def each(body):
            cuts = tokens // small

            def turn(step, carry):
                b, rest = step // (heads * cuts), step % (heads * cuts)
                h = rest // cuts
                cut = pl.ds(pl.multiple_of(rest % cuts * small, small), small)
                rows = pl.multiple_of(h * HEAD_DIM, HEAD_DIM)
                ext = block_ext(ext_ref, where_ref, b, tokens)
                keys = jnp.concatenate([buf[b, pl.ds(rows, HEAD_DIM), :], ext], axis=0)
                vals = buf[b, pl.ds(pl.multiple_of(inner + rows, HEAD_DIM), HEAD_DIM), :]
                body(h, cut, keys, jnp.concatenate([vals, ones], axis=0))
                return carry

            lax.fori_loop(0, len(parts) * heads * cuts, turn, 0)

        def raise_top(h, cut, keys, vals):
            base = qx[h, cut, :].astype(f32)
            old = jnp.sum(jnp.where(inside, base, 0.0), axis=1, keepdims=True)
            plain = jnp.where(inside, 0.0, base)
            scores = dot(plain.astype(bf16), keys, 1, 0)
            top = jnp.maximum(old, jnp.max(scores, axis=1, keepdims=True))
            qx[h, cut, :] = with_parts(plain, top).astype(bf16)

        def add_up(h, cut, keys, vals):
            weights = jnp.exp(dot(qx[h, cut, :], keys, 1, 0)).astype(bf16)
            acc[h, :, cut] += dot(vals, weights, 1, 1)

        each(raise_top)
        acc[...] = jnp.zeros_like(acc)
        each(add_up)

    lane = lax.broadcasted_iota(jnp.int32, (tile, WIDE), 1)
    inside = jnp.logical_and(lane >= HEAD_DIM, lane < HEAD_DIM + 3)
    for h in range(heads):
        rows = slice(h * HEAD_DIM, (h + 1) * HEAD_DIM)
        for start in range(0, tokens, tile):
            cut = slice(start, start + tile)
            block = acc[h, :, cut]
            normed = block[:HEAD_DIM, :] * (1.0 / block[HEAD_DIM : HEAD_DIM + 1, :])
            ot_ref[rows, cut] = normed.astype(bf16)
            stacked = jnp.concatenate([normed, jnp.log(block[HEAD_DIM:, :])], axis=0).T
            on_ref[h, cut, :] = stacked[:, :HEAD_DIM]
            base = qx[h, cut, :].astype(f32)
            top = jnp.sum(jnp.where(inside, base, 0.0), axis=1, keepdims=True)
            shift = top + stacked[:, HEAD_DIM : HEAD_DIM + 1]
            qx2_ref[h, cut, :] = with_parts(base, shift).astype(bf16)


def delta_kernel(heads, where, own_ref, got_ref, on_ref, dox_ref, dot_ref):
    tokens = own_ref.shape[1]
    for tile in range(2):
        cut = slice(tile * tokens, (tile + 1) * tokens)

        @pl.when(where[0] == tile)
        def _():
            dot_ref[:, cut] = own_ref[...]

        @pl.when(where[0] != tile)
        def _():
            dot_ref[:, cut] = got_ref[...]

        for h in range(heads):
            rows = slice(h * HEAD_DIM, (h + 1) * HEAD_DIM)
            natural = dot_ref[rows, cut].astype(f32).T
            delta = jnp.sum(natural * on_ref[h, cut, :], axis=1, keepdims=True)
            base = jnp.concatenate([natural, jnp.zeros((tokens, EXT), f32)], axis=1)
            dox_ref[h, cut, :] = with_parts(base, delta).astype(bf16)


def back_kernel(heads, q_tile, where_ref, ext_ref, qx_ref, dox_ref, qt_ref, dot_ref, dq_in, *refs):
    block, (dq_ref, dkv_ref) = refs[:-2], refs[-2:]
    tokens, inner = qt_ref.shape[1], qt_ref.shape[0]
    ext = block_ext(ext_ref, where_ref, 0, tokens)
    for h in range(heads):
        rows = slice(h * HEAD_DIM, (h + 1) * HEAD_DIM)
        k_rows, v_rows = block_rows(block, h)
        keys = jnp.concatenate([k_rows, ext], axis=0)
        vals = jnp.concatenate([v_rows, ext], axis=0)
        d_key, d_value = 0.0, 0.0
        for start in range(0, tokens, q_tile):
            cut = slice(start, start + q_tile)
            weights = jnp.exp(dot(qx_ref[h, cut, :], keys, 1, 0))
            shifted = dot(dox_ref[h, cut, :], vals, 1, 0)
            d_scores = (weights * shifted).astype(bf16)
            d_value = d_value + dot(dot_ref[rows, cut], weights.astype(bf16), 1, 0)
            d_key = d_key + dot(qt_ref[rows, cut], d_scores, 1, 0)
            dq_ref[rows, cut] = dq_in[rows, cut] + dot(k_rows, d_scores, 1, 1)
        dkv_ref[rows, :] = d_key.astype(bf16)
        dkv_ref[inner + h * HEAD_DIM : inner + (h + 1) * HEAD_DIM, :] = d_value.astype(bf16)


def pack_kernel(parts, s_ref, up_ref, gate_ref, down_ref, last_ref, *refs):
    vectors, out_ref = refs[:4], refs[4]
    s = s_ref[0]
    rows = up_ref.shape[0]
    width = parts * rows
    for i, ref in enumerate((up_ref, gate_ref)):
        pieces = []
        for k in range(parts):
            run = ref[:, 4 * rows * k : 4 * rows * (k + 1)]
            pieces.append(pltpu.roll(run, (4 * rows - s * rows) % (4 * rows), 1)[:, :rows])
        out_ref[:, i * width : (i + 1) * width] = jnp.concatenate(pieces, axis=1).astype(bf16)
    own = down_ref[pl.ds(pl.multiple_of(s * rows, 8), rows), :]
    out_ref[:, 2 * width : 3 * width] = own.astype(bf16)
    inner = width // 4
    columns = pltpu.roll(last_ref[...], (width - s * inner) % width, 1)[:, :inner]
    spare = out_ref.shape[1] - 3 * width - inner
    side = jnp.concatenate([ref[...] for ref in vectors] + [jnp.zeros((4, rows), f32)], axis=0).T
    out_ref[:, 3 * width :] = jnp.concatenate(
        [columns, side, jnp.zeros((rows, spare - 8), f32)], axis=1
    ).astype(bf16)


def unpack_kernel(parts, width, *refs):
    quarters, (up_ref, gate_ref, down_ref, out_ref), vectors = refs[:4], refs[4:8], refs[8:]
    rows = up_ref.shape[0]
    inner = width // 4
    for i, ref in enumerate((up_ref, gate_ref)):
        for k in range(parts):
            at = i * width + k * rows
            ref[:, 4 * rows * k : 4 * rows * (k + 1)] = jnp.concatenate(
                [q[:, at : at + rows].astype(f32) for q in quarters], axis=1
            )
    for g, q in enumerate(quarters):
        down_ref[g * rows : (g + 1) * rows, :] = q[:, 2 * width : 3 * width].astype(f32)
    at = 3 * width
    out_ref[...] = jnp.concatenate([q[:, at : at + inner].astype(f32) for q in quarters], axis=1)
    sums = sum(q[:, at + inner :].astype(f32) for q in quarters).T
    for i, ref in enumerate(vectors):
        ref[...] = sums[i : i + 1, :]


def ordered_kernel(kernel, count, order, *refs):
    buffer = refs[-1]
    for i in range(count):
        buffer[order[i]] = refs[i][...]
    kernel(*[buffer.at[i] for i in range(count)], *refs[count:-1])


def grads_kernel(order, hidden_ref, branch_ref, heads_ref, first_sums, second_sums, *refs):
    sides, mine_ref, runs, buffer = (refs[:4], refs[4:8]), refs[8], refs[9:-1], refs[-1]
    count, rows = mine_ref.shape[0], mine_ref.shape[1]
    width = hidden_ref.shape[1]
    hidden_t = hidden_ref[...].T
    heads = heads_ref[...].reshape(width, heads_ref.shape[2])
    vectors = (first_sums[...] + second_sums[...]).T
    vectors = jnp.concatenate(
        [vectors, jnp.zeros((width, mine_ref.shape[2] - 3 * width - width // 4 - 8), f32)], axis=1
    ).astype(bf16)
    for which, (up_ref, gate_ref, inner_ref, cols_ref) in enumerate(sides):

        def put(value, at):
            for k in range(count):
                buffer[k, :, at : at + value.shape[1]] = value[k * rows : (k + 1) * rows]

        put(dot(hidden_t, up_ref[...], 1, 0).astype(bf16), 0)
        put(dot(hidden_t, gate_ref[...], 1, 0).astype(bf16), width)
        put(dot(inner_ref[...].T, branch_ref[...], 1, 0).astype(bf16), 2 * width)
        tail = dot(heads, cols_ref[...], 1, 0).astype(bf16)
        rest = vectors if which == 0 else jnp.zeros_like(vectors)
        put(jnp.concatenate([tail, rest], axis=1), 3 * width)
        if which == 0:
            for i in range(count):
                mine_ref[i] = buffer[order[i]]
        else:
            at = 0
            for run in runs:
                for k in range(run.shape[0]):
                    run[k] = buffer[order[at]]
                    at += 1


def tail_kernel(
    order, where, dq_ref, dkv_ref, right_ref, left_ref, cos_ref, sin_ref, x_ref, w_ref, *refs
):
    grad_ref, sent_ref, kept_ref, raw, buffer = refs
    inner = dq_ref.shape[0]
    cosine, sine = cos_ref[...], sin_ref[...]
    d_kv = dkv_ref[...].astype(f32) + right_ref[...].astype(f32) + left_ref[...].astype(f32)

    def put(base):
        def at_base(at, value):
            raw[base + at : base + at + value.shape[0], :] = value.astype(bf16)

        return at_base

    turn_rows(dq_ref[...] * HEAD_DIM**-0.5, cosine, -sine, put(0))
    turn_rows(d_kv[:inner], cosine, -sine, put(inner))
    raw[2 * inner :, :] = d_kv[inner:].astype(bf16)
    projected = raw[...].T
    count, rows = grad_ref.shape[0], grad_ref.shape[1]
    width, quarter = x_ref.shape[2], x_ref.shape[1]
    terms = dot(projected, w_ref[...].reshape(width, 3 * inner), 1, 1)
    for core in range(2):
        side = [terms[(2 * y + core) * quarter : (2 * y + core + 1) * quarter] for y in range(2)]

        @pl.when(where[1] == core)
        def _():
            for y in range(2):
                kept_ref[y] = side[y]

        @pl.when(where[1] != core)
        def _():
            for y in range(2):
                sent_ref[y] = side[y].astype(bf16)

    grad = dot(x_ref[...].reshape(4 * quarter, width).T, projected, 1, 0).astype(bf16)
    for k in range(count):
        buffer[k] = grad[k * rows : (k + 1) * rows]
    for i in range(count):
        grad_ref[i] = buffer[order[i]]


def unpack_qkv_kernel(*refs):
    quarters, out_ref = refs[:4], refs[4]
    inner = quarters[0].shape[1] // 3
    out_ref[...] = jnp.concatenate(
        [q[:, i * inner : (i + 1) * inner].astype(f32) for i in range(3) for q in quarters], axis=1
    )


def tables_kernel(at_ref, docs_ref, key_ref, query_ref):
    length, tokens = key_ref.shape[1], query_ref.shape[0]

    def kinds(start, count):
        docs = docs_ref[:, pl.ds(pl.multiple_of(start, count), count)] - at_ref[1]
        docs = jnp.broadcast_to(docs, (EXT, count))
        row = lax.broadcasted_iota(jnp.int32, (EXT, count), 0)
        return row, docs == row - 3

    row, same = kinds(at_ref[0], length)
    mark = jnp.where(jnp.logical_or(row < 3, jnp.logical_not(same)), -1.0, 0.0)
    key_ref[...] = jnp.where(row < 6, mark, 0.0).astype(bf16)
    row, same = kinds(at_ref[2], tokens)
    inside = jnp.logical_and(same, jnp.logical_and(row >= 3, row < 6))
    query_ref[...] = jnp.where(inside, BIG, 0.0).T.astype(bf16)


def turn_rows(value, cosine, sine, put):
    half = HEAD_DIM // 2
    for at in range(0, value.shape[0], HEAD_DIM):
        lead, last = value[at : at + half], value[at + half : at + HEAD_DIM]
        put(at, lead * cosine - last * sine)
        put(at + half, last * cosine + lead * sine)


def project_kernel(count, order, places, cos_ref, sin_ref, *refs):
    weights, tokens = refs[:count], refs[count : count + 4]
    q_ref, kv_ref, x_ref, w_ref = refs[count + 4 :]
    inner = q_ref.shape[0]
    for i, ref in enumerate(weights):
        w_ref[order[i]] = ref[...]
    for i, ref in enumerate(tokens):
        x_ref[places[i]] = ref[...]
    cosine, sine = cos_ref[...], sin_ref[...]
    width = x_ref.shape[2]
    matrix = w_ref[...].reshape(width, 3 * inner).T
    rows = x_ref[...].reshape(-1, width)

    def put_q(at, value):
        q_ref[at : at + value.shape[0], :] = value.astype(bf16) * bf16(HEAD_DIM**-0.5)

    def put_k(at, value):
        kv_ref[at : at + value.shape[0], :] = value.astype(bf16)

    turn_rows(dot(matrix[:inner], rows, 1, 1), cosine, sine, put_q)
    turn_rows(dot(matrix[inner : 2 * inner], rows, 1, 1), cosine, sine, put_k)
    kv_ref[inner:, :] = dot(matrix[2 * inner :], rows, 1, 1).astype(bf16)


def outer_kernel(places, *refs):
    parts, (out_ref, vec_ref, buffer) = refs[:4], refs[4:]
    inner = out_ref.shape[1] // 4
    for i, ref in enumerate(parts):
        buffer[places[i]] = ref[...]
    out_ref[...] = jnp.concatenate([buffer[g, :, :inner] for g in range(4)], axis=1)
    vec_ref[...] = parts[0][:, inner:].astype(f32).T[:8]


def gate(value, after):
    return pl.pallas_call(
        lambda *refs: None,
        in_specs=[pl.BlockSpec(memory_space=pl.ANY)] * (1 + len(after)),
        out_specs=pl.BlockSpec(memory_space=pl.ANY),
        out_shape=jax.ShapeDtypeStruct(value.shape, value.dtype),
        input_output_aliases={0: 0},
        name="gate",
    )(value, *after)


def norm_parts(rows_in):
    centre = rows_in - jnp.mean(rows_in, axis=-1, keepdims=True)
    rstd = lax.rsqrt(jnp.mean(centre * centre, axis=-1, keepdims=True) + norm_eps)
    return centre * rstd, rstd


def norm_grad(normed, rstd, grad, gain):
    scaled = grad * gain
    mean = jnp.mean(scaled, axis=-1, keepdims=True)
    return rstd * (scaled - mean - normed * jnp.mean(scaled * normed, axis=-1, keepdims=True))


def ff_weights(ref):
    width = ref.shape[0]
    return ref[:, :width], ref[:, width : 2 * width], ref[:, 2 * width : 3 * width]


def forward_kernel(places, where, *refs):
    parts, (x_ref, out_ref, vec_ref, mine_ref, other_ref) = refs[:4], refs[4:9]
    heads_ref, hidden_ref, kept_ref, sent_ref, normed_ref, rstd_ref = refs[9:15]
    acts = (refs[15:18], refs[18:21])
    width, rows = hidden_ref.shape[1], kept_ref.shape[0]
    side, core = where[0], where[1]
    for i, ref in enumerate(parts):
        heads_ref[places[i]] = ref[...]
    for tile in range(2):
        cut = slice(tile * rows, (tile + 1) * rows)
        start = pl.multiple_of((2 * side + tile) * rows, rows)
        heads = heads_ref[:, :, cut].reshape(width, rows).T
        first = x_ref[pl.ds(start, rows), :].astype(f32) + dot(heads, out_ref[...], 1, 0)
        normed, rstd = norm_parts(first)
        hidden = normed * vec_ref[0:1] + vec_ref[1:2]
        low = hidden.astype(bf16)
        hidden_ref[cut, :] = low
        branch = 0.0
        for w_ref, (up_ref, gate_ref, inner_ref) in zip((mine_ref, other_ref), acts):
            up_w, gate_w, down_w = ff_weights(w_ref)
            up, gate = dot(low, up_w, 1, 0), dot(low, gate_w, 1, 0)
            inner = (gate * lax.logistic(gate) * up).astype(bf16)
            up_ref[cut, :], gate_ref[cut, :], inner_ref[cut, :] = up, gate, inner
            branch = branch + dot(inner, down_w, 1, 0)

        @pl.when(core == tile)
        def _():
            kept_ref[...] = hidden + branch
            normed_ref[...] = normed
            rstd_ref[...] = jnp.broadcast_to(rstd, rstd_ref.shape)

        @pl.when(core != tile)
        def _():
            sent_ref[...] = branch.astype(bf16)


def second_kernel(kept_ref, got_ref, grad_ref, vec_ref, result_ref, d_ref, low_ref, sums_ref):
    normed, rstd = norm_parts(kept_ref[...] + got_ref[...].astype(f32))
    gain = vec_ref[2:3]
    result_ref[...] = (normed * gain + vec_ref[3:4]).astype(bf16)
    grad = grad_ref[...].astype(f32)
    d_second = norm_grad(normed, rstd, grad, gain)
    d_ref[...] = d_second
    low_ref[...] = d_second.astype(bf16)
    sums_ref[...] = jnp.zeros_like(sums_ref)
    sums_ref[2:3] = jnp.sum(grad * normed, axis=0, keepdims=True)
    sums_ref[3:4] = jnp.sum(grad, axis=0, keepdims=True)


def backward_kernel(where, own_ref, got_ref, mine_ref, other_ref, *refs):
    acts = (refs[:2], refs[2:4])
    branch_ref, kept_ref, sent_ref = refs[4:7]
    outs = (refs[7:9], refs[9:11])
    rows, core = kept_ref.shape[0], where[1]
    branch_ref[pl.ds(pl.multiple_of(core * rows, rows), rows), :] = own_ref[...]
    branch_ref[pl.ds(pl.multiple_of((1 - core) * rows, rows), rows), :] = got_ref[...]
    for tile in range(2):
        cut = slice(tile * rows, (tile + 1) * rows)
        branch = branch_ref[cut, :]
        total = 0.0
        for w_ref, (up_ref, gate_ref), (d_up_ref, d_gate_ref) in zip(
            (mine_ref, other_ref), acts, outs
        ):
            up_w, gate_w, down_w = ff_weights(w_ref)
            d_inner = dot(branch, down_w, 1, 1)
            up, gate = up_ref[cut, :], gate_ref[cut, :]
            sig = lax.logistic(gate)
            d_gate = (d_inner * up * sig * (1.0 + gate * (1.0 - sig))).astype(bf16)
            d_up = (d_inner * gate * sig).astype(bf16)
            d_up_ref[cut, :], d_gate_ref[cut, :] = d_up, d_gate
            total = total + dot(d_up, up_w, 1, 1) + dot(d_gate, gate_w, 1, 1)

        @pl.when(core == tile)
        def _():
            kept_ref[...] = total

        @pl.when(core != tile)
        def _():
            sent_ref[...] = total.astype(bf16)


def first_back_kernel(
    kept_ref, got_ref, d_second_ref, normed_ref, rstd_ref, vec_ref, d_ref, low_ref, sums_ref
):
    d_hidden = d_second_ref[...] + kept_ref[...] + got_ref[...].astype(f32)
    normed = normed_ref[...]
    d_first = norm_grad(normed, rstd_ref[:, 0:1], d_hidden, vec_ref[0:1])
    d_ref[...] = d_first
    low_ref[...] = d_first.astype(bf16)
    sums_ref[...] = jnp.zeros_like(sums_ref)
    sums_ref[0:1] = jnp.sum(d_hidden * normed, axis=0, keepdims=True)
    sums_ref[1:2] = jnp.sum(d_hidden, axis=0, keepdims=True)


def heads_back_kernel(
    where, own_ref, got_ref, out_ref, own_heads_ref, sent_ref, own_cols_ref, other_cols_ref, branch
):
    side, core = where[0], where[1]
    rows, inner = own_ref.shape[0], sent_ref.shape[0]
    branch[pl.ds(pl.multiple_of(core * rows, rows), rows), :] = own_ref[...]
    branch[pl.ds(pl.multiple_of((1 - core) * rows, rows), rows), :] = got_ref[...]
    for which, ref in ((1 - side, sent_ref), (side, own_heads_ref)):
        at = pl.multiple_of((2 * which + core) * inner, inner)
        ref[...] = dot(out_ref[pl.ds(at, inner), :], branch[...], 1, 1).astype(bf16)
    for group in range(4):
        value = branch[:, group * inner : (group + 1) * inner]

        @pl.when(2 * side + core == group)
        def _():
            own_cols_ref[...] = value

        @pl.when(2 * (1 - side) + core == group)
        def _():
            other_cols_ref[...] = value


def input_mid_kernel(where, kept_ref, got_ref, kept_out, sent_out):
    for y in range(2):
        value = kept_ref[y] + got_ref[y].astype(f32)

        @pl.when(where[0] == y)
        def _():
            kept_out[...] = value

        @pl.when(where[0] != y)
        def _():
            sent_out[...] = value.astype(bf16)


def input_end_kernel(first_ref, kept_ref, got_ref, out_ref):
    out_ref[...] = (first_ref[...] + kept_ref[...] + got_ref[...].astype(f32)).astype(bf16)


def piped_call(kernel, outs, ins, name, after=()):
    count = len(ins)

    def body(*refs):
        kernel(*refs[:count], *refs[count + len(after) :])

    def whole(shape):
        return pl.BlockSpec(shape, lambda _: (0,) * len(shape))

    return pl.pallas_call(
        body,
        grid=(1,),
        in_specs=[pl.BlockSpec(memory_space=pltpu.SMEM)]
        + [whole(value.shape) for value in ins[1:]]
        + [pl.BlockSpec(memory_space=pl.ANY)] * len(after),
        out_specs=[whole(shape) for shape, _ in outs],
        out_shape=[jax.ShapeDtypeStruct(shape, dtype) for shape, dtype in outs],
        compiler_params=pltpu.CompilerParams(vmem_limit_bytes=SMALL),
        name=name,
    )(*ins, *after)


def local_call(kernel, outs, ins, flops, name, scratch=(), spaces=None, after=()):
    spaces = list(spaces or [pltpu.VMEM] * len(ins))
    count = len(ins)

    def body(*refs):
        kernel(*refs[:count], *refs[count + len(after) :])

    return pl.pallas_call(
        body,
        in_specs=[pl.BlockSpec(memory_space=space) for space in spaces + [pl.ANY] * len(after)],
        out_specs=[pl.BlockSpec(memory_space=pltpu.VMEM) for _ in outs],
        out_shape=[jax.ShapeDtypeStruct(shape, dtype) for shape, dtype in outs],
        scratch_shapes=list(scratch),
        compiler_params=pltpu.CompilerParams(vmem_limit_bytes=VMEM),
        cost_estimate=pl.CostEstimate(flops=flops * 5, bytes_accessed=2**20, transcendentals=0),
        name=name,
    )(*ins, *after)


def local(
    layer_input,
    out_grad,
    doc_ids,
    w_qkv,
    w_out,
    norm1_gain,
    norm1_bias,
    w_up,
    w_gate,
    w_down,
    norm2_gain,
    norm2_bias,
):
    fsdp = lax.axis_size("fsdp")
    groups = lax.axis_size("seq")
    f = lax.axis_index("fsdp")
    s = lax.axis_index("seq")
    side, core = s // 2, s % 2
    tok_rows, width = layer_input.shape
    w_rows = w_qkv.shape[0]
    inner = width // groups
    heads = inner // HEAD_DIM
    group_rows = tok_rows * groups
    half_rows = group_rows // 2
    length = SPAN * group_rows
    place = ring_place(f, fsdp)
    spot = ring_place(f % SPAN, SPAN)
    base = f // SPAN * SPAN

    seq_order = [s, s ^ 2, s ^ 1, s ^ 3]
    seq_places = jnp.stack(seq_order).astype(jnp.int32)
    where = jnp.stack([side, core]).astype(jnp.int32)
    smem, vmem = pltpu.SMEM, pltpu.VMEM
    aligned = w_rows * groups % 128 == 0 and w_rows % 16 == 0

    def quarter(matrix, start):
        return lax.dynamic_slice_in_dim(matrix, start + s * inner, inner, 1)

    qkv_own = jnp.concatenate([quarter(w_qkv, i * width) for i in range(3)], axis=1).astype(bf16)
    x_side = seq_swap(layer_input, 2)
    x_core = seq_swap(layer_input, 1)
    x_far = seq_swap(layer_input, 3)
    qkv_blocks, order = ring_gather(qkv_own, fsdp, place)
    early, qkv_second = qkv_blocks[-3:-1], qkv_blocks[3:5]
    ring_order_now = jnp.stack(order).astype(jnp.int32)
    if not aligned:
        qkv_blocks = [arrange(qkv_blocks, order).reshape(width, 3 * inner)]
        ring_order_now = jnp.zeros((1,), jnp.int32)
    key_ext, query_ext = local_call(
        tables_kernel,
        [((EXT, length), bf16), ((group_rows, EXT), bf16)],
        [
            jnp.stack([f // SPAN * length, f // SPAN * 3, f * group_rows]).astype(jnp.int32),
            doc_ids[None, :],
        ],
        2**20,
        "tables",
        spaces=[smem, vmem],
        after=[*early, x_core, x_far],
    )
    positions = f % SPAN * group_rows + jnp.arange(group_rows, dtype=jnp.int32)
    steps = jnp.arange(HEAD_DIM // 2, dtype=f32)
    freqs = jnp.exp(steps * (-2.0 * base_log / HEAD_DIM))
    angles = freqs[:, None] * positions.astype(f32)[None, :]
    cosine, sine = jnp.cos(angles), jnp.sin(angles)

    queries, own_kv, x_all, qkv_full = local_call(
        functools.partial(project_kernel, len(qkv_blocks)),
        [
            ((inner, group_rows), bf16),
            ((2 * inner, group_rows), bf16),
            ((groups, tok_rows, width), bf16),
            ((len(qkv_blocks),) + qkv_blocks[0].shape, bf16),
        ],
        [
            ring_order_now,
            seq_places,
            cosine,
            sine,
            *qkv_blocks,
            layer_input,
            x_side,
            x_core,
            x_far,
        ],
        2**32,
        "project",
        spaces=[smem, smem] + [vmem] * (len(qkv_blocks) + 6),
    )

    def ff_quarter(matrix):
        split = matrix.reshape(w_rows, fsdp, groups, w_rows)
        return lax.dynamic_index_in_dim(split, s, 2, False).reshape(w_rows, width)

    spare = 256 - inner % 256
    packed_width = 3 * width + inner + spare
    if aligned:
        (own,) = piped_call(
            functools.partial(pack_kernel, fsdp),
            [((w_rows, packed_width), bf16)],
            [
                s.reshape(1),
                w_up,
                w_gate,
                w_down,
                w_out,
                *[v[None, :] for v in (norm1_gain, norm1_bias, norm2_gain, norm2_bias)],
            ],
            "pack",
            after=[*qkv_second, x_core, x_far],
        )
    else:
        down_rows = lax.dynamic_slice_in_dim(w_down, s * w_rows, w_rows, 0)
        gains = jnp.stack([norm1_gain, norm1_bias, norm2_gain, norm2_bias], axis=1)
        own = jnp.concatenate(
            [
                ff_quarter(w_up),
                ff_quarter(w_gate),
                down_rows,
                quarter(w_out, 0),
                gains,
                jnp.zeros((w_rows, spare - 4), f32),
            ],
            axis=1,
        ).astype(bf16)
    mine, order = ring_gather(own, fsdp, place)
    steady = [jnp.int32(i) for i in range(fsdp)]
    others = [seq_swap(own, 2)[None]]
    for start in range(1, fsdp, 2):
        run = mine[start : start + 2]
        others.append(seq_swap(arrange(run, steady[: len(run)], others[-1:]), 2))
    others = arrange_runs(others, order).reshape(width, own.shape[1])
    mine = arrange(mine, order).reshape(width, own.shape[1])
    out_own, out_side = mine[:, 3 * width :], others[:, 3 * width :]
    out_core, out_far = seq_swap(out_own, 1), seq_swap(out_side, 1)
    out_full, vectors = local_call(
        outer_kernel,
        [((width, width), bf16), ((8, width), f32)],
        [seq_places, out_own, out_side, out_core, out_far],
        2**20,
        "outer",
        scratch=[pltpu.VMEM((groups,) + out_own.shape, bf16)],
        spaces=[smem] + [vmem] * 4,
    )

    def spots(*offsets):
        return jnp.stack([ring_index(spot + o, SPAN) for o in offsets]).astype(jnp.int32)

    block_flops = 8 * 256 * heads * group_rows * group_rows
    acc_out = ((heads, WIDE, group_rows), f32)
    wide_out = ((heads, group_rows, WIDE), bf16)
    tile = min(512, group_rows)
    qx, acc = local_call(
        functools.partial(first_kernel, heads, tile),
        [wide_out, acc_out],
        [spots(0), key_ext, queries, query_ext, own_kv],
        block_flops,
        "attend_own",
        spaces=[smem] + [vmem] * 4,
    )
    far = SPAN // 2
    blocks = {0: (own_kv,)}
    right, left = own_kv, own_kv
    for t in range(1, far + 1):
        if t < far:
            right, left = ring_shift(right, 1, SPAN), ring_shift(left, -1, SPAN)
            blocks[-t], blocks[t] = (right,), (left,)
            now = [-t, t]
        else:
            blocks[t] = (ring_shift(right[:inner], 1, SPAN), ring_shift(left[inner:], -1, SPAN))
            now = [t]
        refs = [ref for o in now for ref in blocks[o]]
        (acc,) = local_call(
            functools.partial(step_kernel, heads, tile, [len(blocks[o]) for o in now]),
            [acc_out],
            [spots(*now), key_ext, qx, acc, *refs],
            block_flops * len(now),
            "attend_step",
            spaces=[smem] + [vmem] * (3 + len(refs)),
            after=[mine] if t == far - 1 else [],
        )
    offsets = sorted(blocks)
    refs = [ref for o in offsets for ref in blocks[o]]
    heads_t, heads_n, qx = local_call(
        functools.partial(
            finish_kernel, heads, min(512, group_rows), [len(blocks[o]) for o in offsets]
        ),
        [((inner, group_rows), bf16), ((heads, group_rows, HEAD_DIM), f32), wide_out],
        [spots(*offsets), key_ext, qx, acc, *refs],
        block_flops // 4,
        "attend_finish",
        scratch=[
            pltpu.VMEM((SPAN, 2 * inner, group_rows), bf16),
            pltpu.VMEM(*acc_out),
            pltpu.VMEM(*wide_out),
        ],
        spaces=[smem] + [vmem] * 3 + [pl.ANY] * len(refs),
        after=[out_full],
    )

    def my_half(value, axis):
        return lax.dynamic_slice_in_dim(value, side * half_rows, half_rows, axis)

    def other_half(value, axis):
        return lax.dynamic_slice_in_dim(value, (1 - side) * half_rows, half_rows, axis)

    heads_own = my_half(heads_t, 1)
    heads_side = seq_swap(other_half(heads_t, 1), 2)
    heads_core = seq_swap(heads_own, 1)
    heads_far = seq_swap(heads_side, 1)
    half_low = ((half_rows, width), bf16)
    half_acts = [((half_rows, width), f32)] * 2 + [half_low]
    own_low, own_full = ((tok_rows, width), bf16), ((tok_rows, width), f32)
    sums_out = ((8, width), f32)
    heads_all, hidden_low, kept, sent, normed_one, rstd_one, *acts = local_call(
        forward_kernel,
        [
            ((groups, inner, half_rows), bf16),
            half_low,
            own_full,
            own_low,
            own_full,
            ((tok_rows, 128), f32),
            *half_acts,
            *half_acts,
        ],
        [
            seq_places,
            where,
            heads_own,
            heads_side,
            heads_core,
            heads_far,
            x_all.reshape(group_rows, width),
            out_full,
            vectors,
            mine,
            others,
        ],
        2**33,
        "feed_forward",
        spaces=[smem, smem] + [vmem] * 9,
    )
    result, d_second, d_branch_two, sums_two = local_call(
        second_kernel,
        [own_low, own_full, own_low, sums_out],
        [kept, seq_swap(sent, 1), out_grad, vectors],
        2**20,
        "second_norm",
    )
    d_branch_two, kept, sent, d_up, d_gate, d_up_other, d_gate_other = local_call(
        backward_kernel,
        [half_low, own_full, own_low] + [half_low] * 4,
        [
            where,
            d_branch_two,
            seq_swap(d_branch_two, 1),
            mine,
            others,
            acts[0],
            acts[1],
            acts[3],
            acts[4],
        ],
        2**33,
        "feed_back",
        spaces=[smem] + [vmem] * 8,
    )
    d_first, d_branch_one, sums_one = local_call(
        first_back_kernel,
        [own_full, own_low, sums_out],
        [kept, seq_swap(sent, 1), d_second, normed_one, rstd_one, vectors],
        2**20,
        "first_norm_back",
    )

    part = ((inner, half_rows), bf16)
    columns = ((half_rows, inner), bf16)
    d_heads_own, d_heads_sent, cols_own, cols_other = local_call(
        heads_back_kernel,
        [part, part, columns, columns],
        [where, d_branch_one, seq_swap(d_branch_one, 1), out_full],
        2**30,
        "heads_back",
        scratch=[pltpu.VMEM(*half_low)],
        spaces=[smem] + [vmem] * 3,
    )
    dox, d_heads_t = local_call(
        functools.partial(delta_kernel, heads),
        [wide_out, ((inner, group_rows), bf16)],
        [where, d_heads_own, seq_swap(d_heads_sent, 2), heads_n],
        block_flops // 4,
        "delta",
        spaces=[smem] + [vmem] * 3,
    )

    steps_out = [fsdp // 2] + [o for t in range(fsdp // 2 - 1, 0, -1) for o in (t, -t)] + [0]
    step_of = {o: i for i, o in enumerate(steps_out)}
    ring_rows = jnp.stack([ring_index(place + o, fsdp) for o in steps_out]).astype(jnp.int32)
    packed = ((fsdp, w_rows, own.shape[1]), bf16)
    cuts = [0, 3 * fsdp // 8, 5 * fsdp // 8, fsdp]
    grads_mine, *grads_other = local_call(
        grads_kernel,
        [packed] + [((b - a,) + packed[0][1:], bf16) for a, b in zip(cuts, cuts[1:])],
        [
            ring_rows,
            hidden_low,
            d_branch_two,
            heads_all,
            sums_one,
            sums_two,
            d_up,
            d_gate,
            acts[2],
            cols_own,
            d_up_other,
            d_gate_other,
            acts[5],
            cols_other,
        ],
        2**32,
        "grads",
        scratch=[pltpu.VMEM(*packed)],
        spaces=[smem] + [vmem] * 13,
    )

    got = [seq_swap(run, 2) for run in grads_other]

    def grads_part(offset):
        i = step_of[offset]
        which = sum(i >= cut for cut in cuts[1:])
        return [(grads_mine, i), (got[which], i - cuts[which])]

    d_query = jnp.zeros((inner, group_rows), f32)

    def back(offset, d_query, after):
        return local_call(
            functools.partial(back_kernel, heads, min(256, group_rows)),
            [((inner, group_rows), f32), ((2 * inner, group_rows), bf16)],
            [spots(offset), key_ext, qx, dox, queries, d_heads_t, d_query, *blocks[offset]],
            block_flops * 2,
            "attend_back",
            spaces=[smem] + [vmem] * (6 + len(blocks[offset])),
            after=after,
        )

    d_query, d_far = back(far, d_query, [])
    d_query, up = back(far - 1, d_query, [])
    d_query, down = back(1 - far, d_query, [])
    right, left = ring_shift(d_far[:inner], 1, SPAN), ring_shift(d_far[inner:], -1, SPAN)
    up = jnp.concatenate([up[:inner] + right, up[inner:]], axis=0)
    down = jnp.concatenate([down[:inner], down[inner:] + left], axis=0)
    after = [right, left]
    for t in range(far - 2, 0, -1):
        d_query, next_up = back(t, d_query, after)
        right, left = ring_shift(up, 1, SPAN), ring_shift(down, -1, SPAN)
        d_query, next_down = back(-t, d_query, [])
        after = [right, left]
        up, down = next_up + right, next_down + left
    right, left = ring_shift(up, 1, SPAN), ring_shift(down, -1, SPAN)
    d_query, d_kv = back(0, d_query, after)
    grads_sent = []
    if fsdp == SPAN:
        half = w_rows // 2
        (grads_far,) = block_sums([(grads_part(far), [])], False, [])
        up, down = block_sums(
            [
                (grads_part(far - 1), [ring_shift(grads_far[:half], 1, fsdp)]),
                (grads_part(1 - far), [ring_shift(grads_far[half:], -1, fsdp)]),
            ],
            True,
            [d_kv, got[1]],
        )
        grads_sent = [ring_shift(up, 1, fsdp), ring_shift(down, -1, fsdp)]
    grad_qkv, sent, kept = local_call(
        tail_kernel,
        [
            ((fsdp, w_rows, 3 * inner), bf16),
            ((2, tok_rows, width), bf16),
            ((2, tok_rows, width), f32),
        ],
        [
            ring_rows,
            where,
            d_query,
            d_kv,
            right,
            left,
            cosine,
            sine,
            x_all,
            qkv_full,
        ],
        2**32,
        "tail",
        scratch=[
            pltpu.VMEM((3 * inner, group_rows), bf16),
            pltpu.VMEM((fsdp, w_rows, 3 * inner), bf16),
        ],
        spaces=[smem, smem] + [vmem] * 8,
        after=grads_sent,
    )
    kept, sent = local_call(
        input_mid_kernel,
        [own_full, own_low],
        [where, kept, seq_swap(sent, 1)],
        2**20,
        "input_mid",
        spaces=[smem, vmem, vmem],
    )
    (d_input,) = local_call(
        input_end_kernel, [own_low], [d_first, kept, seq_swap(sent, 2)], 2**20, "input_end"
    )

    def qkv_part(offset):
        return [(grad_qkv, step_of[offset])]

    if fsdp == SPAN:
        qkv_own_grad, qkv_sent = ring_scatter(
            qkv_part, fsdp, [[], [kept]] + [[]] * (far - 3) + [[d_input]]
        )
        right, left = grads_sent
        for hop, t in enumerate(range(far - 2, 0, -1)):
            up, down = block_sums(
                [(grads_part(t), [right]), (grads_part(-t), [left])],
                False,
                [qkv_sent[hop + 1]] if hop else [],
            )
            right, left = ring_shift(up, 1, fsdp), ring_shift(down, -1, fsdp)
        (grads_own,) = block_sums([(grads_part(0), [right, left])], False, [qkv_sent[-1]])
    else:
        qkv_own_grad, _ = ring_scatter(qkv_part, fsdp, [])
        grads_own, _ = ring_scatter(grads_part, fsdp, [])

    def seq_gather(value, after):
        other = gate(seq_swap(value, 2), after) if after else seq_swap(value, 2)
        return [value, other, seq_swap(value, 1), seq_swap(other, 1)]

    parts = seq_gather(grads_own, [qkv_own_grad])
    qkv_parts = seq_gather(qkv_own_grad, [])
    if aligned:
        final_up, final_gate, final_down, final_out, *final_vectors = local_call(
            functools.partial(ordered_kernel, functools.partial(unpack_kernel, fsdp, width), 4),
            [(w.shape, f32) for w in (w_up, w_gate, w_down, w_out)] + [((1, w_rows), f32)] * 4,
            [seq_places, *parts],
            2**20,
            "unpack",
            scratch=[pltpu.VMEM((groups,) + parts[0].shape, bf16)],
            spaces=[smem] + [vmem] * 4,
        )
        final_vectors = [v.reshape(w_rows) for v in final_vectors]
    else:
        parts = arrange(parts, seq_order).astype(f32)

        def columns(at):
            value = parts[:, :, at : at + width].reshape(groups, w_rows, fsdp, w_rows)
            return value.transpose(1, 2, 0, 3).reshape(w_rows, groups * width)

        final_up, final_gate = columns(0), columns(width)
        final_down = parts[:, :, 2 * width : 3 * width].reshape(groups * w_rows, width)
        final_out = parts[:, :, 3 * width : 3 * width + inner].transpose(1, 0, 2)
        final_out = final_out.reshape(w_rows, width)
        final_vectors = jnp.sum(parts[:, :, 3 * width + inner :], axis=0).T
    (final_qkv,) = local_call(
        functools.partial(ordered_kernel, unpack_qkv_kernel, 4),
        [(w_qkv.shape, f32)],
        [seq_places, *qkv_parts],
        2**20,
        "unpack_qkv",
        scratch=[pltpu.VMEM((groups, w_rows, 3 * inner), bf16)],
        spaces=[smem] + [vmem] * 4,
    )
    return (
        result,
        d_input,
        final_qkv,
        final_out,
        final_vectors[0],
        final_vectors[1],
        final_up,
        final_gate,
        final_down,
        final_vectors[2],
        final_vectors[3],
    )


def solution(mesh):
    rows = P(("fsdp", "seq"), None)
    param, vector = P("fsdp", None), P("fsdp")
    in_specs = (rows, rows, P(), param, param, vector, vector, param, param, param, vector, vector)
    out_specs = (rows, rows, param, param, vector, vector, param, param, param, vector, vector)
    return jax.shard_map(local, mesh=mesh, in_specs=in_specs, out_specs=out_specs, check_vma=False)
```

```python
import functools
import math

import jax
import jax.numpy as jnp
from jax import lax
from jax.experimental import pallas as pl
from jax.experimental.pallas import tpu as pltpu
from jax.sharding import PartitionSpec as P

HEADS = 12
HEAD_DIM = 64
SPAN = 8
EXT = 16
WIDE = HEAD_DIM + EXT
BIG = 2.0**30
SAFE_SUM = 2.0**100
VMEM = 24 * 2**20
SMALL = 16 * 2**20

bf16 = jnp.bfloat16
f32 = jnp.float32
norm_eps = 1e-12
base_log = math.log(1000.0)


def dot(left_op, right_op, left_dim, right_dim):
    return lax.dot_general(
        left_op, right_op, (((left_dim,), (right_dim,)), ((), ())), preferred_element_type=f32
    )


def ring_order(size):
    return list(range(0, size, 2)) + list(range(size - 1, 0, -2))


def ring_place(index, size):
    return jnp.where(index % 2 == 0, index // 2, size - 1 - index // 2)


def ring_index(place, size):
    place = place % size
    return jnp.where(place < size // 2, 2 * place, 2 * (size - 1 - place) + 1)


def ring_shift(value, step, size):
    order = ring_order(size)
    pairs = [
        (base + order[i], base + order[(i + step) % size])
        for base in range(0, lax.axis_size("fsdp"), size)
        for i in range(size)
    ]
    return lax.ppermute(value, "fsdp", pairs)


def seq_swap(value, mask):
    return lax.ppermute(value, "seq", [(i, i ^ mask) for i in range(lax.axis_size("seq"))])


def arrange_kernel(count, order, *refs):
    for i, ref in enumerate(refs[:count]):
        refs[-1][order[i]] = ref[...]


def arrange(blocks, order, after=()):
    return pl.pallas_call(
        functools.partial(arrange_kernel, len(blocks)),
        in_specs=[pl.BlockSpec(memory_space=pltpu.SMEM)]
        + [pl.BlockSpec(memory_space=pltpu.VMEM)] * len(blocks)
        + [pl.BlockSpec(memory_space=pl.ANY)] * len(after),
        out_specs=pl.BlockSpec(memory_space=pltpu.VMEM),
        out_shape=jax.ShapeDtypeStruct((len(blocks),) + blocks[0].shape, blocks[0].dtype),
        compiler_params=pltpu.CompilerParams(vmem_limit_bytes=SMALL),
        name="arrange",
    )(jnp.stack(order).astype(jnp.int32), *blocks, *after)


def arrange_runs_kernel(order, *refs):
    at = 0
    for ref in refs[:-1]:
        for k in range(ref.shape[0]):
            refs[-1][order[at]] = ref[k]
            at += 1


def arrange_runs(runs, order):
    return pl.pallas_call(
        arrange_runs_kernel,
        in_specs=[pl.BlockSpec(memory_space=pltpu.SMEM)]
        + [pl.BlockSpec(memory_space=pltpu.VMEM)] * len(runs),
        out_specs=pl.BlockSpec(memory_space=pltpu.VMEM),
        out_shape=jax.ShapeDtypeStruct((len(order),) + runs[0].shape[1:], runs[0].dtype),
        compiler_params=pltpu.CompilerParams(vmem_limit_bytes=VMEM),
        name="arrange_runs",
    )(jnp.stack(order).astype(jnp.int32), *runs)


def ring_gather(block, size, place):
    half = block.shape[0] // 2
    right, left = block, block
    blocks, order = [block], [ring_index(place, size)]
    for t in range(1, size // 2):
        right, left = ring_shift(right, 1, size), ring_shift(left, -1, size)
        blocks += [right, left]
        order += [ring_index(place - t, size), ring_index(place + t, size)]
    last = jnp.concatenate(
        [ring_shift(right[:half], 1, size), ring_shift(left[half:], -1, size)], axis=0
    )
    return blocks + [last], order + [ring_index(place + size // 2, size)]


def sum_kernel(counts, split, *refs):
    outs = refs[-len(counts) :]
    at = 0
    for which, (count, arrived) in enumerate(counts):
        blocks, got = refs[at : at + count], refs[at + count : at + count + arrived]
        at += count + arrived
        total = sum(ref[0].astype(f32) for ref in blocks)
        if split and arrived:
            half = total.shape[0] // 2
            cut = slice(0, half) if which == 0 else slice(half, 2 * half)
            other = slice(half, 2 * half) if which == 0 else slice(0, half)
            outs[which][cut, :] = (total[cut] + got[0][...].astype(f32)).astype(bf16)
            outs[which][other, :] = total[other].astype(bf16)
        else:
            total = total + sum(ref[...].astype(f32) for ref in got)
            outs[which][...] = total.astype(bf16)


def block_sums(directions, split, after):
    specs, ins = [], []
    for blocks, got in directions:
        for stacked, index in blocks:
            shape = (1,) + stacked.shape[1:]
            specs.append(pl.BlockSpec(shape, lambda _, index=index: (index, 0, 0)))
            ins.append(stacked)
        for value in got:
            specs.append(pl.BlockSpec(value.shape, lambda _: (0, 0)))
            ins.append(value)
    shape = directions[0][0][0][0].shape[1:]
    counts = [(len(blocks), len(got)) for blocks, got in directions]
    used = len(ins)

    def body(*refs):
        sum_kernel(counts, split, *refs[:used], *refs[used + len(after) :])

    return pl.pallas_call(
        body,
        grid=(1,),
        in_specs=specs + [pl.BlockSpec(memory_space=pl.ANY)] * len(after),
        out_specs=[pl.BlockSpec(shape, lambda _: (0, 0)) for _ in counts],
        out_shape=[jax.ShapeDtypeStruct(shape, bf16) for _ in counts],
        compiler_params=pltpu.CompilerParams(vmem_limit_bytes=SMALL),
        name="sums",
    )(*ins, *after)


def ring_scatter(blocks, size, after):
    after = {i: list(values) for i, values in enumerate(after)}
    (far,) = block_sums([(blocks(size // 2), [])], False, after.get(0, []))
    half = far.shape[0] // 2
    sent = [far]
    right = ring_shift(far[:half], 1, size)
    left = ring_shift(far[half:], -1, size)
    first = [right, left]
    for hop, t in enumerate(range(size // 2 - 1, 0, -1)):
        up, down = block_sums(
            [(blocks(t), [right]), (blocks(-t), [left])], hop == 0, after.get(hop + 1, [])
        )
        right, left = ring_shift(up, 1, size), ring_shift(down, -1, size)
        sent.append(up)
    (total,) = block_sums([(blocks(0), [right, left])], False, after.get(size // 2, []))
    return total, sent, first


def three_parts(value):
    high = value.astype(bf16).astype(f32)
    rest = value - high
    mid = rest.astype(bf16).astype(f32)
    return high, mid, rest - mid


def with_parts(base, value):
    high, mid, low = three_parts(value)
    lane = lax.broadcasted_iota(jnp.int32, base.shape, 1)
    filled = jnp.where(lane == HEAD_DIM, high, base)
    filled = jnp.where(lane == HEAD_DIM + 1, mid, filled)
    return jnp.where(lane == HEAD_DIM + 2, low, filled)


def first_kernel(heads, tile, where_ref, ext_ref, qt_ref, qe_ref, kv_ref, qx_ref, acc_ref):
    tokens = qt_ref.shape[1]
    ones = jnp.ones((EXT, tokens), bf16)
    ext = block_ext(ext_ref, where_ref, 0, tokens)
    for h in range(heads):
        rows = slice(h * HEAD_DIM, (h + 1) * HEAD_DIM)
        k_rows, v_rows = block_rows([kv_ref], h)
        keys = jnp.concatenate([k_rows, ext], axis=0)
        vals = jnp.concatenate([v_rows, ones], axis=0)
        for start in range(0, tokens, tile):
            cut = slice(start, start + tile)
            natural = qt_ref[rows, cut].astype(f32).T
            queries = jnp.concatenate([natural, qe_ref[cut, :].astype(f32)], axis=1)
            scores = dot(queries.astype(bf16), keys, 1, 0)
            top = jnp.max(scores, axis=1, keepdims=True)
            weights = jnp.exp(scores - top).astype(bf16)
            acc_ref[h, :, cut] = dot(vals, weights, 1, 1)
            qx_ref[h, cut, :] = with_parts(queries, top).astype(bf16)


def block_rows(refs, h):
    if len(refs) == 2:
        rows = slice(h * HEAD_DIM, (h + 1) * HEAD_DIM)
        return refs[0][rows, :], refs[1][rows, :]
    inner = refs[0].shape[0] // 2
    return (
        refs[0][h * HEAD_DIM : (h + 1) * HEAD_DIM, :],
        refs[0][inner + h * HEAD_DIM : inner + (h + 1) * HEAD_DIM, :],
    )


def block_ext(ext_ref, where_ref, index, tokens):
    return ext_ref[:, pl.ds(pl.multiple_of(where_ref[index] * tokens, tokens), tokens)]


def step_kernel(heads, tile, parts, where_ref, ext_ref, qx_ref, acc_in, *refs):
    acc_ref, tokens = refs[-1], qx_ref.shape[1]
    ones = jnp.ones((EXT, tokens), bf16)
    blocks, at = [], 0
    for b, part in enumerate(parts):
        blocks.append((refs[at : at + part], block_ext(ext_ref, where_ref, b, tokens)))
        at += part
    for h in range(heads):
        pairs = []
        for block, ext in blocks:
            k_rows, v_rows = block_rows(block, h)
            pairs.append(
                (jnp.concatenate([k_rows, ext], axis=0), jnp.concatenate([v_rows, ones], axis=0))
            )
        for start in range(0, tokens, tile):
            cut = slice(start, start + tile)
            total = acc_in[h, :, cut]
            for keys, vals in pairs:
                weights = jnp.exp(dot(qx_ref[h, cut, :], keys, 1, 0)).astype(bf16)
                total = total + dot(vals, weights, 1, 1)
            acc_ref[h, :, cut] = total


def finish_kernel(heads, tile, parts, where_ref, ext_ref, qx_ref, acc_ref, *refs):
    count = sum(parts)
    blocks = refs[:count]
    ot_ref, on_ref, qx2_ref, buf, acc, qx = refs[count:]
    tokens = qx_ref.shape[1]
    inner = buf.shape[1] // 2
    fine = True
    for h in range(heads):
        sums = acc_ref[h, HEAD_DIM : HEAD_DIM + 8, :]
        fine = jnp.logical_and(fine, jnp.logical_and(sums <= SAFE_SUM, sums >= 0.5))
    good = jnp.min(jnp.where(fine, 1.0, 0.0)) > 0.5
    acc[...] = acc_ref[...]
    qx[...] = qx_ref[...]

    @pl.when(jnp.logical_not(good))
    def _():
        small = tile // 2
        ones = jnp.ones((EXT, tokens), bf16)
        lane = lax.broadcasted_iota(jnp.int32, (small, WIDE), 1)
        inside = jnp.logical_and(lane >= HEAD_DIM, lane < HEAD_DIM + 3)
        at = 0
        for b, part in enumerate(parts):
            if part == 2:
                pltpu.sync_copy(blocks[at], buf.at[b, pl.ds(0, inner)])
                pltpu.sync_copy(blocks[at + 1], buf.at[b, pl.ds(inner, inner)])
            else:
                pltpu.sync_copy(blocks[at], buf.at[b])
            at += part

        def each(body):
            cuts = tokens // small

            def turn(step, carry):
                b, rest = step // (heads * cuts), step % (heads * cuts)
                h = rest // cuts
                cut = pl.ds(pl.multiple_of(rest % cuts * small, small), small)
                rows = pl.multiple_of(h * HEAD_DIM, HEAD_DIM)
                ext = block_ext(ext_ref, where_ref, b, tokens)
                keys = jnp.concatenate([buf[b, pl.ds(rows, HEAD_DIM), :], ext], axis=0)
                vals = buf[b, pl.ds(pl.multiple_of(inner + rows, HEAD_DIM), HEAD_DIM), :]
                body(h, cut, keys, jnp.concatenate([vals, ones], axis=0))
                return carry

            lax.fori_loop(0, len(parts) * heads * cuts, turn, 0)

        def raise_top(h, cut, keys, vals):
            base = qx[h, cut, :].astype(f32)
            old = jnp.sum(jnp.where(inside, base, 0.0), axis=1, keepdims=True)
            plain = jnp.where(inside, 0.0, base)
            scores = dot(plain.astype(bf16), keys, 1, 0)
            top = jnp.maximum(old, jnp.max(scores, axis=1, keepdims=True))
            qx[h, cut, :] = with_parts(plain, top).astype(bf16)

        def add_up(h, cut, keys, vals):
            weights = jnp.exp(dot(qx[h, cut, :], keys, 1, 0)).astype(bf16)
            acc[h, :, cut] += dot(vals, weights, 1, 1)

        each(raise_top)
        acc[...] = jnp.zeros_like(acc)
        each(add_up)

    lane = lax.broadcasted_iota(jnp.int32, (tile, WIDE), 1)
    inside = jnp.logical_and(lane >= HEAD_DIM, lane < HEAD_DIM + 3)
    for h in range(heads):
        rows = slice(h * HEAD_DIM, (h + 1) * HEAD_DIM)
        for start in range(0, tokens, tile):
            cut = slice(start, start + tile)
            block = acc[h, :, cut]
            normed = block[:HEAD_DIM, :] * (1.0 / block[HEAD_DIM : HEAD_DIM + 1, :])
            ot_ref[rows, cut] = normed.astype(bf16)
            stacked = jnp.concatenate([normed, jnp.log(block[HEAD_DIM:, :])], axis=0).T
            on_ref[h, cut, :] = stacked[:, :HEAD_DIM]
            base = qx[h, cut, :].astype(f32)
            top = jnp.sum(jnp.where(inside, base, 0.0), axis=1, keepdims=True)
            shift = top + stacked[:, HEAD_DIM : HEAD_DIM + 1]
            qx2_ref[h, cut, :] = with_parts(base, shift).astype(bf16)


def delta_kernel(heads, where, own_ref, got_ref, on_ref, dox_ref, dot_ref):
    tokens = own_ref.shape[1]
    for tile in range(2):
        cut = slice(tile * tokens, (tile + 1) * tokens)

        @pl.when(where[0] == tile)
        def _():
            dot_ref[:, cut] = own_ref[...]

        @pl.when(where[0] != tile)
        def _():
            dot_ref[:, cut] = got_ref[...]

        for h in range(heads):
            rows = slice(h * HEAD_DIM, (h + 1) * HEAD_DIM)
            natural = dot_ref[rows, cut].astype(f32).T
            delta = jnp.sum(natural * on_ref[h, cut, :], axis=1, keepdims=True)
            base = jnp.concatenate([natural, jnp.zeros((tokens, EXT), f32)], axis=1)
            dox_ref[h, cut, :] = with_parts(base, delta).astype(bf16)


def back_kernel(heads, q_tile, where_ref, ext_ref, qx_ref, dox_ref, qt_ref, dot_ref, dq_in, *refs):
    block, (dq_ref, dkv_ref) = refs[:-2], refs[-2:]
    tokens, inner = qt_ref.shape[1], qt_ref.shape[0]
    ext = block_ext(ext_ref, where_ref, 0, tokens)
    for h in range(heads):
        rows = slice(h * HEAD_DIM, (h + 1) * HEAD_DIM)
        k_rows, v_rows = block_rows(block, h)
        keys = jnp.concatenate([k_rows, ext], axis=0)
        vals = jnp.concatenate([v_rows, ext], axis=0)
        d_key, d_value = 0.0, 0.0
        for start in range(0, tokens, q_tile):
            cut = slice(start, start + q_tile)
            weights = jnp.exp(dot(qx_ref[h, cut, :], keys, 1, 0))
            shifted = dot(dox_ref[h, cut, :], vals, 1, 0)
            d_scores = (weights * shifted).astype(bf16)
            d_value = d_value + dot(dot_ref[rows, cut], weights.astype(bf16), 1, 0)
            d_key = d_key + dot(qt_ref[rows, cut], d_scores, 1, 0)
            dq_ref[rows, cut] = dq_in[rows, cut] + dot(k_rows, d_scores, 1, 1)
        dkv_ref[rows, :] = d_key.astype(bf16)
        dkv_ref[inner + h * HEAD_DIM : inner + (h + 1) * HEAD_DIM, :] = d_value.astype(bf16)


def pack_kernel(parts, s_ref, up_ref, gate_ref, down_ref, last_ref, *refs):
    vectors, out_ref = refs[:4], refs[4]
    s = s_ref[0]
    rows = up_ref.shape[0]
    width = parts * rows
    for i, ref in enumerate((up_ref, gate_ref)):
        pieces = []
        for k in range(parts):
            run = ref[:, 4 * rows * k : 4 * rows * (k + 1)]
            pieces.append(pltpu.roll(run, (4 * rows - s * rows) % (4 * rows), 1)[:, :rows])
        out_ref[:, i * width : (i + 1) * width] = jnp.concatenate(pieces, axis=1).astype(bf16)
    own = down_ref[pl.ds(pl.multiple_of(s * rows, 8), rows), :]
    out_ref[:, 2 * width : 3 * width] = own.astype(bf16)
    inner = width // 4
    columns = pltpu.roll(last_ref[...], (width - s * inner) % width, 1)[:, :inner]
    spare = out_ref.shape[1] - 3 * width - inner
    side = jnp.concatenate([ref[...] for ref in vectors] + [jnp.zeros((4, rows), f32)], axis=0).T
    out_ref[:, 3 * width :] = jnp.concatenate(
        [columns, side, jnp.zeros((rows, spare - 8), f32)], axis=1
    ).astype(bf16)


def unpack_kernel(parts, width, *refs):
    quarters, (up_ref, gate_ref, down_ref, out_ref), vectors = refs[:4], refs[4:8], refs[8:]
    rows = up_ref.shape[0]
    inner = width // 4
    for i, ref in enumerate((up_ref, gate_ref)):
        for k in range(parts):
            at = i * width + k * rows
            ref[:, 4 * rows * k : 4 * rows * (k + 1)] = jnp.concatenate(
                [q[:, at : at + rows].astype(f32) for q in quarters], axis=1
            )
    for g, q in enumerate(quarters):
        down_ref[g * rows : (g + 1) * rows, :] = q[:, 2 * width : 3 * width].astype(f32)
    at = 3 * width
    out_ref[...] = jnp.concatenate([q[:, at : at + inner].astype(f32) for q in quarters], axis=1)
    sums = sum(q[:, at + inner :].astype(f32) for q in quarters).T
    for i, ref in enumerate(vectors):
        ref[...] = sums[i : i + 1, :]


def ordered_kernel(kernel, count, order, *refs):
    buffer = refs[-1]
    for i in range(count):
        buffer[order[i]] = refs[i][...]
    kernel(*[buffer.at[i] for i in range(count)], *refs[count:-1])


def grads_kernel(order, hidden_ref, branch_ref, heads_ref, first_sums, second_sums, *refs):
    sides, mine_ref, runs, buffer = (refs[:4], refs[4:8]), refs[8], refs[9:-1], refs[-1]
    count, rows = mine_ref.shape[0], mine_ref.shape[1]
    width = hidden_ref.shape[1]
    hidden_t = hidden_ref[...].T
    heads = heads_ref[...].reshape(width, heads_ref.shape[2])
    vectors = (first_sums[...] + second_sums[...]).T
    vectors = jnp.concatenate(
        [vectors, jnp.zeros((width, mine_ref.shape[2] - 3 * width - width // 4 - 8), f32)], axis=1
    ).astype(bf16)
    for which, (up_ref, gate_ref, inner_ref, cols_ref) in enumerate(sides):

        def put(value, at):
            for k in range(count):
                buffer[k, :, at : at + value.shape[1]] = value[k * rows : (k + 1) * rows]

        put(dot(hidden_t, up_ref[...], 1, 0).astype(bf16), 0)
        put(dot(hidden_t, gate_ref[...], 1, 0).astype(bf16), width)
        put(dot(inner_ref[...].T, branch_ref[...], 1, 0).astype(bf16), 2 * width)
        tail = dot(heads, cols_ref[...], 1, 0).astype(bf16)
        rest = vectors if which == 0 else jnp.zeros_like(vectors)
        put(jnp.concatenate([tail, rest], axis=1), 3 * width)
        if which == 0:
            for i in range(count):
                mine_ref[i] = buffer[order[i]]
        else:
            at = 0
            for run in runs:
                for k in range(run.shape[0]):
                    run[k] = buffer[order[at]]
                    at += 1


def tail_kernel(
    order, where, dq_ref, dkv_ref, right_ref, left_ref, cos_ref, sin_ref, x_ref, w_ref, *refs
):
    grad_ref, sent_ref, kept_ref, raw, buffer = refs
    inner = dq_ref.shape[0]
    cosine, sine = cos_ref[...], sin_ref[...]
    d_kv = dkv_ref[...].astype(f32) + right_ref[...].astype(f32) + left_ref[...].astype(f32)

    def put(base):
        def at_base(at, value):
            raw[base + at : base + at + value.shape[0], :] = value.astype(bf16)

        return at_base

    turn_rows(dq_ref[...] * HEAD_DIM**-0.5, cosine, -sine, put(0))
    turn_rows(d_kv[:inner], cosine, -sine, put(inner))
    raw[2 * inner :, :] = d_kv[inner:].astype(bf16)
    projected = raw[...].T
    count, rows = grad_ref.shape[0], grad_ref.shape[1]
    width, quarter = x_ref.shape[2], x_ref.shape[1]
    terms = dot(projected, w_ref[...].reshape(width, 3 * inner), 1, 1)
    for core in range(2):
        side = [terms[(2 * y + core) * quarter : (2 * y + core + 1) * quarter] for y in range(2)]

        @pl.when(where[1] == core)
        def _():
            for y in range(2):
                kept_ref[y] = side[y]

        @pl.when(where[1] != core)
        def _():
            for y in range(2):
                sent_ref[y] = side[y].astype(bf16)

    grad = dot(x_ref[...].reshape(4 * quarter, width).T, projected, 1, 0).astype(bf16)
    for k in range(count):
        buffer[k] = grad[k * rows : (k + 1) * rows]
    for i in range(count):
        grad_ref[i] = buffer[order[i]]


def unpack_qkv_kernel(*refs):
    quarters, out_ref = refs[:4], refs[4]
    inner = quarters[0].shape[1] // 3
    out_ref[...] = jnp.concatenate(
        [q[:, i * inner : (i + 1) * inner].astype(f32) for i in range(3) for q in quarters], axis=1
    )


def tables_kernel(at_ref, docs_ref, key_ref, query_ref):
    length, tokens = key_ref.shape[1], query_ref.shape[0]

    def kinds(start, count):
        docs = docs_ref[:, pl.ds(pl.multiple_of(start, count), count)] - at_ref[1]
        docs = jnp.broadcast_to(docs, (EXT, count))
        row = lax.broadcasted_iota(jnp.int32, (EXT, count), 0)
        return row, docs == row - 3

    row, same = kinds(at_ref[0], length)
    mark = jnp.where(jnp.logical_or(row < 3, jnp.logical_not(same)), -1.0, 0.0)
    key_ref[...] = jnp.where(row < 6, mark, 0.0).astype(bf16)
    row, same = kinds(at_ref[2], tokens)
    inside = jnp.logical_and(same, jnp.logical_and(row >= 3, row < 6))
    query_ref[...] = jnp.where(inside, BIG, 0.0).T.astype(bf16)


def turn_rows(value, cosine, sine, put):
    half = HEAD_DIM // 2
    for at in range(0, value.shape[0], HEAD_DIM):
        lead, last = value[at : at + half], value[at + half : at + HEAD_DIM]
        put(at, lead * cosine - last * sine)
        put(at + half, last * cosine + lead * sine)


def project_kernel(count, order, places, cos_ref, sin_ref, *refs):
    weights, tokens = refs[:count], refs[count : count + 4]
    q_ref, kv_ref, x_ref, w_ref = refs[count + 4 :]
    inner = q_ref.shape[0]
    for i, ref in enumerate(weights):
        w_ref[order[i]] = ref[...]
    for i, ref in enumerate(tokens):
        x_ref[places[i]] = ref[...]
    cosine, sine = cos_ref[...], sin_ref[...]
    width = x_ref.shape[2]
    matrix = w_ref[...].reshape(width, 3 * inner).T
    rows = x_ref[...].reshape(-1, width)

    def put_q(at, value):
        q_ref[at : at + value.shape[0], :] = value.astype(bf16) * bf16(HEAD_DIM**-0.5)

    def put_k(at, value):
        kv_ref[at : at + value.shape[0], :] = value.astype(bf16)

    turn_rows(dot(matrix[:inner], rows, 1, 1), cosine, sine, put_q)
    turn_rows(dot(matrix[inner : 2 * inner], rows, 1, 1), cosine, sine, put_k)
    kv_ref[inner:, :] = dot(matrix[2 * inner :], rows, 1, 1).astype(bf16)


def outer_kernel(places, *refs):
    parts, (out_ref, vec_ref, buffer) = refs[:4], refs[4:]
    inner = out_ref.shape[1] // 4
    for i, ref in enumerate(parts):
        buffer[places[i]] = ref[...]
    out_ref[...] = jnp.concatenate([buffer[g, :, :inner] for g in range(4)], axis=1)
    vec_ref[...] = parts[0][:, inner:].astype(f32).T[:8]


def gate(value, after):
    return pl.pallas_call(
        lambda *refs: None,
        in_specs=[pl.BlockSpec(memory_space=pl.ANY)] * (1 + len(after)),
        out_specs=pl.BlockSpec(memory_space=pl.ANY),
        out_shape=jax.ShapeDtypeStruct(value.shape, value.dtype),
        input_output_aliases={0: 0},
        name="gate",
    )(value, *after)


def norm_parts(rows_in):
    centre = rows_in - jnp.mean(rows_in, axis=-1, keepdims=True)
    rstd = lax.rsqrt(jnp.mean(centre * centre, axis=-1, keepdims=True) + norm_eps)
    return centre * rstd, rstd


def norm_grad(normed, rstd, grad, gain):
    scaled = grad * gain
    mean = jnp.mean(scaled, axis=-1, keepdims=True)
    return rstd * (scaled - mean - normed * jnp.mean(scaled * normed, axis=-1, keepdims=True))


def ff_weights(ref):
    width = ref.shape[0]
    return ref[:, :width], ref[:, width : 2 * width], ref[:, 2 * width : 3 * width]


def forward_kernel(places, where, *refs):
    parts, (x_ref, out_ref, vec_ref, mine_ref, other_ref) = refs[:4], refs[4:9]
    heads_ref, hidden_ref, kept_ref, sent_ref, normed_ref, rstd_ref = refs[9:15]
    acts = (refs[15:18], refs[18:21])
    width, rows = hidden_ref.shape[1], kept_ref.shape[0]
    side, core = where[0], where[1]
    for i, ref in enumerate(parts):
        heads_ref[places[i]] = ref[...]
    for tile in range(2):
        cut = slice(tile * rows, (tile + 1) * rows)
        start = pl.multiple_of((2 * side + tile) * rows, rows)
        heads = heads_ref[:, :, cut].reshape(width, rows).T
        first = x_ref[pl.ds(start, rows), :].astype(f32) + dot(heads, out_ref[...], 1, 0)
        normed, rstd = norm_parts(first)
        hidden = normed * vec_ref[0:1] + vec_ref[1:2]
        low = hidden.astype(bf16)
        hidden_ref[cut, :] = low
        branch = 0.0
        for w_ref, (up_ref, gate_ref, inner_ref) in zip((mine_ref, other_ref), acts):
            up_w, gate_w, down_w = ff_weights(w_ref)
            up, gate = dot(low, up_w, 1, 0), dot(low, gate_w, 1, 0)
            inner = (gate * lax.logistic(gate) * up).astype(bf16)
            up_ref[cut, :], gate_ref[cut, :], inner_ref[cut, :] = up, gate, inner
            branch = branch + dot(inner, down_w, 1, 0)

        @pl.when(core == tile)
        def _():
            kept_ref[...] = hidden + branch
            normed_ref[...] = normed
            rstd_ref[...] = jnp.broadcast_to(rstd, rstd_ref.shape)

        @pl.when(core != tile)
        def _():
            sent_ref[...] = branch.astype(bf16)


def second_kernel(kept_ref, got_ref, grad_ref, vec_ref, result_ref, d_ref, low_ref, sums_ref):
    normed, rstd = norm_parts(kept_ref[...] + got_ref[...].astype(f32))
    gain = vec_ref[2:3]
    result_ref[...] = (normed * gain + vec_ref[3:4]).astype(bf16)
    grad = grad_ref[...].astype(f32)
    d_second = norm_grad(normed, rstd, grad, gain)
    d_ref[...] = d_second
    low_ref[...] = d_second.astype(bf16)
    sums_ref[...] = jnp.zeros_like(sums_ref)
    sums_ref[2:3] = jnp.sum(grad * normed, axis=0, keepdims=True)
    sums_ref[3:4] = jnp.sum(grad, axis=0, keepdims=True)


def backward_kernel(where, own_ref, got_ref, mine_ref, other_ref, *refs):
    acts = (refs[:2], refs[2:4])
    branch_ref, kept_ref, sent_ref = refs[4:7]
    outs = (refs[7:9], refs[9:11])
    rows, core = kept_ref.shape[0], where[1]
    branch_ref[pl.ds(pl.multiple_of(core * rows, rows), rows), :] = own_ref[...]
    branch_ref[pl.ds(pl.multiple_of((1 - core) * rows, rows), rows), :] = got_ref[...]
    for tile in range(2):
        cut = slice(tile * rows, (tile + 1) * rows)
        branch = branch_ref[cut, :]
        total = 0.0
        for w_ref, (up_ref, gate_ref), (d_up_ref, d_gate_ref) in zip(
            (mine_ref, other_ref), acts, outs
        ):
            up_w, gate_w, down_w = ff_weights(w_ref)
            d_inner = dot(branch, down_w, 1, 1)
            up, gate = up_ref[cut, :], gate_ref[cut, :]
            sig = lax.logistic(gate)
            d_gate = (d_inner * up * sig * (1.0 + gate * (1.0 - sig))).astype(bf16)
            d_up = (d_inner * gate * sig).astype(bf16)
            d_up_ref[cut, :], d_gate_ref[cut, :] = d_up, d_gate
            total = total + dot(d_up, up_w, 1, 1) + dot(d_gate, gate_w, 1, 1)

        @pl.when(core == tile)
        def _():
            kept_ref[...] = total

        @pl.when(core != tile)
        def _():
            sent_ref[...] = total.astype(bf16)


def first_back_kernel(
    kept_ref, got_ref, d_second_ref, normed_ref, rstd_ref, vec_ref, d_ref, low_ref, sums_ref
):
    d_hidden = d_second_ref[...] + kept_ref[...] + got_ref[...].astype(f32)
    normed = normed_ref[...]
    d_first = norm_grad(normed, rstd_ref[:, 0:1], d_hidden, vec_ref[0:1])
    d_ref[...] = d_first
    low_ref[...] = d_first.astype(bf16)
    sums_ref[...] = jnp.zeros_like(sums_ref)
    sums_ref[0:1] = jnp.sum(d_hidden * normed, axis=0, keepdims=True)
    sums_ref[1:2] = jnp.sum(d_hidden, axis=0, keepdims=True)


def heads_back_kernel(
    where, own_ref, got_ref, out_ref, own_heads_ref, sent_ref, own_cols_ref, other_cols_ref, branch
):
    side, core = where[0], where[1]
    rows, inner = own_ref.shape[0], sent_ref.shape[0]
    branch[pl.ds(pl.multiple_of(core * rows, rows), rows), :] = own_ref[...]
    branch[pl.ds(pl.multiple_of((1 - core) * rows, rows), rows), :] = got_ref[...]
    for which, ref in ((1 - side, sent_ref), (side, own_heads_ref)):
        at = pl.multiple_of((2 * which + core) * inner, inner)
        ref[...] = dot(out_ref[pl.ds(at, inner), :], branch[...], 1, 1).astype(bf16)
    for group in range(4):
        value = branch[:, group * inner : (group + 1) * inner]

        @pl.when(2 * side + core == group)
        def _():
            own_cols_ref[...] = value

        @pl.when(2 * (1 - side) + core == group)
        def _():
            other_cols_ref[...] = value


def input_mid_kernel(where, kept_ref, got_ref, kept_out, sent_out):
    for y in range(2):
        value = kept_ref[y] + got_ref[y].astype(f32)

        @pl.when(where[0] == y)
        def _():
            kept_out[...] = value

        @pl.when(where[0] != y)
        def _():
            sent_out[...] = value.astype(bf16)


def input_end_kernel(first_ref, kept_ref, got_ref, out_ref):
    out_ref[...] = (first_ref[...] + kept_ref[...] + got_ref[...].astype(f32)).astype(bf16)


def piped_call(kernel, outs, ins, name, after=()):
    count = len(ins)

    def body(*refs):
        kernel(*refs[:count], *refs[count + len(after) :])

    def whole(shape):
        return pl.BlockSpec(shape, lambda _: (0,) * len(shape))

    return pl.pallas_call(
        body,
        grid=(1,),
        in_specs=[pl.BlockSpec(memory_space=pltpu.SMEM)]
        + [whole(value.shape) for value in ins[1:]]
        + [pl.BlockSpec(memory_space=pl.ANY)] * len(after),
        out_specs=[whole(shape) for shape, _ in outs],
        out_shape=[jax.ShapeDtypeStruct(shape, dtype) for shape, dtype in outs],
        compiler_params=pltpu.CompilerParams(vmem_limit_bytes=SMALL),
        name=name,
    )(*ins, *after)


def local_call(kernel, outs, ins, flops, name, scratch=(), spaces=None, after=()):
    spaces = list(spaces or [pltpu.VMEM] * len(ins))
    count = len(ins)

    def body(*refs):
        kernel(*refs[:count], *refs[count + len(after) :])

    return pl.pallas_call(
        body,
        in_specs=[pl.BlockSpec(memory_space=space) for space in spaces + [pl.ANY] * len(after)],
        out_specs=[pl.BlockSpec(memory_space=pltpu.VMEM) for _ in outs],
        out_shape=[jax.ShapeDtypeStruct(shape, dtype) for shape, dtype in outs],
        scratch_shapes=list(scratch),
        compiler_params=pltpu.CompilerParams(vmem_limit_bytes=VMEM),
        cost_estimate=pl.CostEstimate(flops=flops * 5, bytes_accessed=2**20, transcendentals=0),
        name=name,
    )(*ins, *after)


def local(
    layer_input,
    out_grad,
    doc_ids,
    w_qkv,
    w_out,
    norm1_gain,
    norm1_bias,
    w_up,
    w_gate,
    w_down,
    norm2_gain,
    norm2_bias,
):
    fsdp = lax.axis_size("fsdp")
    groups = lax.axis_size("seq")
    f = lax.axis_index("fsdp")
    s = lax.axis_index("seq")
    side, core = s // 2, s % 2
    tok_rows, width = layer_input.shape
    w_rows = w_qkv.shape[0]
    inner = width // groups
    heads = inner // HEAD_DIM
    group_rows = tok_rows * groups
    half_rows = group_rows // 2
    length = SPAN * group_rows
    place = ring_place(f, fsdp)
    spot = ring_place(f % SPAN, SPAN)
    base = f // SPAN * SPAN

    seq_order = [s, s ^ 2, s ^ 1, s ^ 3]
    seq_places = jnp.stack(seq_order).astype(jnp.int32)
    where = jnp.stack([side, core]).astype(jnp.int32)
    smem, vmem = pltpu.SMEM, pltpu.VMEM
    aligned = w_rows * groups % 128 == 0 and w_rows % 16 == 0

    def quarter(matrix, start):
        return lax.dynamic_slice_in_dim(matrix, start + s * inner, inner, 1)

    qkv_own = jnp.concatenate([quarter(w_qkv, i * width) for i in range(3)], axis=1).astype(bf16)
    x_side = seq_swap(layer_input, 2)
    x_core = seq_swap(layer_input, 1)
    x_far = seq_swap(layer_input, 3)
    qkv_blocks, order = ring_gather(qkv_own, fsdp, place)
    early, qkv_second = qkv_blocks[-3:-1], qkv_blocks[3:5]
    ring_order_now = jnp.stack(order).astype(jnp.int32)
    if not aligned:
        qkv_blocks = [arrange(qkv_blocks, order).reshape(width, 3 * inner)]
        ring_order_now = jnp.zeros((1,), jnp.int32)
    key_ext, query_ext = local_call(
        tables_kernel,
        [((EXT, length), bf16), ((group_rows, EXT), bf16)],
        [
            jnp.stack([f // SPAN * length, f // SPAN * 3, f * group_rows]).astype(jnp.int32),
            doc_ids[None, :],
        ],
        2**20,
        "tables",
        spaces=[smem, vmem],
        after=[*early, x_core, x_far],
    )
    positions = f % SPAN * group_rows + jnp.arange(group_rows, dtype=jnp.int32)
    steps = jnp.arange(HEAD_DIM // 2, dtype=f32)
    freqs = jnp.exp(steps * (-2.0 * base_log / HEAD_DIM))
    angles = freqs[:, None] * positions.astype(f32)[None, :]
    cosine, sine = jnp.cos(angles), jnp.sin(angles)

    queries, own_kv, x_all, qkv_full = local_call(
        functools.partial(project_kernel, len(qkv_blocks)),
        [
            ((inner, group_rows), bf16),
            ((2 * inner, group_rows), bf16),
            ((groups, tok_rows, width), bf16),
            ((len(qkv_blocks),) + qkv_blocks[0].shape, bf16),
        ],
        [
            ring_order_now,
            seq_places,
            cosine,
            sine,
            *qkv_blocks,
            layer_input,
            x_side,
            x_core,
            x_far,
        ],
        2**32,
        "project",
        spaces=[smem, smem] + [vmem] * (len(qkv_blocks) + 6),
    )

    def ff_quarter(matrix):
        split = matrix.reshape(w_rows, fsdp, groups, w_rows)
        return lax.dynamic_index_in_dim(split, s, 2, False).reshape(w_rows, width)

    spare = 256 - inner % 256
    packed_width = 3 * width + inner + spare
    if aligned:
        (own,) = piped_call(
            functools.partial(pack_kernel, fsdp),
            [((w_rows, packed_width), bf16)],
            [
                s.reshape(1),
                w_up,
                w_gate,
                w_down,
                w_out,
                *[v[None, :] for v in (norm1_gain, norm1_bias, norm2_gain, norm2_bias)],
            ],
            "pack",
            after=[*qkv_second, x_core, x_far],
        )
    else:
        down_rows = lax.dynamic_slice_in_dim(w_down, s * w_rows, w_rows, 0)
        gains = jnp.stack([norm1_gain, norm1_bias, norm2_gain, norm2_bias], axis=1)
        own = jnp.concatenate(
            [
                ff_quarter(w_up),
                ff_quarter(w_gate),
                down_rows,
                quarter(w_out, 0),
                gains,
                jnp.zeros((w_rows, spare - 4), f32),
            ],
            axis=1,
        ).astype(bf16)
    mine, order = ring_gather(own, fsdp, place)
    steady = [jnp.int32(i) for i in range(fsdp)]
    others = [seq_swap(own, 2)[None]]
    for start in range(1, fsdp, 2):
        run = mine[start : start + 2]
        others.append(seq_swap(arrange(run, steady[: len(run)], others[-1:]), 2))
    others = arrange_runs(others, order).reshape(width, own.shape[1])
    mine = arrange(mine, order).reshape(width, own.shape[1])
    out_own, out_side = mine[:, 3 * width :], others[:, 3 * width :]
    out_core, out_far = seq_swap(out_own, 1), seq_swap(out_side, 1)
    out_full, vectors = local_call(
        outer_kernel,
        [((width, width), bf16), ((8, width), f32)],
        [seq_places, out_own, out_side, out_core, out_far],
        2**20,
        "outer",
        scratch=[pltpu.VMEM((groups,) + out_own.shape, bf16)],
        spaces=[smem] + [vmem] * 4,
    )

    def spots(*offsets):
        return jnp.stack([ring_index(spot + o, SPAN) for o in offsets]).astype(jnp.int32)

    block_flops = 8 * 256 * heads * group_rows * group_rows
    acc_out = ((heads, WIDE, group_rows), f32)
    wide_out = ((heads, group_rows, WIDE), bf16)
    tile = min(512, group_rows)
    qx, acc = local_call(
        functools.partial(first_kernel, heads, tile),
        [wide_out, acc_out],
        [spots(0), key_ext, queries, query_ext, own_kv],
        block_flops,
        "attend_own",
        spaces=[smem] + [vmem] * 4,
    )
    far = SPAN // 2
    blocks = {0: (own_kv,)}
    right, left = own_kv, own_kv
    for t in range(1, far + 1):
        if t < far:
            right, left = ring_shift(right, 1, SPAN), ring_shift(left, -1, SPAN)
            blocks[-t], blocks[t] = (right,), (left,)
            now = [-t, t]
        else:
            blocks[t] = (ring_shift(right[:inner], 1, SPAN), ring_shift(left[inner:], -1, SPAN))
            now = [t]
        refs = [ref for o in now for ref in blocks[o]]
        (acc,) = local_call(
            functools.partial(step_kernel, heads, tile, [len(blocks[o]) for o in now]),
            [acc_out],
            [spots(*now), key_ext, qx, acc, *refs],
            block_flops * len(now),
            "attend_step",
            spaces=[smem] + [vmem] * (3 + len(refs)),
            after=[mine] if t == far - 1 else [],
        )
    offsets = sorted(blocks)
    refs = [ref for o in offsets for ref in blocks[o]]
    heads_t, heads_n, qx = local_call(
        functools.partial(
            finish_kernel, heads, min(512, group_rows), [len(blocks[o]) for o in offsets]
        ),
        [((inner, group_rows), bf16), ((heads, group_rows, HEAD_DIM), f32), wide_out],
        [spots(*offsets), key_ext, qx, acc, *refs],
        block_flops // 4,
        "attend_finish",
        scratch=[
            pltpu.VMEM((SPAN, 2 * inner, group_rows), bf16),
            pltpu.VMEM(*acc_out),
            pltpu.VMEM(*wide_out),
        ],
        spaces=[smem] + [vmem] * 3 + [pl.ANY] * len(refs),
        after=[out_full],
    )

    def my_half(value, axis):
        return lax.dynamic_slice_in_dim(value, side * half_rows, half_rows, axis)

    def other_half(value, axis):
        return lax.dynamic_slice_in_dim(value, (1 - side) * half_rows, half_rows, axis)

    heads_own = my_half(heads_t, 1)
    heads_side = seq_swap(other_half(heads_t, 1), 2)
    heads_core = seq_swap(heads_own, 1)
    heads_far = seq_swap(heads_side, 1)
    half_low = ((half_rows, width), bf16)
    half_acts = [((half_rows, width), f32)] * 2 + [half_low]
    own_low, own_full = ((tok_rows, width), bf16), ((tok_rows, width), f32)
    sums_out = ((8, width), f32)
    heads_all, hidden_low, kept, sent, normed_one, rstd_one, *acts = local_call(
        forward_kernel,
        [
            ((groups, inner, half_rows), bf16),
            half_low,
            own_full,
            own_low,
            own_full,
            ((tok_rows, 128), f32),
            *half_acts,
            *half_acts,
        ],
        [
            seq_places,
            where,
            heads_own,
            heads_side,
            heads_core,
            heads_far,
            x_all.reshape(group_rows, width),
            out_full,
            vectors,
            mine,
            others,
        ],
        2**33,
        "feed_forward",
        spaces=[smem, smem] + [vmem] * 9,
    )
    result, d_second, d_branch_two, sums_two = local_call(
        second_kernel,
        [own_low, own_full, own_low, sums_out],
        [kept, seq_swap(sent, 1), out_grad, vectors],
        2**20,
        "second_norm",
    )
    d_branch_two, kept, sent, d_up, d_gate, d_up_other, d_gate_other = local_call(
        backward_kernel,
        [half_low, own_full, own_low] + [half_low] * 4,
        [
            where,
            d_branch_two,
            seq_swap(d_branch_two, 1),
            mine,
            others,
            acts[0],
            acts[1],
            acts[3],
            acts[4],
        ],
        2**33,
        "feed_back",
        spaces=[smem] + [vmem] * 8,
    )
    d_first, d_branch_one, sums_one = local_call(
        first_back_kernel,
        [own_full, own_low, sums_out],
        [kept, seq_swap(sent, 1), d_second, normed_one, rstd_one, vectors],
        2**20,
        "first_norm_back",
    )

    part = ((inner, half_rows), bf16)
    columns = ((half_rows, inner), bf16)
    d_heads_own, d_heads_sent, cols_own, cols_other = local_call(
        heads_back_kernel,
        [part, part, columns, columns],
        [where, d_branch_one, seq_swap(d_branch_one, 1), out_full],
        2**30,
        "heads_back",
        scratch=[pltpu.VMEM(*half_low)],
        spaces=[smem] + [vmem] * 3,
    )
    dox, d_heads_t = local_call(
        functools.partial(delta_kernel, heads),
        [wide_out, ((inner, group_rows), bf16)],
        [where, d_heads_own, seq_swap(d_heads_sent, 2), heads_n],
        block_flops // 4,
        "delta",
        spaces=[smem] + [vmem] * 3,
    )

    steps_out = [fsdp // 2] + [o for t in range(fsdp // 2 - 1, 0, -1) for o in (t, -t)] + [0]
    step_of = {o: i for i, o in enumerate(steps_out)}
    ring_rows = jnp.stack([ring_index(place + o, fsdp) for o in steps_out]).astype(jnp.int32)
    packed = ((fsdp, w_rows, own.shape[1]), bf16)
    cuts = [0, 3 * fsdp // 8, 5 * fsdp // 8, fsdp]
    grads_mine, *grads_other = local_call(
        grads_kernel,
        [packed] + [((b - a,) + packed[0][1:], bf16) for a, b in zip(cuts, cuts[1:])],
        [
            ring_rows,
            hidden_low,
            d_branch_two,
            heads_all,
            sums_one,
            sums_two,
            d_up,
            d_gate,
            acts[2],
            cols_own,
            d_up_other,
            d_gate_other,
            acts[5],
            cols_other,
        ],
        2**32,
        "grads",
        scratch=[pltpu.VMEM(*packed)],
        spaces=[smem] + [vmem] * 13,
    )

    got = [seq_swap(run, 2) for run in grads_other]

    def grads_part(offset):
        i = step_of[offset]
        which = sum(i >= cut for cut in cuts[1:])
        return [(grads_mine, i), (got[which], i - cuts[which])]

    d_query = jnp.zeros((inner, group_rows), f32)

    def back(offset, d_query, after):
        return local_call(
            functools.partial(back_kernel, heads, min(256, group_rows)),
            [((inner, group_rows), f32), ((2 * inner, group_rows), bf16)],
            [spots(offset), key_ext, qx, dox, queries, d_heads_t, d_query, *blocks[offset]],
            block_flops * 2,
            "attend_back",
            spaces=[smem] + [vmem] * (6 + len(blocks[offset])),
            after=after,
        )

    d_query, d_far = back(far, d_query, [])
    d_query, up = back(far - 1, d_query, [])
    d_query, down = back(1 - far, d_query, [])
    right, left = ring_shift(d_far[:inner], 1, SPAN), ring_shift(d_far[inner:], -1, SPAN)
    up = jnp.concatenate([up[:inner] + right, up[inner:]], axis=0)
    down = jnp.concatenate([down[:inner], down[inner:] + left], axis=0)
    after = [right, left]
    for t in range(far - 2, 0, -1):
        d_query, next_up = back(t, d_query, after)
        right, left = ring_shift(up, 1, SPAN), ring_shift(down, -1, SPAN)
        d_query, next_down = back(-t, d_query, [])
        after = [right, left]
        up, down = next_up + right, next_down + left
    right, left = ring_shift(up, 1, SPAN), ring_shift(down, -1, SPAN)
    d_query, d_kv = back(0, d_query, after)
    grads_sent = []
    if fsdp == SPAN:
        half = w_rows // 2
        (grads_far,) = block_sums([(grads_part(far), [])], False, [])
        up, down = block_sums(
            [
                (grads_part(far - 1), [ring_shift(grads_far[:half], 1, fsdp)]),
                (grads_part(1 - far), [ring_shift(grads_far[half:], -1, fsdp)]),
            ],
            True,
            [d_kv, got[1]],
        )
        grads_sent = [ring_shift(up, 1, fsdp), ring_shift(down, -1, fsdp)]
    grad_qkv, sent, kept = local_call(
        tail_kernel,
        [
            ((fsdp, w_rows, 3 * inner), bf16),
            ((2, tok_rows, width), bf16),
            ((2, tok_rows, width), f32),
        ],
        [
            ring_rows,
            where,
            d_query,
            d_kv,
            right,
            left,
            cosine,
            sine,
            x_all,
            qkv_full,
        ],
        2**32,
        "tail",
        scratch=[
            pltpu.VMEM((3 * inner, group_rows), bf16),
            pltpu.VMEM((fsdp, w_rows, 3 * inner), bf16),
        ],
        spaces=[smem, smem] + [vmem] * 8,
        after=grads_sent,
    )
    kept, sent = local_call(
        input_mid_kernel,
        [own_full, own_low],
        [where, kept, seq_swap(sent, 1)],
        2**20,
        "input_mid",
        spaces=[smem, vmem, vmem],
    )
    (d_input,) = local_call(
        input_end_kernel, [own_low], [d_first, kept, seq_swap(sent, 2)], 2**20, "input_end"
    )

    def qkv_part(offset):
        return [(grad_qkv, step_of[offset])]

    if fsdp == SPAN:
        qkv_own_grad, qkv_sent, qkv_first = ring_scatter(
            qkv_part, fsdp, [[], [kept]] + [[]] * (far - 3) + [[d_input]]
        )
        right, left = grads_sent
        for hop, t in enumerate(range(far - 2, 0, -1)):
            up, down = block_sums(
                [(grads_part(t), [right]), (grads_part(-t), [left])],
                False,
                [qkv_sent[hop + 1]] if hop else qkv_first,
            )
            right, left = ring_shift(up, 1, fsdp), ring_shift(down, -1, fsdp)
        (grads_own,) = block_sums([(grads_part(0), [right, left])], False, [qkv_sent[-1]])
    else:
        qkv_own_grad, *_ = ring_scatter(qkv_part, fsdp, [])
        grads_own, *_ = ring_scatter(grads_part, fsdp, [])

    def seq_gather(value, after):
        other = gate(seq_swap(value, 2), after) if after else seq_swap(value, 2)
        return [value, other, seq_swap(value, 1), seq_swap(other, 1)]

    qkv_parts = seq_gather(qkv_own_grad, [])
    parts = seq_gather(grads_own, qkv_parts[1:2])
    if aligned:
        final_up, final_gate, final_down, final_out, *final_vectors = local_call(
            functools.partial(ordered_kernel, functools.partial(unpack_kernel, fsdp, width), 4),
            [(w.shape, f32) for w in (w_up, w_gate, w_down, w_out)] + [((1, w_rows), f32)] * 4,
            [seq_places, *parts],
            2**20,
            "unpack",
            scratch=[pltpu.VMEM((groups,) + parts[0].shape, bf16)],
            spaces=[smem] + [vmem] * 4,
        )
        final_vectors = [v.reshape(w_rows) for v in final_vectors]
    else:
        parts = arrange(parts, seq_order).astype(f32)

        def columns(at):
            value = parts[:, :, at : at + width].reshape(groups, w_rows, fsdp, w_rows)
            return value.transpose(1, 2, 0, 3).reshape(w_rows, groups * width)

        final_up, final_gate = columns(0), columns(width)
        final_down = parts[:, :, 2 * width : 3 * width].reshape(groups * w_rows, width)
        final_out = parts[:, :, 3 * width : 3 * width + inner].transpose(1, 0, 2)
        final_out = final_out.reshape(w_rows, width)
        final_vectors = jnp.sum(parts[:, :, 3 * width + inner :], axis=0).T
    (final_qkv,) = local_call(
        functools.partial(ordered_kernel, unpack_qkv_kernel, 4),
        [(w_qkv.shape, f32)],
        [seq_places, *qkv_parts],
        2**20,
        "unpack_qkv",
        scratch=[pltpu.VMEM((groups, w_rows, 3 * inner), bf16)],
        spaces=[smem] + [vmem] * 4,
    )
    return (
        result,
        d_input,
        final_qkv,
        final_out,
        final_vectors[0],
        final_vectors[1],
        final_up,
        final_gate,
        final_down,
        final_vectors[2],
        final_vectors[3],
    )


def solution(mesh):
    rows = P(("fsdp", "seq"), None)
    param, vector = P("fsdp", None), P("fsdp")
    in_specs = (rows, rows, P(), param, param, vector, vector, param, param, param, vector, vector)
    out_specs = (rows, rows, param, param, vector, vector, param, param, param, vector, vector)
    return jax.shard_map(local, mesh=mesh, in_specs=in_specs, out_specs=out_specs, check_vma=False)
```

```python
import functools
import math

import jax
import jax.numpy as jnp
from jax import lax
from jax.experimental import pallas as pl
from jax.experimental.pallas import tpu as pltpu
from jax.sharding import PartitionSpec as P

HEADS = 12
HEAD_DIM = 64
SPAN = 8
EXT = 16
WIDE = HEAD_DIM + EXT
BIG = 2.0**30
SAFE_SUM = 2.0**100
VMEM = 24 * 2**20
SMALL = 16 * 2**20

bf16 = jnp.bfloat16
f32 = jnp.float32
norm_eps = 1e-12
base_log = math.log(1000.0)


def dot(left_op, right_op, left_dim, right_dim):
    return lax.dot_general(
        left_op, right_op, (((left_dim,), (right_dim,)), ((), ())), preferred_element_type=f32
    )


def ring_order(size):
    return list(range(0, size, 2)) + list(range(size - 1, 0, -2))


def ring_place(index, size):
    return jnp.where(index % 2 == 0, index // 2, size - 1 - index // 2)


def ring_index(place, size):
    place = place % size
    return jnp.where(place < size // 2, 2 * place, 2 * (size - 1 - place) + 1)


def ring_shift(value, step, size):
    order = ring_order(size)
    pairs = [
        (base + order[i], base + order[(i + step) % size])
        for base in range(0, lax.axis_size("fsdp"), size)
        for i in range(size)
    ]
    return lax.ppermute(value, "fsdp", pairs)


def seq_swap(value, mask):
    return lax.ppermute(value, "seq", [(i, i ^ mask) for i in range(lax.axis_size("seq"))])


def arrange_kernel(count, order, *refs):
    for i, ref in enumerate(refs[:count]):
        refs[-1][order[i]] = ref[...]


def arrange(blocks, order, after=()):
    return pl.pallas_call(
        functools.partial(arrange_kernel, len(blocks)),
        in_specs=[pl.BlockSpec(memory_space=pltpu.SMEM)]
        + [pl.BlockSpec(memory_space=pltpu.VMEM)] * len(blocks)
        + [pl.BlockSpec(memory_space=pl.ANY)] * len(after),
        out_specs=pl.BlockSpec(memory_space=pltpu.VMEM),
        out_shape=jax.ShapeDtypeStruct((len(blocks),) + blocks[0].shape, blocks[0].dtype),
        compiler_params=pltpu.CompilerParams(vmem_limit_bytes=SMALL),
        name="arrange",
    )(jnp.stack(order).astype(jnp.int32), *blocks, *after)


def arrange_runs_kernel(order, *refs):
    at = 0
    for ref in refs[:-1]:
        for k in range(ref.shape[0]):
            refs[-1][order[at]] = ref[k]
            at += 1


def arrange_runs(runs, order):
    return pl.pallas_call(
        arrange_runs_kernel,
        in_specs=[pl.BlockSpec(memory_space=pltpu.SMEM)]
        + [pl.BlockSpec(memory_space=pltpu.VMEM)] * len(runs),
        out_specs=pl.BlockSpec(memory_space=pltpu.VMEM),
        out_shape=jax.ShapeDtypeStruct((len(order),) + runs[0].shape[1:], runs[0].dtype),
        compiler_params=pltpu.CompilerParams(vmem_limit_bytes=VMEM),
        name="arrange_runs",
    )(jnp.stack(order).astype(jnp.int32), *runs)


def ring_gather(block, size, place):
    half = block.shape[0] // 2
    right, left = block, block
    blocks, order = [block], [ring_index(place, size)]
    for t in range(1, size // 2):
        right, left = ring_shift(right, 1, size), ring_shift(left, -1, size)
        blocks += [right, left]
        order += [ring_index(place - t, size), ring_index(place + t, size)]
    last = jnp.concatenate(
        [ring_shift(right[:half], 1, size), ring_shift(left[half:], -1, size)], axis=0
    )
    return blocks + [last], order + [ring_index(place + size // 2, size)]


def sum_kernel(counts, split, *refs):
    outs = refs[-len(counts) :]
    at = 0
    for which, (count, arrived) in enumerate(counts):
        blocks, got = refs[at : at + count], refs[at + count : at + count + arrived]
        at += count + arrived
        total = sum(ref[0].astype(f32) for ref in blocks)
        if split and arrived:
            half = total.shape[0] // 2
            cut = slice(0, half) if which == 0 else slice(half, 2 * half)
            other = slice(half, 2 * half) if which == 0 else slice(0, half)
            outs[which][cut, :] = (total[cut] + got[0][...].astype(f32)).astype(bf16)
            outs[which][other, :] = total[other].astype(bf16)
        else:
            total = total + sum(ref[...].astype(f32) for ref in got)
            outs[which][...] = total.astype(bf16)


def block_sums(directions, split, after):
    specs, ins = [], []
    for blocks, got in directions:
        for stacked, index in blocks:
            shape = (1,) + stacked.shape[1:]
            specs.append(pl.BlockSpec(shape, lambda _, index=index: (index, 0, 0)))
            ins.append(stacked)
        for value in got:
            specs.append(pl.BlockSpec(value.shape, lambda _: (0, 0)))
            ins.append(value)
    shape = directions[0][0][0][0].shape[1:]
    counts = [(len(blocks), len(got)) for blocks, got in directions]
    used = len(ins)

    def body(*refs):
        sum_kernel(counts, split, *refs[:used], *refs[used + len(after) :])

    return pl.pallas_call(
        body,
        grid=(1,),
        in_specs=specs + [pl.BlockSpec(memory_space=pl.ANY)] * len(after),
        out_specs=[pl.BlockSpec(shape, lambda _: (0, 0)) for _ in counts],
        out_shape=[jax.ShapeDtypeStruct(shape, bf16) for _ in counts],
        compiler_params=pltpu.CompilerParams(vmem_limit_bytes=SMALL),
        name="sums",
    )(*ins, *after)


def ring_scatter(blocks, size, after):
    after = {i: list(values) for i, values in enumerate(after)}
    (far,) = block_sums([(blocks(size // 2), [])], False, after.get(0, []))
    half = far.shape[0] // 2
    sent = [far]
    right = ring_shift(far[:half], 1, size)
    left = ring_shift(far[half:], -1, size)
    first = [right, left]
    for hop, t in enumerate(range(size // 2 - 1, 0, -1)):
        up, down = block_sums(
            [(blocks(t), [right]), (blocks(-t), [left])], hop == 0, after.get(hop + 1, [])
        )
        right, left = ring_shift(up, 1, size), ring_shift(down, -1, size)
        sent.append(up)
    (total,) = block_sums([(blocks(0), [right, left])], False, after.get(size // 2, []))
    return total, sent, first


def three_parts(value):
    high = value.astype(bf16).astype(f32)
    rest = value - high
    mid = rest.astype(bf16).astype(f32)
    return high, mid, rest - mid


def with_parts(base, value):
    high, mid, low = three_parts(value)
    lane = lax.broadcasted_iota(jnp.int32, base.shape, 1)
    filled = jnp.where(lane == HEAD_DIM, high, base)
    filled = jnp.where(lane == HEAD_DIM + 1, mid, filled)
    return jnp.where(lane == HEAD_DIM + 2, low, filled)


def first_kernel(heads, tile, where_ref, ext_ref, qt_ref, qe_ref, kv_ref, qx_ref, acc_ref):
    tokens = qt_ref.shape[1]
    ones = jnp.ones((EXT, tokens), bf16)
    ext = block_ext(ext_ref, where_ref, 0, tokens)
    for h in range(heads):
        rows = slice(h * HEAD_DIM, (h + 1) * HEAD_DIM)
        k_rows, v_rows = block_rows([kv_ref], h)
        keys = jnp.concatenate([k_rows, ext], axis=0)
        vals = jnp.concatenate([v_rows, ones], axis=0)
        for start in range(0, tokens, tile):
            cut = slice(start, start + tile)
            natural = qt_ref[rows, cut].astype(f32).T
            queries = jnp.concatenate([natural, qe_ref[cut, :].astype(f32)], axis=1)
            scores = dot(queries.astype(bf16), keys, 1, 0)
            top = jnp.max(scores, axis=1, keepdims=True)
            weights = jnp.exp(scores - top).astype(bf16)
            acc_ref[h, :, cut] = dot(vals, weights, 1, 1)
            qx_ref[h, cut, :] = with_parts(queries, top).astype(bf16)


def block_rows(refs, h):
    if len(refs) == 2:
        rows = slice(h * HEAD_DIM, (h + 1) * HEAD_DIM)
        return refs[0][rows, :], refs[1][rows, :]
    inner = refs[0].shape[0] // 2
    return (
        refs[0][h * HEAD_DIM : (h + 1) * HEAD_DIM, :],
        refs[0][inner + h * HEAD_DIM : inner + (h + 1) * HEAD_DIM, :],
    )


def block_ext(ext_ref, where_ref, index, tokens):
    return ext_ref[:, pl.ds(pl.multiple_of(where_ref[index] * tokens, tokens), tokens)]


def step_kernel(heads, tile, parts, where_ref, ext_ref, qx_ref, acc_in, *refs):
    acc_ref, tokens = refs[-1], qx_ref.shape[1]
    ones = jnp.ones((EXT, tokens), bf16)
    blocks, at = [], 0
    for b, part in enumerate(parts):
        blocks.append((refs[at : at + part], block_ext(ext_ref, where_ref, b, tokens)))
        at += part
    for h in range(heads):
        pairs = []
        for block, ext in blocks:
            k_rows, v_rows = block_rows(block, h)
            pairs.append(
                (jnp.concatenate([k_rows, ext], axis=0), jnp.concatenate([v_rows, ones], axis=0))
            )
        for start in range(0, tokens, tile):
            cut = slice(start, start + tile)
            total = acc_in[h, :, cut]
            for keys, vals in pairs:
                weights = jnp.exp(dot(qx_ref[h, cut, :], keys, 1, 0)).astype(bf16)
                total = total + dot(vals, weights, 1, 1)
            acc_ref[h, :, cut] = total


def finish_kernel(heads, tile, parts, where_ref, ext_ref, qx_ref, acc_ref, *refs):
    count = sum(parts)
    blocks = refs[:count]
    ot_ref, on_ref, qx2_ref, buf, acc, qx = refs[count:]
    tokens = qx_ref.shape[1]
    inner = buf.shape[1] // 2
    fine = True
    for h in range(heads):
        sums = acc_ref[h, HEAD_DIM : HEAD_DIM + 8, :]
        fine = jnp.logical_and(fine, jnp.logical_and(sums <= SAFE_SUM, sums >= 0.5))
    good = jnp.min(jnp.where(fine, 1.0, 0.0)) > 0.5
    acc[...] = acc_ref[...]
    qx[...] = qx_ref[...]

    @pl.when(jnp.logical_not(good))
    def _():
        small = tile // 2
        ones = jnp.ones((EXT, tokens), bf16)
        lane = lax.broadcasted_iota(jnp.int32, (small, WIDE), 1)
        inside = jnp.logical_and(lane >= HEAD_DIM, lane < HEAD_DIM + 3)
        at = 0
        for b, part in enumerate(parts):
            if part == 2:
                pltpu.sync_copy(blocks[at], buf.at[b, pl.ds(0, inner)])
                pltpu.sync_copy(blocks[at + 1], buf.at[b, pl.ds(inner, inner)])
            else:
                pltpu.sync_copy(blocks[at], buf.at[b])
            at += part

        def each(body):
            cuts = tokens // small

            def turn(step, carry):
                b, rest = step // (heads * cuts), step % (heads * cuts)
                h = rest // cuts
                cut = pl.ds(pl.multiple_of(rest % cuts * small, small), small)
                rows = pl.multiple_of(h * HEAD_DIM, HEAD_DIM)
                ext = block_ext(ext_ref, where_ref, b, tokens)
                keys = jnp.concatenate([buf[b, pl.ds(rows, HEAD_DIM), :], ext], axis=0)
                vals = buf[b, pl.ds(pl.multiple_of(inner + rows, HEAD_DIM), HEAD_DIM), :]
                body(h, cut, keys, jnp.concatenate([vals, ones], axis=0))
                return carry

            lax.fori_loop(0, len(parts) * heads * cuts, turn, 0)

        def raise_top(h, cut, keys, vals):
            base = qx[h, cut, :].astype(f32)
            old = jnp.sum(jnp.where(inside, base, 0.0), axis=1, keepdims=True)
            plain = jnp.where(inside, 0.0, base)
            scores = dot(plain.astype(bf16), keys, 1, 0)
            top = jnp.maximum(old, jnp.max(scores, axis=1, keepdims=True))
            qx[h, cut, :] = with_parts(plain, top).astype(bf16)

        def add_up(h, cut, keys, vals):
            weights = jnp.exp(dot(qx[h, cut, :], keys, 1, 0)).astype(bf16)
            acc[h, :, cut] += dot(vals, weights, 1, 1)

        each(raise_top)
        acc[...] = jnp.zeros_like(acc)
        each(add_up)

    lane = lax.broadcasted_iota(jnp.int32, (tile, WIDE), 1)
    inside = jnp.logical_and(lane >= HEAD_DIM, lane < HEAD_DIM + 3)
    for h in range(heads):
        rows = slice(h * HEAD_DIM, (h + 1) * HEAD_DIM)
        for start in range(0, tokens, tile):
            cut = slice(start, start + tile)
            block = acc[h, :, cut]
            normed = block[:HEAD_DIM, :] * (1.0 / block[HEAD_DIM : HEAD_DIM + 1, :])
            ot_ref[rows, cut] = normed.astype(bf16)
            stacked = jnp.concatenate([normed, jnp.log(block[HEAD_DIM:, :])], axis=0).T
            on_ref[h, cut, :] = stacked[:, :HEAD_DIM]
            base = qx[h, cut, :].astype(f32)
            top = jnp.sum(jnp.where(inside, base, 0.0), axis=1, keepdims=True)
            shift = top + stacked[:, HEAD_DIM : HEAD_DIM + 1]
            qx2_ref[h, cut, :] = with_parts(base, shift).astype(bf16)


def delta_kernel(heads, where, own_ref, got_ref, on_ref, dox_ref, dot_ref):
    tokens = own_ref.shape[1]
    for tile in range(2):
        cut = slice(tile * tokens, (tile + 1) * tokens)

        @pl.when(where[0] == tile)
        def _():
            dot_ref[:, cut] = own_ref[...]

        @pl.when(where[0] != tile)
        def _():
            dot_ref[:, cut] = got_ref[...]

        for h in range(heads):
            rows = slice(h * HEAD_DIM, (h + 1) * HEAD_DIM)
            natural = dot_ref[rows, cut].astype(f32).T
            delta = jnp.sum(natural * on_ref[h, cut, :], axis=1, keepdims=True)
            base = jnp.concatenate([natural, jnp.zeros((tokens, EXT), f32)], axis=1)
            dox_ref[h, cut, :] = with_parts(base, delta).astype(bf16)


def back_kernel(heads, q_tile, where_ref, ext_ref, qx_ref, dox_ref, qt_ref, dot_ref, dq_in, *refs):
    block, (dq_ref, dkv_ref) = refs[:-2], refs[-2:]
    tokens, inner = qt_ref.shape[1], qt_ref.shape[0]
    ext = block_ext(ext_ref, where_ref, 0, tokens)
    for h in range(heads):
        rows = slice(h * HEAD_DIM, (h + 1) * HEAD_DIM)
        k_rows, v_rows = block_rows(block, h)
        keys = jnp.concatenate([k_rows, ext], axis=0)
        vals = jnp.concatenate([v_rows, ext], axis=0)
        d_key, d_value = 0.0, 0.0
        for start in range(0, tokens, q_tile):
            cut = slice(start, start + q_tile)
            weights = jnp.exp(dot(qx_ref[h, cut, :], keys, 1, 0))
            shifted = dot(dox_ref[h, cut, :], vals, 1, 0)
            d_scores = (weights * shifted).astype(bf16)
            d_value = d_value + dot(dot_ref[rows, cut], weights.astype(bf16), 1, 0)
            d_key = d_key + dot(qt_ref[rows, cut], d_scores, 1, 0)
            dq_ref[rows, cut] = dq_in[rows, cut] + dot(k_rows, d_scores, 1, 1)
        dkv_ref[rows, :] = d_key.astype(bf16)
        dkv_ref[inner + h * HEAD_DIM : inner + (h + 1) * HEAD_DIM, :] = d_value.astype(bf16)


def pack_kernel(parts, s_ref, up_ref, gate_ref, down_ref, last_ref, *refs):
    vectors, out_ref = refs[:4], refs[4]
    s = s_ref[0]
    rows = up_ref.shape[0]
    width = parts * rows
    for i, ref in enumerate((up_ref, gate_ref)):
        pieces = []
        for k in range(parts):
            run = ref[:, 4 * rows * k : 4 * rows * (k + 1)]
            pieces.append(pltpu.roll(run, (4 * rows - s * rows) % (4 * rows), 1)[:, :rows])
        out_ref[:, i * width : (i + 1) * width] = jnp.concatenate(pieces, axis=1).astype(bf16)
    own = down_ref[pl.ds(pl.multiple_of(s * rows, 8), rows), :]
    out_ref[:, 2 * width : 3 * width] = own.astype(bf16)
    inner = width // 4
    columns = pltpu.roll(last_ref[...], (width - s * inner) % width, 1)[:, :inner]
    spare = out_ref.shape[1] - 3 * width - inner
    side = jnp.concatenate([ref[...] for ref in vectors] + [jnp.zeros((4, rows), f32)], axis=0).T
    out_ref[:, 3 * width :] = jnp.concatenate(
        [columns, side, jnp.zeros((rows, spare - 8), f32)], axis=1
    ).astype(bf16)


def unpack_kernel(parts, width, *refs):
    quarters, (up_ref, gate_ref, down_ref, out_ref), vectors = refs[:4], refs[4:8], refs[8:]
    rows = up_ref.shape[0]
    inner = width // 4
    for i, ref in enumerate((up_ref, gate_ref)):
        for k in range(parts):
            at = i * width + k * rows
            ref[:, 4 * rows * k : 4 * rows * (k + 1)] = jnp.concatenate(
                [q[:, at : at + rows].astype(f32) for q in quarters], axis=1
            )
    for g, q in enumerate(quarters):
        down_ref[g * rows : (g + 1) * rows, :] = q[:, 2 * width : 3 * width].astype(f32)
    at = 3 * width
    out_ref[...] = jnp.concatenate([q[:, at : at + inner].astype(f32) for q in quarters], axis=1)
    sums = sum(q[:, at + inner :].astype(f32) for q in quarters).T
    for i, ref in enumerate(vectors):
        ref[...] = sums[i : i + 1, :]


def ordered_kernel(kernel, count, order, *refs):
    buffer = refs[-1]
    for i in range(count):
        buffer[order[i]] = refs[i][...]
    kernel(*[buffer.at[i] for i in range(count)], *refs[count:-1])


def grads_kernel(order, hidden_ref, branch_ref, heads_ref, first_sums, second_sums, *refs):
    sides, mine_ref, runs, buffer = (refs[:4], refs[4:8]), refs[8], refs[9:-1], refs[-1]
    count, rows = mine_ref.shape[0], mine_ref.shape[1]
    width = hidden_ref.shape[1]
    hidden_t = hidden_ref[...].T
    heads = heads_ref[...].reshape(width, heads_ref.shape[2])
    vectors = (first_sums[...] + second_sums[...]).T
    vectors = jnp.concatenate(
        [vectors, jnp.zeros((width, mine_ref.shape[2] - 3 * width - width // 4 - 8), f32)], axis=1
    ).astype(bf16)
    for which, (up_ref, gate_ref, inner_ref, cols_ref) in enumerate(sides):

        def put(value, at):
            for k in range(count):
                buffer[k, :, at : at + value.shape[1]] = value[k * rows : (k + 1) * rows]

        put(dot(hidden_t, up_ref[...], 1, 0).astype(bf16), 0)
        put(dot(hidden_t, gate_ref[...], 1, 0).astype(bf16), width)
        put(dot(inner_ref[...].T, branch_ref[...], 1, 0).astype(bf16), 2 * width)
        tail = dot(heads, cols_ref[...], 1, 0).astype(bf16)
        rest = vectors if which == 0 else jnp.zeros_like(vectors)
        put(jnp.concatenate([tail, rest], axis=1), 3 * width)
        if which == 0:
            for i in range(count):
                mine_ref[i] = buffer[order[i]]
        else:
            at = 0
            for run in runs:
                for k in range(run.shape[0]):
                    run[k] = buffer[order[at]]
                    at += 1


def tail_kernel(
    order, where, dq_ref, dkv_ref, right_ref, left_ref, cos_ref, sin_ref, x_ref, w_ref, *refs
):
    grad_ref, sent_ref, kept_ref, raw, buffer = refs
    inner = dq_ref.shape[0]
    cosine, sine = cos_ref[...], sin_ref[...]
    d_kv = dkv_ref[...].astype(f32) + right_ref[...].astype(f32) + left_ref[...].astype(f32)

    def put(base):
        def at_base(at, value):
            raw[base + at : base + at + value.shape[0], :] = value.astype(bf16)

        return at_base

    turn_rows(dq_ref[...] * HEAD_DIM**-0.5, cosine, -sine, put(0))
    turn_rows(d_kv[:inner], cosine, -sine, put(inner))
    raw[2 * inner :, :] = d_kv[inner:].astype(bf16)
    projected = raw[...].T
    count, rows = grad_ref.shape[0], grad_ref.shape[1]
    width, quarter = x_ref.shape[2], x_ref.shape[1]
    terms = dot(projected, w_ref[...].reshape(width, 3 * inner), 1, 1)
    for core in range(2):
        side = [terms[(2 * y + core) * quarter : (2 * y + core + 1) * quarter] for y in range(2)]

        @pl.when(where[1] == core)
        def _():
            for y in range(2):
                kept_ref[y] = side[y]

        @pl.when(where[1] != core)
        def _():
            for y in range(2):
                sent_ref[y] = side[y].astype(bf16)

    grad = dot(x_ref[...].reshape(4 * quarter, width).T, projected, 1, 0).astype(bf16)
    for k in range(count):
        buffer[k] = grad[k * rows : (k + 1) * rows]
    for i in range(count):
        grad_ref[i] = buffer[order[i]]


def unpack_qkv_kernel(*refs):
    quarters, out_ref = refs[:4], refs[4]
    inner = quarters[0].shape[1] // 3
    out_ref[...] = jnp.concatenate(
        [q[:, i * inner : (i + 1) * inner].astype(f32) for i in range(3) for q in quarters], axis=1
    )


def tables_kernel(at_ref, docs_ref, key_ref, query_ref):
    length, tokens = key_ref.shape[1], query_ref.shape[0]

    def kinds(start, count):
        docs = docs_ref[:, pl.ds(pl.multiple_of(start, count), count)] - at_ref[1]
        docs = jnp.broadcast_to(docs, (EXT, count))
        row = lax.broadcasted_iota(jnp.int32, (EXT, count), 0)
        return row, docs == row - 3

    row, same = kinds(at_ref[0], length)
    mark = jnp.where(jnp.logical_or(row < 3, jnp.logical_not(same)), -1.0, 0.0)
    key_ref[...] = jnp.where(row < 6, mark, 0.0).astype(bf16)
    row, same = kinds(at_ref[2], tokens)
    inside = jnp.logical_and(same, jnp.logical_and(row >= 3, row < 6))
    query_ref[...] = jnp.where(inside, BIG, 0.0).T.astype(bf16)


def turn_rows(value, cosine, sine, put):
    half = HEAD_DIM // 2
    for at in range(0, value.shape[0], HEAD_DIM):
        lead, last = value[at : at + half], value[at + half : at + HEAD_DIM]
        put(at, lead * cosine - last * sine)
        put(at + half, last * cosine + lead * sine)


def project_kernel(count, order, places, cos_ref, sin_ref, *refs):
    weights, tokens = refs[:count], refs[count : count + 4]
    q_ref, kv_ref, x_ref, w_ref = refs[count + 4 :]
    inner = q_ref.shape[0]
    for i, ref in enumerate(weights):
        w_ref[order[i]] = ref[...]
    for i, ref in enumerate(tokens):
        x_ref[places[i]] = ref[...]
    cosine, sine = cos_ref[...], sin_ref[...]
    width = x_ref.shape[2]
    matrix = w_ref[...].reshape(width, 3 * inner).T
    rows = x_ref[...].reshape(-1, width)

    def put_q(at, value):
        q_ref[at : at + value.shape[0], :] = value.astype(bf16) * bf16(HEAD_DIM**-0.5)

    def put_k(at, value):
        kv_ref[at : at + value.shape[0], :] = value.astype(bf16)

    turn_rows(dot(matrix[:inner], rows, 1, 1), cosine, sine, put_q)
    turn_rows(dot(matrix[inner : 2 * inner], rows, 1, 1), cosine, sine, put_k)
    kv_ref[inner:, :] = dot(matrix[2 * inner :], rows, 1, 1).astype(bf16)


def outer_kernel(places, *refs):
    parts, (out_ref, vec_ref, buffer) = refs[:4], refs[4:]
    inner = out_ref.shape[1] // 4
    for i, ref in enumerate(parts):
        buffer[places[i]] = ref[...]
    out_ref[...] = jnp.concatenate([buffer[g, :, :inner] for g in range(4)], axis=1)
    vec_ref[...] = parts[0][:, inner:].astype(f32).T[:8]


def gate(value, after):
    return pl.pallas_call(
        lambda *refs: None,
        in_specs=[pl.BlockSpec(memory_space=pl.ANY)] * (1 + len(after)),
        out_specs=pl.BlockSpec(memory_space=pl.ANY),
        out_shape=jax.ShapeDtypeStruct(value.shape, value.dtype),
        input_output_aliases={0: 0},
        name="gate",
    )(value, *after)


def norm_parts(rows_in):
    centre = rows_in - jnp.mean(rows_in, axis=-1, keepdims=True)
    rstd = lax.rsqrt(jnp.mean(centre * centre, axis=-1, keepdims=True) + norm_eps)
    return centre * rstd, rstd


def norm_grad(normed, rstd, grad, gain):
    scaled = grad * gain
    mean = jnp.mean(scaled, axis=-1, keepdims=True)
    return rstd * (scaled - mean - normed * jnp.mean(scaled * normed, axis=-1, keepdims=True))


def ff_weights(ref):
    width = ref.shape[0]
    return ref[:, :width], ref[:, width : 2 * width], ref[:, 2 * width : 3 * width]


def forward_kernel(places, where, *refs):
    parts, (x_ref, out_ref, vec_ref, mine_ref, other_ref) = refs[:4], refs[4:9]
    heads_ref, hidden_ref, kept_ref, sent_ref, normed_ref, rstd_ref = refs[9:15]
    acts = (refs[15:18], refs[18:21])
    width, rows = hidden_ref.shape[1], kept_ref.shape[0]
    side, core = where[0], where[1]
    for i, ref in enumerate(parts):
        heads_ref[places[i]] = ref[...]
    for tile in range(2):
        cut = slice(tile * rows, (tile + 1) * rows)
        start = pl.multiple_of((2 * side + tile) * rows, rows)
        heads = heads_ref[:, :, cut].reshape(width, rows).T
        first = x_ref[pl.ds(start, rows), :].astype(f32) + dot(heads, out_ref[...], 1, 0)
        normed, rstd = norm_parts(first)
        hidden = normed * vec_ref[0:1] + vec_ref[1:2]
        low = hidden.astype(bf16)
        hidden_ref[cut, :] = low
        branch = 0.0
        for w_ref, (up_ref, gate_ref, inner_ref) in zip((mine_ref, other_ref), acts):
            up_w, gate_w, down_w = ff_weights(w_ref)
            up, gate = dot(low, up_w, 1, 0), dot(low, gate_w, 1, 0)
            inner = (gate * lax.logistic(gate) * up).astype(bf16)
            up_ref[cut, :], gate_ref[cut, :], inner_ref[cut, :] = up, gate, inner
            branch = branch + dot(inner, down_w, 1, 0)

        @pl.when(core == tile)
        def _():
            kept_ref[...] = hidden + branch
            normed_ref[...] = normed
            rstd_ref[...] = jnp.broadcast_to(rstd, rstd_ref.shape)

        @pl.when(core != tile)
        def _():
            sent_ref[...] = branch.astype(bf16)


def second_kernel(kept_ref, got_ref, grad_ref, vec_ref, result_ref, d_ref, low_ref, sums_ref):
    normed, rstd = norm_parts(kept_ref[...] + got_ref[...].astype(f32))
    gain = vec_ref[2:3]
    result_ref[...] = (normed * gain + vec_ref[3:4]).astype(bf16)
    grad = grad_ref[...].astype(f32)
    d_second = norm_grad(normed, rstd, grad, gain)
    d_ref[...] = d_second
    low_ref[...] = d_second.astype(bf16)
    sums_ref[...] = jnp.zeros_like(sums_ref)
    sums_ref[2:3] = jnp.sum(grad * normed, axis=0, keepdims=True)
    sums_ref[3:4] = jnp.sum(grad, axis=0, keepdims=True)


def backward_kernel(where, own_ref, got_ref, mine_ref, other_ref, *refs):
    acts = (refs[:2], refs[2:4])
    branch_ref, kept_ref, sent_ref = refs[4:7]
    outs = (refs[7:9], refs[9:11])
    rows, core = kept_ref.shape[0], where[1]
    branch_ref[pl.ds(pl.multiple_of(core * rows, rows), rows), :] = own_ref[...]
    branch_ref[pl.ds(pl.multiple_of((1 - core) * rows, rows), rows), :] = got_ref[...]
    for tile in range(2):
        cut = slice(tile * rows, (tile + 1) * rows)
        branch = branch_ref[cut, :]
        total = 0.0
        for w_ref, (up_ref, gate_ref), (d_up_ref, d_gate_ref) in zip(
            (mine_ref, other_ref), acts, outs
        ):
            up_w, gate_w, down_w = ff_weights(w_ref)
            d_inner = dot(branch, down_w, 1, 1)
            up, gate = up_ref[cut, :], gate_ref[cut, :]
            sig = lax.logistic(gate)
            d_gate = (d_inner * up * sig * (1.0 + gate * (1.0 - sig))).astype(bf16)
            d_up = (d_inner * gate * sig).astype(bf16)
            d_up_ref[cut, :], d_gate_ref[cut, :] = d_up, d_gate
            total = total + dot(d_up, up_w, 1, 1) + dot(d_gate, gate_w, 1, 1)

        @pl.when(core == tile)
        def _():
            kept_ref[...] = total

        @pl.when(core != tile)
        def _():
            sent_ref[...] = total.astype(bf16)


def first_back_kernel(
    kept_ref, got_ref, d_second_ref, normed_ref, rstd_ref, vec_ref, d_ref, low_ref, sums_ref
):
    d_hidden = d_second_ref[...] + kept_ref[...] + got_ref[...].astype(f32)
    normed = normed_ref[...]
    d_first = norm_grad(normed, rstd_ref[:, 0:1], d_hidden, vec_ref[0:1])
    d_ref[...] = d_first
    low_ref[...] = d_first.astype(bf16)
    sums_ref[...] = jnp.zeros_like(sums_ref)
    sums_ref[0:1] = jnp.sum(d_hidden * normed, axis=0, keepdims=True)
    sums_ref[1:2] = jnp.sum(d_hidden, axis=0, keepdims=True)


def heads_back_kernel(
    where, own_ref, got_ref, out_ref, own_heads_ref, sent_ref, own_cols_ref, other_cols_ref, branch
):
    side, core = where[0], where[1]
    rows, inner = own_ref.shape[0], sent_ref.shape[0]
    branch[pl.ds(pl.multiple_of(core * rows, rows), rows), :] = own_ref[...]
    branch[pl.ds(pl.multiple_of((1 - core) * rows, rows), rows), :] = got_ref[...]
    for which, ref in ((1 - side, sent_ref), (side, own_heads_ref)):
        at = pl.multiple_of((2 * which + core) * inner, inner)
        ref[...] = dot(out_ref[pl.ds(at, inner), :], branch[...], 1, 1).astype(bf16)
    for group in range(4):
        value = branch[:, group * inner : (group + 1) * inner]

        @pl.when(2 * side + core == group)
        def _():
            own_cols_ref[...] = value

        @pl.when(2 * (1 - side) + core == group)
        def _():
            other_cols_ref[...] = value


def input_mid_kernel(where, kept_ref, got_ref, kept_out, sent_out):
    for y in range(2):
        value = kept_ref[y] + got_ref[y].astype(f32)

        @pl.when(where[0] == y)
        def _():
            kept_out[...] = value

        @pl.when(where[0] != y)
        def _():
            sent_out[...] = value.astype(bf16)


def input_end_kernel(first_ref, kept_ref, got_ref, out_ref):
    out_ref[...] = (first_ref[...] + kept_ref[...] + got_ref[...].astype(f32)).astype(bf16)


def piped_call(kernel, outs, ins, name, after=()):
    count = len(ins)

    def body(*refs):
        kernel(*refs[:count], *refs[count + len(after) :])

    def whole(shape):
        return pl.BlockSpec(shape, lambda _: (0,) * len(shape))

    return pl.pallas_call(
        body,
        grid=(1,),
        in_specs=[pl.BlockSpec(memory_space=pltpu.SMEM)]
        + [whole(value.shape) for value in ins[1:]]
        + [pl.BlockSpec(memory_space=pl.ANY)] * len(after),
        out_specs=[whole(shape) for shape, _ in outs],
        out_shape=[jax.ShapeDtypeStruct(shape, dtype) for shape, dtype in outs],
        compiler_params=pltpu.CompilerParams(vmem_limit_bytes=SMALL),
        name=name,
    )(*ins, *after)


def local_call(kernel, outs, ins, flops, name, scratch=(), spaces=None, after=()):
    limit = SMALL if name.startswith("attend") or name in ("outer", "tables", "project") else VMEM
    spaces = list(spaces or [pltpu.VMEM] * len(ins))
    count = len(ins)

    def body(*refs):
        kernel(*refs[:count], *refs[count + len(after) :])

    return pl.pallas_call(
        body,
        in_specs=[pl.BlockSpec(memory_space=space) for space in spaces + [pl.ANY] * len(after)],
        out_specs=[pl.BlockSpec(memory_space=pltpu.VMEM) for _ in outs],
        out_shape=[jax.ShapeDtypeStruct(shape, dtype) for shape, dtype in outs],
        scratch_shapes=list(scratch),
        compiler_params=pltpu.CompilerParams(vmem_limit_bytes=limit),
        cost_estimate=pl.CostEstimate(flops=flops * 5, bytes_accessed=2**20, transcendentals=0),
        name=name,
    )(*ins, *after)


def local(
    layer_input,
    out_grad,
    doc_ids,
    w_qkv,
    w_out,
    norm1_gain,
    norm1_bias,
    w_up,
    w_gate,
    w_down,
    norm2_gain,
    norm2_bias,
):
    fsdp = lax.axis_size("fsdp")
    groups = lax.axis_size("seq")
    f = lax.axis_index("fsdp")
    s = lax.axis_index("seq")
    side, core = s // 2, s % 2
    tok_rows, width = layer_input.shape
    w_rows = w_qkv.shape[0]
    inner = width // groups
    heads = inner // HEAD_DIM
    group_rows = tok_rows * groups
    half_rows = group_rows // 2
    length = SPAN * group_rows
    place = ring_place(f, fsdp)
    spot = ring_place(f % SPAN, SPAN)
    base = f // SPAN * SPAN

    seq_order = [s, s ^ 2, s ^ 1, s ^ 3]
    seq_places = jnp.stack(seq_order).astype(jnp.int32)
    where = jnp.stack([side, core]).astype(jnp.int32)
    smem, vmem = pltpu.SMEM, pltpu.VMEM
    aligned = w_rows * groups % 128 == 0 and w_rows % 16 == 0

    def quarter(matrix, start):
        return lax.dynamic_slice_in_dim(matrix, start + s * inner, inner, 1)

    qkv_own = jnp.concatenate([quarter(w_qkv, i * width) for i in range(3)], axis=1).astype(bf16)
    x_side = seq_swap(layer_input, 2)
    x_core = seq_swap(layer_input, 1)
    x_far = seq_swap(layer_input, 3)
    qkv_blocks, order = ring_gather(qkv_own, fsdp, place)
    early, qkv_second = qkv_blocks[-3:-1], qkv_blocks[3:5]
    ring_order_now = jnp.stack(order).astype(jnp.int32)
    if not aligned:
        qkv_blocks = [arrange(qkv_blocks, order).reshape(width, 3 * inner)]
        ring_order_now = jnp.zeros((1,), jnp.int32)
    key_ext, query_ext = local_call(
        tables_kernel,
        [((EXT, length), bf16), ((group_rows, EXT), bf16)],
        [
            jnp.stack([f // SPAN * length, f // SPAN * 3, f * group_rows]).astype(jnp.int32),
            doc_ids[None, :],
        ],
        2**20,
        "tables",
        spaces=[smem, vmem],
        after=[*early, x_core, x_far],
    )
    positions = f % SPAN * group_rows + jnp.arange(group_rows, dtype=jnp.int32)
    steps = jnp.arange(HEAD_DIM // 2, dtype=f32)
    freqs = jnp.exp(steps * (-2.0 * base_log / HEAD_DIM))
    angles = freqs[:, None] * positions.astype(f32)[None, :]
    cosine, sine = jnp.cos(angles), jnp.sin(angles)

    queries, own_kv, x_all, qkv_full = local_call(
        functools.partial(project_kernel, len(qkv_blocks)),
        [
            ((inner, group_rows), bf16),
            ((2 * inner, group_rows), bf16),
            ((groups, tok_rows, width), bf16),
            ((len(qkv_blocks),) + qkv_blocks[0].shape, bf16),
        ],
        [
            ring_order_now,
            seq_places,
            cosine,
            sine,
            *qkv_blocks,
            layer_input,
            x_side,
            x_core,
            x_far,
        ],
        2**32,
        "project",
        spaces=[smem, smem] + [vmem] * (len(qkv_blocks) + 6),
    )

    def ff_quarter(matrix):
        split = matrix.reshape(w_rows, fsdp, groups, w_rows)
        return lax.dynamic_index_in_dim(split, s, 2, False).reshape(w_rows, width)

    spare = 256 - inner % 256
    packed_width = 3 * width + inner + spare
    if aligned:
        (own,) = piped_call(
            functools.partial(pack_kernel, fsdp),
            [((w_rows, packed_width), bf16)],
            [
                s.reshape(1),
                w_up,
                w_gate,
                w_down,
                w_out,
                *[v[None, :] for v in (norm1_gain, norm1_bias, norm2_gain, norm2_bias)],
            ],
            "pack",
            after=[*qkv_second, x_core, x_far],
        )
    else:
        down_rows = lax.dynamic_slice_in_dim(w_down, s * w_rows, w_rows, 0)
        gains = jnp.stack([norm1_gain, norm1_bias, norm2_gain, norm2_bias], axis=1)
        own = jnp.concatenate(
            [
                ff_quarter(w_up),
                ff_quarter(w_gate),
                down_rows,
                quarter(w_out, 0),
                gains,
                jnp.zeros((w_rows, spare - 4), f32),
            ],
            axis=1,
        ).astype(bf16)
    mine, order = ring_gather(own, fsdp, place)
    steady = [jnp.int32(i) for i in range(fsdp)]
    others = [seq_swap(own, 2)[None]]
    for start in range(1, fsdp, 2):
        run = mine[start : start + 2]
        others.append(seq_swap(arrange(run, steady[: len(run)], others[-1:]), 2))
    others = arrange_runs(others, order).reshape(width, own.shape[1])
    mine = arrange(mine, order).reshape(width, own.shape[1])
    out_own, out_side = mine[:, 3 * width :], others[:, 3 * width :]
    out_core, out_far = seq_swap(out_own, 1), seq_swap(out_side, 1)
    out_full, vectors = local_call(
        outer_kernel,
        [((width, width), bf16), ((8, width), f32)],
        [seq_places, out_own, out_side, out_core, out_far],
        2**20,
        "outer",
        scratch=[pltpu.VMEM((groups,) + out_own.shape, bf16)],
        spaces=[smem] + [vmem] * 4,
    )

    def spots(*offsets):
        return jnp.stack([ring_index(spot + o, SPAN) for o in offsets]).astype(jnp.int32)

    block_flops = 8 * 256 * heads * group_rows * group_rows
    acc_out = ((heads, WIDE, group_rows), f32)
    wide_out = ((heads, group_rows, WIDE), bf16)
    tile = min(512, group_rows)
    qx, acc = local_call(
        functools.partial(first_kernel, heads, tile),
        [wide_out, acc_out],
        [spots(0), key_ext, queries, query_ext, own_kv],
        block_flops,
        "attend_own",
        spaces=[smem] + [vmem] * 4,
    )
    far = SPAN // 2
    blocks = {0: (own_kv,)}
    right, left = own_kv, own_kv
    for t in range(1, far + 1):
        if t < far:
            right, left = ring_shift(right, 1, SPAN), ring_shift(left, -1, SPAN)
            blocks[-t], blocks[t] = (right,), (left,)
            now = [-t, t]
        else:
            blocks[t] = (ring_shift(right[:inner], 1, SPAN), ring_shift(left[inner:], -1, SPAN))
            now = [t]
        refs = [ref for o in now for ref in blocks[o]]
        (acc,) = local_call(
            functools.partial(step_kernel, heads, tile, [len(blocks[o]) for o in now]),
            [acc_out],
            [spots(*now), key_ext, qx, acc, *refs],
            block_flops * len(now),
            "attend_step",
            spaces=[smem] + [vmem] * (3 + len(refs)),
            after=[mine] if t == far - 1 else [],
        )
    offsets = sorted(blocks)
    refs = [ref for o in offsets for ref in blocks[o]]
    heads_t, heads_n, qx = local_call(
        functools.partial(
            finish_kernel, heads, min(512, group_rows), [len(blocks[o]) for o in offsets]
        ),
        [((inner, group_rows), bf16), ((heads, group_rows, HEAD_DIM), f32), wide_out],
        [spots(*offsets), key_ext, qx, acc, *refs],
        block_flops // 4,
        "attend_finish",
        scratch=[
            pltpu.VMEM((SPAN, 2 * inner, group_rows), bf16),
            pltpu.VMEM(*acc_out),
            pltpu.VMEM(*wide_out),
        ],
        spaces=[smem] + [vmem] * 3 + [pl.ANY] * len(refs),
        after=[out_full],
    )

    def my_half(value, axis):
        return lax.dynamic_slice_in_dim(value, side * half_rows, half_rows, axis)

    def other_half(value, axis):
        return lax.dynamic_slice_in_dim(value, (1 - side) * half_rows, half_rows, axis)

    heads_own = my_half(heads_t, 1)
    heads_side = seq_swap(other_half(heads_t, 1), 2)
    heads_core = seq_swap(heads_own, 1)
    heads_far = seq_swap(heads_side, 1)
    half_low = ((half_rows, width), bf16)
    half_acts = [((half_rows, width), f32)] * 2 + [half_low]
    own_low, own_full = ((tok_rows, width), bf16), ((tok_rows, width), f32)
    sums_out = ((8, width), f32)
    heads_all, hidden_low, kept, sent, normed_one, rstd_one, *acts = local_call(
        forward_kernel,
        [
            ((groups, inner, half_rows), bf16),
            half_low,
            own_full,
            own_low,
            own_full,
            ((tok_rows, 128), f32),
            *half_acts,
            *half_acts,
        ],
        [
            seq_places,
            where,
            heads_own,
            heads_side,
            heads_core,
            heads_far,
            x_all.reshape(group_rows, width),
            out_full,
            vectors,
            mine,
            others,
        ],
        2**33,
        "feed_forward",
        spaces=[smem, smem] + [vmem] * 9,
    )
    result, d_second, d_branch_two, sums_two = local_call(
        second_kernel,
        [own_low, own_full, own_low, sums_out],
        [kept, seq_swap(sent, 1), out_grad, vectors],
        2**20,
        "second_norm",
    )
    d_branch_two, kept, sent, d_up, d_gate, d_up_other, d_gate_other = local_call(
        backward_kernel,
        [half_low, own_full, own_low] + [half_low] * 4,
        [
            where,
            d_branch_two,
            seq_swap(d_branch_two, 1),
            mine,
            others,
            acts[0],
            acts[1],
            acts[3],
            acts[4],
        ],
        2**33,
        "feed_back",
        spaces=[smem] + [vmem] * 8,
    )
    d_first, d_branch_one, sums_one = local_call(
        first_back_kernel,
        [own_full, own_low, sums_out],
        [kept, seq_swap(sent, 1), d_second, normed_one, rstd_one, vectors],
        2**20,
        "first_norm_back",
    )

    part = ((inner, half_rows), bf16)
    columns = ((half_rows, inner), bf16)
    d_heads_own, d_heads_sent, cols_own, cols_other = local_call(
        heads_back_kernel,
        [part, part, columns, columns],
        [where, d_branch_one, seq_swap(d_branch_one, 1), out_full],
        2**30,
        "heads_back",
        scratch=[pltpu.VMEM(*half_low)],
        spaces=[smem] + [vmem] * 3,
    )
    dox, d_heads_t = local_call(
        functools.partial(delta_kernel, heads),
        [wide_out, ((inner, group_rows), bf16)],
        [where, d_heads_own, seq_swap(d_heads_sent, 2), heads_n],
        block_flops // 4,
        "delta",
        spaces=[smem] + [vmem] * 3,
    )

    steps_out = [fsdp // 2] + [o for t in range(fsdp // 2 - 1, 0, -1) for o in (t, -t)] + [0]
    step_of = {o: i for i, o in enumerate(steps_out)}
    ring_rows = jnp.stack([ring_index(place + o, fsdp) for o in steps_out]).astype(jnp.int32)
    packed = ((fsdp, w_rows, own.shape[1]), bf16)
    cuts = [0, 3 * fsdp // 8, 5 * fsdp // 8, fsdp]
    grads_mine, *grads_other = local_call(
        grads_kernel,
        [packed] + [((b - a,) + packed[0][1:], bf16) for a, b in zip(cuts, cuts[1:])],
        [
            ring_rows,
            hidden_low,
            d_branch_two,
            heads_all,
            sums_one,
            sums_two,
            d_up,
            d_gate,
            acts[2],
            cols_own,
            d_up_other,
            d_gate_other,
            acts[5],
            cols_other,
        ],
        2**32,
        "grads",
        scratch=[pltpu.VMEM(*packed)],
        spaces=[smem] + [vmem] * 13,
    )

    got = [seq_swap(run, 2) for run in grads_other]

    def grads_part(offset):
        i = step_of[offset]
        which = sum(i >= cut for cut in cuts[1:])
        return [(grads_mine, i), (got[which], i - cuts[which])]

    d_query = jnp.zeros((inner, group_rows), f32)

    def back(offset, d_query, after):
        return local_call(
            functools.partial(back_kernel, heads, min(256, group_rows)),
            [((inner, group_rows), f32), ((2 * inner, group_rows), bf16)],
            [spots(offset), key_ext, qx, dox, queries, d_heads_t, d_query, *blocks[offset]],
            block_flops * 2,
            "attend_back",
            spaces=[smem] + [vmem] * (6 + len(blocks[offset])),
            after=after,
        )

    d_query, d_far = back(far, d_query, [])
    d_query, up = back(far - 1, d_query, [])
    d_query, down = back(1 - far, d_query, [])
    right, left = ring_shift(d_far[:inner], 1, SPAN), ring_shift(d_far[inner:], -1, SPAN)
    up = jnp.concatenate([up[:inner] + right, up[inner:]], axis=0)
    down = jnp.concatenate([down[:inner], down[inner:] + left], axis=0)
    after = [right, left]
    for t in range(far - 2, 0, -1):
        d_query, next_up = back(t, d_query, after)
        right, left = ring_shift(up, 1, SPAN), ring_shift(down, -1, SPAN)
        d_query, next_down = back(-t, d_query, [])
        after = [right, left]
        up, down = next_up + right, next_down + left
    right, left = ring_shift(up, 1, SPAN), ring_shift(down, -1, SPAN)
    d_query, d_kv = back(0, d_query, after)
    grads_sent = []
    if fsdp == SPAN:
        half = w_rows // 2
        (grads_far,) = block_sums([(grads_part(far), [])], False, [])
        up, down = block_sums(
            [
                (grads_part(far - 1), [ring_shift(grads_far[:half], 1, fsdp)]),
                (grads_part(1 - far), [ring_shift(grads_far[half:], -1, fsdp)]),
            ],
            True,
            [d_kv, got[1]],
        )
        grads_sent = [ring_shift(up, 1, fsdp), ring_shift(down, -1, fsdp)]
    grad_qkv, sent, kept = local_call(
        tail_kernel,
        [
            ((fsdp, w_rows, 3 * inner), bf16),
            ((2, tok_rows, width), bf16),
            ((2, tok_rows, width), f32),
        ],
        [
            ring_rows,
            where,
            d_query,
            d_kv,
            right,
            left,
            cosine,
            sine,
            x_all,
            qkv_full,
        ],
        2**32,
        "tail",
        scratch=[
            pltpu.VMEM((3 * inner, group_rows), bf16),
            pltpu.VMEM((fsdp, w_rows, 3 * inner), bf16),
        ],
        spaces=[smem, smem] + [vmem] * 8,
        after=grads_sent,
    )
    kept, sent = local_call(
        input_mid_kernel,
        [own_full, own_low],
        [where, kept, seq_swap(sent, 1)],
        2**20,
        "input_mid",
        spaces=[smem, vmem, vmem],
    )
    (d_input,) = local_call(
        input_end_kernel, [own_low], [d_first, kept, seq_swap(sent, 2)], 2**20, "input_end"
    )

    def qkv_part(offset):
        return [(grad_qkv, step_of[offset])]

    if fsdp == SPAN:
        qkv_own_grad, qkv_sent, qkv_first = ring_scatter(
            qkv_part, fsdp, [[], [kept]] + [[]] * (far - 3) + [[d_input]]
        )
        right, left = grads_sent
        for hop, t in enumerate(range(far - 2, 0, -1)):
            up, down = block_sums(
                [(grads_part(t), [right]), (grads_part(-t), [left])],
                False,
                [qkv_sent[hop + 1]] if hop else qkv_first,
            )
            right, left = ring_shift(up, 1, fsdp), ring_shift(down, -1, fsdp)
        (grads_own,) = block_sums([(grads_part(0), [right, left])], False, [qkv_sent[-1]])
    else:
        qkv_own_grad, *_ = ring_scatter(qkv_part, fsdp, [])
        grads_own, *_ = ring_scatter(grads_part, fsdp, [])

    def seq_gather(value, after):
        other = gate(seq_swap(value, 2), after) if after else seq_swap(value, 2)
        return [value, other, seq_swap(value, 1), seq_swap(other, 1)]

    qkv_parts = seq_gather(qkv_own_grad, [])
    parts = seq_gather(grads_own, qkv_parts[1:2])
    if aligned:
        final_up, final_gate, final_down, final_out, *final_vectors = local_call(
            functools.partial(ordered_kernel, functools.partial(unpack_kernel, fsdp, width), 4),
            [(w.shape, f32) for w in (w_up, w_gate, w_down, w_out)] + [((1, w_rows), f32)] * 4,
            [seq_places, *parts],
            2**20,
            "unpack",
            scratch=[pltpu.VMEM((groups,) + parts[0].shape, bf16)],
            spaces=[smem] + [vmem] * 4,
        )
        final_vectors = [v.reshape(w_rows) for v in final_vectors]
    else:
        parts = arrange(parts, seq_order).astype(f32)

        def columns(at):
            value = parts[:, :, at : at + width].reshape(groups, w_rows, fsdp, w_rows)
            return value.transpose(1, 2, 0, 3).reshape(w_rows, groups * width)

        final_up, final_gate = columns(0), columns(width)
        final_down = parts[:, :, 2 * width : 3 * width].reshape(groups * w_rows, width)
        final_out = parts[:, :, 3 * width : 3 * width + inner].transpose(1, 0, 2)
        final_out = final_out.reshape(w_rows, width)
        final_vectors = jnp.sum(parts[:, :, 3 * width + inner :], axis=0).T
    (final_qkv,) = local_call(
        functools.partial(ordered_kernel, unpack_qkv_kernel, 4),
        [(w_qkv.shape, f32)],
        [seq_places, *qkv_parts],
        2**20,
        "unpack_qkv",
        scratch=[pltpu.VMEM((groups, w_rows, 3 * inner), bf16)],
        spaces=[smem] + [vmem] * 4,
    )
    return (
        result,
        d_input,
        final_qkv,
        final_out,
        final_vectors[0],
        final_vectors[1],
        final_up,
        final_gate,
        final_down,
        final_vectors[2],
        final_vectors[3],
    )


def solution(mesh):
    rows = P(("fsdp", "seq"), None)
    param, vector = P("fsdp", None), P("fsdp")
    in_specs = (rows, rows, P(), param, param, vector, vector, param, param, param, vector, vector)
    out_specs = (rows, rows, param, param, vector, vector, param, param, param, vector, vector)
    return jax.shard_map(local, mesh=mesh, in_specs=in_specs, out_specs=out_specs, check_vma=False)
```

```python
import functools
import math

import jax
import jax.numpy as jnp
from jax import lax
from jax.experimental import pallas as pl
from jax.experimental.pallas import tpu as pltpu
from jax.sharding import PartitionSpec as P

HEADS = 12
HEAD_DIM = 64
SPAN = 8
EXT = 16
WIDE = HEAD_DIM + EXT
BIG = 2.0**30
SAFE_SUM = 2.0**100
VMEM = 24 * 2**20
SMALL = 16 * 2**20

bf16 = jnp.bfloat16
f32 = jnp.float32
norm_eps = 1e-12
base_log = math.log(1000.0)


def dot(left_op, right_op, left_dim, right_dim):
    return lax.dot_general(
        left_op, right_op, (((left_dim,), (right_dim,)), ((), ())), preferred_element_type=f32
    )


def ring_order(size):
    return list(range(0, size, 2)) + list(range(size - 1, 0, -2))


def ring_place(index, size):
    return jnp.where(index % 2 == 0, index // 2, size - 1 - index // 2)


def ring_index(place, size):
    place = place % size
    return jnp.where(place < size // 2, 2 * place, 2 * (size - 1 - place) + 1)


def ring_shift(value, step, size):
    order = ring_order(size)
    pairs = [
        (base + order[i], base + order[(i + step) % size])
        for base in range(0, lax.axis_size("fsdp"), size)
        for i in range(size)
    ]
    return lax.ppermute(value, "fsdp", pairs)


def seq_swap(value, mask):
    return lax.ppermute(value, "seq", [(i, i ^ mask) for i in range(lax.axis_size("seq"))])


def arrange_kernel(count, order, *refs):
    for i, ref in enumerate(refs[:count]):
        refs[-1][order[i]] = ref[...]


def arrange(blocks, order, after=()):
    return pl.pallas_call(
        functools.partial(arrange_kernel, len(blocks)),
        in_specs=[pl.BlockSpec(memory_space=pltpu.SMEM)]
        + [pl.BlockSpec(memory_space=pltpu.VMEM)] * len(blocks)
        + [pl.BlockSpec(memory_space=pl.ANY)] * len(after),
        out_specs=pl.BlockSpec(memory_space=pltpu.VMEM),
        out_shape=jax.ShapeDtypeStruct((len(blocks),) + blocks[0].shape, blocks[0].dtype),
        compiler_params=pltpu.CompilerParams(vmem_limit_bytes=SMALL),
        name="arrange",
    )(jnp.stack(order).astype(jnp.int32), *blocks, *after)


def arrange_runs_kernel(order, *refs):
    at = 0
    for ref in refs[:-1]:
        for k in range(ref.shape[0]):
            refs[-1][order[at]] = ref[k]
            at += 1


def arrange_runs(runs, order):
    return pl.pallas_call(
        arrange_runs_kernel,
        in_specs=[pl.BlockSpec(memory_space=pltpu.SMEM)]
        + [pl.BlockSpec(memory_space=pltpu.VMEM)] * len(runs),
        out_specs=pl.BlockSpec(memory_space=pltpu.VMEM),
        out_shape=jax.ShapeDtypeStruct((len(order),) + runs[0].shape[1:], runs[0].dtype),
        compiler_params=pltpu.CompilerParams(vmem_limit_bytes=VMEM),
        name="arrange_runs",
    )(jnp.stack(order).astype(jnp.int32), *runs)


def ring_gather(block, size, place):
    half = block.shape[0] // 2
    right, left = block, block
    blocks, order = [block], [ring_index(place, size)]
    for t in range(1, size // 2):
        right, left = ring_shift(right, 1, size), ring_shift(left, -1, size)
        blocks += [right, left]
        order += [ring_index(place - t, size), ring_index(place + t, size)]
    last = jnp.concatenate(
        [ring_shift(right[:half], 1, size), ring_shift(left[half:], -1, size)], axis=0
    )
    return blocks + [last], order + [ring_index(place + size // 2, size)]


def sum_kernel(counts, split, *refs):
    outs = refs[-len(counts) :]
    at = 0
    for which, (count, arrived) in enumerate(counts):
        blocks, got = refs[at : at + count], refs[at + count : at + count + arrived]
        at += count + arrived
        total = sum(ref[0].astype(f32) for ref in blocks)
        if split and arrived:
            half = total.shape[0] // 2
            cut = slice(0, half) if which == 0 else slice(half, 2 * half)
            other = slice(half, 2 * half) if which == 0 else slice(0, half)
            outs[which][cut, :] = (total[cut] + got[0][...].astype(f32)).astype(bf16)
            outs[which][other, :] = total[other].astype(bf16)
        else:
            total = total + sum(ref[...].astype(f32) for ref in got)
            outs[which][...] = total.astype(bf16)


def block_sums(directions, split, after):
    specs, ins = [], []
    for blocks, got in directions:
        for stacked, index in blocks:
            shape = (1,) + stacked.shape[1:]
            specs.append(pl.BlockSpec(shape, lambda _, index=index: (index, 0, 0)))
            ins.append(stacked)
        for value in got:
            specs.append(pl.BlockSpec(value.shape, lambda _: (0, 0)))
            ins.append(value)
    shape = directions[0][0][0][0].shape[1:]
    counts = [(len(blocks), len(got)) for blocks, got in directions]
    used = len(ins)

    def body(*refs):
        sum_kernel(counts, split, *refs[:used], *refs[used + len(after) :])

    return pl.pallas_call(
        body,
        grid=(1,),
        in_specs=specs + [pl.BlockSpec(memory_space=pl.ANY)] * len(after),
        out_specs=[pl.BlockSpec(shape, lambda _: (0, 0)) for _ in counts],
        out_shape=[jax.ShapeDtypeStruct(shape, bf16) for _ in counts],
        compiler_params=pltpu.CompilerParams(vmem_limit_bytes=SMALL),
        name="sums",
    )(*ins, *after)


def ring_scatter(blocks, size, after):
    after = {i: list(values) for i, values in enumerate(after)}
    (far,) = block_sums([(blocks(size // 2), [])], False, after.get(0, []))
    half = far.shape[0] // 2
    sent = [far]
    right = ring_shift(far[:half], 1, size)
    left = ring_shift(far[half:], -1, size)
    first = [right, left]
    for hop, t in enumerate(range(size // 2 - 1, 0, -1)):
        up, down = block_sums(
            [(blocks(t), [right]), (blocks(-t), [left])], hop == 0, after.get(hop + 1, [])
        )
        right, left = ring_shift(up, 1, size), ring_shift(down, -1, size)
        sent.append(up)
    (total,) = block_sums([(blocks(0), [right, left])], False, after.get(size // 2, []))
    return total, sent, first


def three_parts(value):
    high = value.astype(bf16).astype(f32)
    rest = value - high
    mid = rest.astype(bf16).astype(f32)
    return high, mid, rest - mid


def with_parts(base, value):
    high, mid, low = three_parts(value)
    lane = lax.broadcasted_iota(jnp.int32, base.shape, 1)
    filled = jnp.where(lane == HEAD_DIM, high, base)
    filled = jnp.where(lane == HEAD_DIM + 1, mid, filled)
    return jnp.where(lane == HEAD_DIM + 2, low, filled)


def first_kernel(heads, tile, where_ref, ext_ref, qt_ref, qe_ref, kv_ref, qx_ref, acc_ref):
    tokens = qt_ref.shape[1]
    ones = jnp.ones((EXT, tokens), bf16)
    ext = block_ext(ext_ref, where_ref, 0, tokens)
    for h in range(heads):
        rows = slice(h * HEAD_DIM, (h + 1) * HEAD_DIM)
        k_rows, v_rows = block_rows([kv_ref], h)
        keys = jnp.concatenate([k_rows, ext], axis=0)
        vals = jnp.concatenate([v_rows, ones], axis=0)
        for start in range(0, tokens, tile):
            cut = slice(start, start + tile)
            natural = qt_ref[rows, cut].astype(f32).T
            queries = jnp.concatenate([natural, qe_ref[cut, :].astype(f32)], axis=1)
            scores = dot(queries.astype(bf16), keys, 1, 0)
            top = jnp.max(scores, axis=1, keepdims=True)
            weights = jnp.exp(scores - top).astype(bf16)
            acc_ref[h, :, cut] = dot(vals, weights, 1, 1)
            qx_ref[h, cut, :] = with_parts(queries, top).astype(bf16)


def block_rows(refs, h):
    if len(refs) == 2:
        rows = slice(h * HEAD_DIM, (h + 1) * HEAD_DIM)
        return refs[0][rows, :], refs[1][rows, :]
    inner = refs[0].shape[0] // 2
    return (
        refs[0][h * HEAD_DIM : (h + 1) * HEAD_DIM, :],
        refs[0][inner + h * HEAD_DIM : inner + (h + 1) * HEAD_DIM, :],
    )


def block_ext(ext_ref, where_ref, index, tokens):
    return ext_ref[:, pl.ds(pl.multiple_of(where_ref[index] * tokens, tokens), tokens)]


def step_kernel(heads, tile, parts, where_ref, ext_ref, qx_ref, acc_in, *refs):
    acc_ref, tokens = refs[-1], qx_ref.shape[1]
    ones = jnp.ones((EXT, tokens), bf16)
    blocks, at = [], 0
    for b, part in enumerate(parts):
        blocks.append((refs[at : at + part], block_ext(ext_ref, where_ref, b, tokens)))
        at += part
    for h in range(heads):
        pairs = []
        for block, ext in blocks:
            k_rows, v_rows = block_rows(block, h)
            pairs.append(
                (jnp.concatenate([k_rows, ext], axis=0), jnp.concatenate([v_rows, ones], axis=0))
            )
        for start in range(0, tokens, tile):
            cut = slice(start, start + tile)
            total = acc_in[h, :, cut]
            for keys, vals in pairs:
                weights = jnp.exp(dot(qx_ref[h, cut, :], keys, 1, 0)).astype(bf16)
                total = total + dot(vals, weights, 1, 1)
            acc_ref[h, :, cut] = total


def finish_kernel(heads, tile, parts, where_ref, ext_ref, qx_ref, acc_ref, *refs):
    count = sum(parts)
    blocks = refs[:count]
    ot_ref, on_ref, qx2_ref, buf, acc, qx = refs[count:]
    tokens = qx_ref.shape[1]
    inner = buf.shape[1] // 2
    fine = True
    for h in range(heads):
        sums = acc_ref[h, HEAD_DIM : HEAD_DIM + 8, :]
        fine = jnp.logical_and(fine, jnp.logical_and(sums <= SAFE_SUM, sums >= 0.5))
    good = jnp.min(jnp.where(fine, 1.0, 0.0)) > 0.5
    acc[...] = acc_ref[...]
    qx[...] = qx_ref[...]

    @pl.when(jnp.logical_not(good))
    def _():
        small = tile // 2
        ones = jnp.ones((EXT, tokens), bf16)
        lane = lax.broadcasted_iota(jnp.int32, (small, WIDE), 1)
        inside = jnp.logical_and(lane >= HEAD_DIM, lane < HEAD_DIM + 3)
        at = 0
        for b, part in enumerate(parts):
            if part == 2:
                pltpu.sync_copy(blocks[at], buf.at[b, pl.ds(0, inner)])
                pltpu.sync_copy(blocks[at + 1], buf.at[b, pl.ds(inner, inner)])
            else:
                pltpu.sync_copy(blocks[at], buf.at[b])
            at += part

        def each(body):
            cuts = tokens // small

            def turn(step, carry):
                b, rest = step // (heads * cuts), step % (heads * cuts)
                h = rest // cuts
                cut = pl.ds(pl.multiple_of(rest % cuts * small, small), small)
                rows = pl.multiple_of(h * HEAD_DIM, HEAD_DIM)
                ext = block_ext(ext_ref, where_ref, b, tokens)
                keys = jnp.concatenate([buf[b, pl.ds(rows, HEAD_DIM), :], ext], axis=0)
                vals = buf[b, pl.ds(pl.multiple_of(inner + rows, HEAD_DIM), HEAD_DIM), :]
                body(h, cut, keys, jnp.concatenate([vals, ones], axis=0))
                return carry

            lax.fori_loop(0, len(parts) * heads * cuts, turn, 0)

        def raise_top(h, cut, keys, vals):
            base = qx[h, cut, :].astype(f32)
            old = jnp.sum(jnp.where(inside, base, 0.0), axis=1, keepdims=True)
            plain = jnp.where(inside, 0.0, base)
            scores = dot(plain.astype(bf16), keys, 1, 0)
            top = jnp.maximum(old, jnp.max(scores, axis=1, keepdims=True))
            qx[h, cut, :] = with_parts(plain, top).astype(bf16)

        def add_up(h, cut, keys, vals):
            weights = jnp.exp(dot(qx[h, cut, :], keys, 1, 0)).astype(bf16)
            acc[h, :, cut] += dot(vals, weights, 1, 1)

        each(raise_top)
        acc[...] = jnp.zeros_like(acc)
        each(add_up)

    lane = lax.broadcasted_iota(jnp.int32, (tile, WIDE), 1)
    inside = jnp.logical_and(lane >= HEAD_DIM, lane < HEAD_DIM + 3)
    for h in range(heads):
        rows = slice(h * HEAD_DIM, (h + 1) * HEAD_DIM)
        for start in range(0, tokens, tile):
            cut = slice(start, start + tile)
            block = acc[h, :, cut]
            normed = block[:HEAD_DIM, :] * (1.0 / block[HEAD_DIM : HEAD_DIM + 1, :])
            ot_ref[rows, cut] = normed.astype(bf16)
            stacked = jnp.concatenate([normed, jnp.log(block[HEAD_DIM:, :])], axis=0).T
            on_ref[h, cut, :] = stacked[:, :HEAD_DIM]
            base = qx[h, cut, :].astype(f32)
            top = jnp.sum(jnp.where(inside, base, 0.0), axis=1, keepdims=True)
            shift = top + stacked[:, HEAD_DIM : HEAD_DIM + 1]
            qx2_ref[h, cut, :] = with_parts(base, shift).astype(bf16)


def delta_kernel(heads, where, own_ref, got_ref, on_ref, dox_ref, dot_ref):
    tokens = own_ref.shape[1]
    for tile in range(2):
        cut = slice(tile * tokens, (tile + 1) * tokens)

        @pl.when(where[0] == tile)
        def _():
            dot_ref[:, cut] = own_ref[...]

        @pl.when(where[0] != tile)
        def _():
            dot_ref[:, cut] = got_ref[...]

        for h in range(heads):
            rows = slice(h * HEAD_DIM, (h + 1) * HEAD_DIM)
            natural = dot_ref[rows, cut].astype(f32).T
            delta = jnp.sum(natural * on_ref[h, cut, :], axis=1, keepdims=True)
            base = jnp.concatenate([natural, jnp.zeros((tokens, EXT), f32)], axis=1)
            dox_ref[h, cut, :] = with_parts(base, delta).astype(bf16)


def back_kernel(heads, q_tile, where_ref, ext_ref, qx_ref, dox_ref, qt_ref, dot_ref, dq_in, *refs):
    block, (dq_ref, dkv_ref) = refs[:-2], refs[-2:]
    tokens, inner = qt_ref.shape[1], qt_ref.shape[0]
    ext = block_ext(ext_ref, where_ref, 0, tokens)
    for h in range(heads):
        rows = slice(h * HEAD_DIM, (h + 1) * HEAD_DIM)
        k_rows, v_rows = block_rows(block, h)
        keys = jnp.concatenate([k_rows, ext], axis=0)
        vals = jnp.concatenate([v_rows, ext], axis=0)
        d_key, d_value = 0.0, 0.0
        for start in range(0, tokens, q_tile):
            cut = slice(start, start + q_tile)
            weights = jnp.exp(dot(qx_ref[h, cut, :], keys, 1, 0))
            shifted = dot(dox_ref[h, cut, :], vals, 1, 0)
            d_scores = (weights * shifted).astype(bf16)
            d_value = d_value + dot(dot_ref[rows, cut], weights.astype(bf16), 1, 0)
            d_key = d_key + dot(qt_ref[rows, cut], d_scores, 1, 0)
            dq_ref[rows, cut] = dq_in[rows, cut] + dot(k_rows, d_scores, 1, 1)
        dkv_ref[rows, :] = d_key.astype(bf16)
        dkv_ref[inner + h * HEAD_DIM : inner + (h + 1) * HEAD_DIM, :] = d_value.astype(bf16)


def pack_kernel(parts, s_ref, up_ref, gate_ref, down_ref, last_ref, *refs):
    vectors, out_ref = refs[:4], refs[4]
    s = s_ref[0]
    rows = up_ref.shape[0]
    width = parts * rows
    for i, ref in enumerate((up_ref, gate_ref)):
        pieces = []
        for k in range(parts):
            run = ref[:, 4 * rows * k : 4 * rows * (k + 1)]
            pieces.append(pltpu.roll(run, (4 * rows - s * rows) % (4 * rows), 1)[:, :rows])
        out_ref[:, i * width : (i + 1) * width] = jnp.concatenate(pieces, axis=1).astype(bf16)
    own = down_ref[pl.ds(pl.multiple_of(s * rows, 8), rows), :]
    out_ref[:, 2 * width : 3 * width] = own.astype(bf16)
    inner = width // 4
    columns = pltpu.roll(last_ref[...], (width - s * inner) % width, 1)[:, :inner]
    spare = out_ref.shape[1] - 3 * width - inner
    side = jnp.concatenate([ref[...] for ref in vectors] + [jnp.zeros((4, rows), f32)], axis=0).T
    out_ref[:, 3 * width :] = jnp.concatenate(
        [columns, side, jnp.zeros((rows, spare - 8), f32)], axis=1
    ).astype(bf16)


def unpack_kernel(parts, width, *refs):
    quarters, (up_ref, gate_ref, down_ref, out_ref), vectors = refs[:4], refs[4:8], refs[8:]
    rows = up_ref.shape[0]
    inner = width // 4
    for i, ref in enumerate((up_ref, gate_ref)):
        for k in range(parts):
            at = i * width + k * rows
            ref[:, 4 * rows * k : 4 * rows * (k + 1)] = jnp.concatenate(
                [q[:, at : at + rows].astype(f32) for q in quarters], axis=1
            )
    for g, q in enumerate(quarters):
        down_ref[g * rows : (g + 1) * rows, :] = q[:, 2 * width : 3 * width].astype(f32)
    at = 3 * width
    out_ref[...] = jnp.concatenate([q[:, at : at + inner].astype(f32) for q in quarters], axis=1)
    sums = sum(q[:, at + inner :].astype(f32) for q in quarters).T
    for i, ref in enumerate(vectors):
        ref[...] = sums[i : i + 1, :]


def ordered_kernel(kernel, count, order, *refs):
    buffer = refs[-1]
    for i in range(count):
        buffer[order[i]] = refs[i][...]
    kernel(*[buffer.at[i] for i in range(count)], *refs[count:-1])


def unpack_all_kernel(parts, width, order, *refs):
    ordered_kernel(unpack_qkv_kernel, 4, order, *refs[4:8], refs[8], refs[-1])
    ordered_kernel(functools.partial(unpack_kernel, parts, width), 4, order, *refs[:4], *refs[9:-1])


def grads_kernel(order, hidden_ref, branch_ref, heads_ref, first_sums, second_sums, *refs):
    sides, mine_ref, runs, buffer = (refs[:4], refs[4:8]), refs[8], refs[9:-1], refs[-1]
    count, rows = mine_ref.shape[0], mine_ref.shape[1]
    width = hidden_ref.shape[1]
    hidden_t = hidden_ref[...].T
    heads = heads_ref[...].reshape(width, heads_ref.shape[2])
    vectors = (first_sums[...] + second_sums[...]).T
    vectors = jnp.concatenate(
        [vectors, jnp.zeros((width, mine_ref.shape[2] - 3 * width - width // 4 - 8), f32)], axis=1
    ).astype(bf16)
    for which, (up_ref, gate_ref, inner_ref, cols_ref) in enumerate(sides):

        def put(value, at):
            for k in range(count):
                buffer[k, :, at : at + value.shape[1]] = value[k * rows : (k + 1) * rows]

        put(dot(hidden_t, up_ref[...], 1, 0).astype(bf16), 0)
        put(dot(hidden_t, gate_ref[...], 1, 0).astype(bf16), width)
        put(dot(inner_ref[...].T, branch_ref[...], 1, 0).astype(bf16), 2 * width)
        tail = dot(heads, cols_ref[...], 1, 0).astype(bf16)
        rest = vectors if which == 0 else jnp.zeros_like(vectors)
        put(jnp.concatenate([tail, rest], axis=1), 3 * width)
        if which == 0:
            for i in range(count):
                mine_ref[i] = buffer[order[i]]
        else:
            at = 0
            for run in runs:
                for k in range(run.shape[0]):
                    run[k] = buffer[order[at]]
                    at += 1


def tail_kernel(
    order, where, dq_ref, dkv_ref, right_ref, left_ref, cos_ref, sin_ref, x_ref, w_ref, *refs
):
    grad_ref, sent_ref, kept_ref, raw, buffer = refs
    inner = dq_ref.shape[0]
    cosine, sine = cos_ref[...], sin_ref[...]
    d_kv = dkv_ref[...].astype(f32) + right_ref[...].astype(f32) + left_ref[...].astype(f32)

    def put(base):
        def at_base(at, value):
            raw[base + at : base + at + value.shape[0], :] = value.astype(bf16)

        return at_base

    turn_rows(dq_ref[...] * HEAD_DIM**-0.5, cosine, -sine, put(0))
    turn_rows(d_kv[:inner], cosine, -sine, put(inner))
    raw[2 * inner :, :] = d_kv[inner:].astype(bf16)
    projected = raw[...].T
    count, rows = grad_ref.shape[0], grad_ref.shape[1]
    width, quarter = x_ref.shape[2], x_ref.shape[1]
    terms = dot(projected, w_ref[...].reshape(width, 3 * inner), 1, 1)
    for core in range(2):
        side = [terms[(2 * y + core) * quarter : (2 * y + core + 1) * quarter] for y in range(2)]

        @pl.when(where[1] == core)
        def _():
            for y in range(2):
                kept_ref[y] = side[y]

        @pl.when(where[1] != core)
        def _():
            for y in range(2):
                sent_ref[y] = side[y].astype(bf16)

    grad = dot(x_ref[...].reshape(4 * quarter, width).T, projected, 1, 0).astype(bf16)
    for k in range(count):
        buffer[k] = grad[k * rows : (k + 1) * rows]
    for i in range(count):
        grad_ref[i] = buffer[order[i]]


def unpack_qkv_kernel(*refs):
    quarters, out_ref = refs[:4], refs[4]
    inner = quarters[0].shape[1] // 3
    out_ref[...] = jnp.concatenate(
        [q[:, i * inner : (i + 1) * inner].astype(f32) for i in range(3) for q in quarters], axis=1
    )


def tables_kernel(at_ref, docs_ref, key_ref, query_ref):
    length, tokens = key_ref.shape[1], query_ref.shape[0]

    def kinds(start, count):
        docs = docs_ref[:, pl.ds(pl.multiple_of(start, count), count)] - at_ref[1]
        docs = jnp.broadcast_to(docs, (EXT, count))
        row = lax.broadcasted_iota(jnp.int32, (EXT, count), 0)
        return row, docs == row - 3

    row, same = kinds(at_ref[0], length)
    mark = jnp.where(jnp.logical_or(row < 3, jnp.logical_not(same)), -1.0, 0.0)
    key_ref[...] = jnp.where(row < 6, mark, 0.0).astype(bf16)
    row, same = kinds(at_ref[2], tokens)
    inside = jnp.logical_and(same, jnp.logical_and(row >= 3, row < 6))
    query_ref[...] = jnp.where(inside, BIG, 0.0).T.astype(bf16)


def turn_rows(value, cosine, sine, put):
    half = HEAD_DIM // 2
    for at in range(0, value.shape[0], HEAD_DIM):
        lead, last = value[at : at + half], value[at + half : at + HEAD_DIM]
        put(at, lead * cosine - last * sine)
        put(at + half, last * cosine + lead * sine)


def project_kernel(count, order, places, cos_ref, sin_ref, *refs):
    weights, tokens = refs[:count], refs[count : count + 4]
    q_ref, kv_ref, x_ref, w_ref = refs[count + 4 :]
    inner = q_ref.shape[0]
    for i, ref in enumerate(weights):
        w_ref[order[i]] = ref[...]
    for i, ref in enumerate(tokens):
        x_ref[places[i]] = ref[...]
    cosine, sine = cos_ref[...], sin_ref[...]
    width = x_ref.shape[2]
    matrix = w_ref[...].reshape(width, 3 * inner).T
    rows = x_ref[...].reshape(-1, width)

    def put_q(at, value):
        q_ref[at : at + value.shape[0], :] = value.astype(bf16) * bf16(HEAD_DIM**-0.5)

    def put_k(at, value):
        kv_ref[at : at + value.shape[0], :] = value.astype(bf16)

    turn_rows(dot(matrix[:inner], rows, 1, 1), cosine, sine, put_q)
    turn_rows(dot(matrix[inner : 2 * inner], rows, 1, 1), cosine, sine, put_k)
    kv_ref[inner:, :] = dot(matrix[2 * inner :], rows, 1, 1).astype(bf16)


def outer_kernel(places, *refs):
    parts, (out_ref, vec_ref, buffer) = refs[:4], refs[4:]
    inner = out_ref.shape[1] // 4
    for i, ref in enumerate(parts):
        buffer[places[i]] = ref[...]
    out_ref[...] = jnp.concatenate([buffer[g, :, :inner] for g in range(4)], axis=1)
    vec_ref[...] = parts[0][:, inner:].astype(f32).T[:8]


def gate(value, after):
    return pl.pallas_call(
        lambda *refs: None,
        in_specs=[pl.BlockSpec(memory_space=pl.ANY)] * (1 + len(after)),
        out_specs=pl.BlockSpec(memory_space=pl.ANY),
        out_shape=jax.ShapeDtypeStruct(value.shape, value.dtype),
        input_output_aliases={0: 0},
        name="gate",
    )(value, *after)


def norm_parts(rows_in):
    centre = rows_in - jnp.mean(rows_in, axis=-1, keepdims=True)
    rstd = lax.rsqrt(jnp.mean(centre * centre, axis=-1, keepdims=True) + norm_eps)
    return centre * rstd, rstd


def norm_grad(normed, rstd, grad, gain):
    scaled = grad * gain
    mean = jnp.mean(scaled, axis=-1, keepdims=True)
    return rstd * (scaled - mean - normed * jnp.mean(scaled * normed, axis=-1, keepdims=True))


def ff_weights(ref):
    width = ref.shape[0]
    return ref[:, :width], ref[:, width : 2 * width], ref[:, 2 * width : 3 * width]


def forward_kernel(places, where, *refs):
    parts, (x_ref, out_ref, vec_ref, mine_ref, other_ref) = refs[:4], refs[4:9]
    heads_ref, hidden_ref, kept_ref, sent_ref, normed_ref, rstd_ref = refs[9:15]
    acts = (refs[15:18], refs[18:21])
    width, rows = hidden_ref.shape[1], kept_ref.shape[0]
    side, core = where[0], where[1]
    for i, ref in enumerate(parts):
        heads_ref[places[i]] = ref[...]
    for tile in range(2):
        cut = slice(tile * rows, (tile + 1) * rows)
        start = pl.multiple_of((2 * side + tile) * rows, rows)
        heads = heads_ref[:, :, cut].reshape(width, rows).T
        first = x_ref[pl.ds(start, rows), :].astype(f32) + dot(heads, out_ref[...], 1, 0)
        normed, rstd = norm_parts(first)
        hidden = normed * vec_ref[0:1] + vec_ref[1:2]
        low = hidden.astype(bf16)
        hidden_ref[cut, :] = low
        branch = 0.0
        for w_ref, (up_ref, gate_ref, inner_ref) in zip((mine_ref, other_ref), acts):
            up_w, gate_w, down_w = ff_weights(w_ref)
            up, gate = dot(low, up_w, 1, 0), dot(low, gate_w, 1, 0)
            inner = (gate * lax.logistic(gate) * up).astype(bf16)
            up_ref[cut, :], gate_ref[cut, :], inner_ref[cut, :] = up, gate, inner
            branch = branch + dot(inner, down_w, 1, 0)

        @pl.when(core == tile)
        def _():
            kept_ref[...] = hidden + branch
            normed_ref[...] = normed
            rstd_ref[...] = jnp.broadcast_to(rstd, rstd_ref.shape)

        @pl.when(core != tile)
        def _():
            sent_ref[...] = branch.astype(bf16)


def second_kernel(kept_ref, got_ref, grad_ref, vec_ref, result_ref, d_ref, low_ref, sums_ref):
    normed, rstd = norm_parts(kept_ref[...] + got_ref[...].astype(f32))
    gain = vec_ref[2:3]
    result_ref[...] = (normed * gain + vec_ref[3:4]).astype(bf16)
    grad = grad_ref[...].astype(f32)
    d_second = norm_grad(normed, rstd, grad, gain)
    d_ref[...] = d_second
    low_ref[...] = d_second.astype(bf16)
    sums_ref[...] = jnp.zeros_like(sums_ref)
    sums_ref[2:3] = jnp.sum(grad * normed, axis=0, keepdims=True)
    sums_ref[3:4] = jnp.sum(grad, axis=0, keepdims=True)


def backward_kernel(where, own_ref, got_ref, mine_ref, other_ref, *refs):
    acts = (refs[:2], refs[2:4])
    branch_ref, kept_ref, sent_ref = refs[4:7]
    outs = (refs[7:9], refs[9:11])
    rows, core = kept_ref.shape[0], where[1]
    branch_ref[pl.ds(pl.multiple_of(core * rows, rows), rows), :] = own_ref[...]
    branch_ref[pl.ds(pl.multiple_of((1 - core) * rows, rows), rows), :] = got_ref[...]
    for tile in range(2):
        cut = slice(tile * rows, (tile + 1) * rows)
        branch = branch_ref[cut, :]
        total = 0.0
        for w_ref, (up_ref, gate_ref), (d_up_ref, d_gate_ref) in zip(
            (mine_ref, other_ref), acts, outs
        ):
            up_w, gate_w, down_w = ff_weights(w_ref)
            d_inner = dot(branch, down_w, 1, 1)
            up, gate = up_ref[cut, :], gate_ref[cut, :]
            sig = lax.logistic(gate)
            d_gate = (d_inner * up * sig * (1.0 + gate * (1.0 - sig))).astype(bf16)
            d_up = (d_inner * gate * sig).astype(bf16)
            d_up_ref[cut, :], d_gate_ref[cut, :] = d_up, d_gate
            total = total + dot(d_up, up_w, 1, 1) + dot(d_gate, gate_w, 1, 1)

        @pl.when(core == tile)
        def _():
            kept_ref[...] = total

        @pl.when(core != tile)
        def _():
            sent_ref[...] = total.astype(bf16)


def first_back_kernel(
    kept_ref, got_ref, d_second_ref, normed_ref, rstd_ref, vec_ref, d_ref, low_ref, sums_ref
):
    d_hidden = d_second_ref[...] + kept_ref[...] + got_ref[...].astype(f32)
    normed = normed_ref[...]
    d_first = norm_grad(normed, rstd_ref[:, 0:1], d_hidden, vec_ref[0:1])
    d_ref[...] = d_first
    low_ref[...] = d_first.astype(bf16)
    sums_ref[...] = jnp.zeros_like(sums_ref)
    sums_ref[0:1] = jnp.sum(d_hidden * normed, axis=0, keepdims=True)
    sums_ref[1:2] = jnp.sum(d_hidden, axis=0, keepdims=True)


def heads_back_kernel(
    where, own_ref, got_ref, out_ref, own_heads_ref, sent_ref, own_cols_ref, other_cols_ref, branch
):
    side, core = where[0], where[1]
    rows, inner = own_ref.shape[0], sent_ref.shape[0]
    branch[pl.ds(pl.multiple_of(core * rows, rows), rows), :] = own_ref[...]
    branch[pl.ds(pl.multiple_of((1 - core) * rows, rows), rows), :] = got_ref[...]
    for which, ref in ((1 - side, sent_ref), (side, own_heads_ref)):
        at = pl.multiple_of((2 * which + core) * inner, inner)
        ref[...] = dot(out_ref[pl.ds(at, inner), :], branch[...], 1, 1).astype(bf16)
    for group in range(4):
        value = branch[:, group * inner : (group + 1) * inner]

        @pl.when(2 * side + core == group)
        def _():
            own_cols_ref[...] = value

        @pl.when(2 * (1 - side) + core == group)
        def _():
            other_cols_ref[...] = value


def input_mid_kernel(where, kept_ref, got_ref, kept_out, sent_out):
    for y in range(2):
        value = kept_ref[y] + got_ref[y].astype(f32)

        @pl.when(where[0] == y)
        def _():
            kept_out[...] = value

        @pl.when(where[0] != y)
        def _():
            sent_out[...] = value.astype(bf16)


def input_end_kernel(first_ref, kept_ref, got_ref, out_ref):
    out_ref[...] = (first_ref[...] + kept_ref[...] + got_ref[...].astype(f32)).astype(bf16)


def piped_call(kernel, outs, ins, name, after=()):
    count = len(ins)

    def body(*refs):
        kernel(*refs[:count], *refs[count + len(after) :])

    def whole(shape):
        return pl.BlockSpec(shape, lambda _: (0,) * len(shape))

    return pl.pallas_call(
        body,
        grid=(1,),
        in_specs=[pl.BlockSpec(memory_space=pltpu.SMEM)]
        + [whole(value.shape) for value in ins[1:]]
        + [pl.BlockSpec(memory_space=pl.ANY)] * len(after),
        out_specs=[whole(shape) for shape, _ in outs],
        out_shape=[jax.ShapeDtypeStruct(shape, dtype) for shape, dtype in outs],
        compiler_params=pltpu.CompilerParams(vmem_limit_bytes=SMALL),
        name=name,
    )(*ins, *after)


def local_call(kernel, outs, ins, flops, name, scratch=(), spaces=None, after=()):
    limit = SMALL if name.startswith("attend") or name in ("outer", "tables", "project") else VMEM
    spaces = list(spaces or [pltpu.VMEM] * len(ins))
    count = len(ins)

    def body(*refs):
        kernel(*refs[:count], *refs[count + len(after) :])

    return pl.pallas_call(
        body,
        in_specs=[pl.BlockSpec(memory_space=space) for space in spaces + [pl.ANY] * len(after)],
        out_specs=[pl.BlockSpec(memory_space=pltpu.VMEM) for _ in outs],
        out_shape=[jax.ShapeDtypeStruct(shape, dtype) for shape, dtype in outs],
        scratch_shapes=list(scratch),
        compiler_params=pltpu.CompilerParams(vmem_limit_bytes=limit),
        cost_estimate=pl.CostEstimate(flops=flops * 5, bytes_accessed=2**20, transcendentals=0),
        name=name,
    )(*ins, *after)


def local(
    layer_input,
    out_grad,
    doc_ids,
    w_qkv,
    w_out,
    norm1_gain,
    norm1_bias,
    w_up,
    w_gate,
    w_down,
    norm2_gain,
    norm2_bias,
):
    fsdp = lax.axis_size("fsdp")
    groups = lax.axis_size("seq")
    f = lax.axis_index("fsdp")
    s = lax.axis_index("seq")
    side, core = s // 2, s % 2
    tok_rows, width = layer_input.shape
    w_rows = w_qkv.shape[0]
    inner = width // groups
    heads = inner // HEAD_DIM
    group_rows = tok_rows * groups
    half_rows = group_rows // 2
    length = SPAN * group_rows
    place = ring_place(f, fsdp)
    spot = ring_place(f % SPAN, SPAN)
    base = f // SPAN * SPAN

    seq_order = [s, s ^ 2, s ^ 1, s ^ 3]
    seq_places = jnp.stack(seq_order).astype(jnp.int32)
    where = jnp.stack([side, core]).astype(jnp.int32)
    smem, vmem = pltpu.SMEM, pltpu.VMEM
    aligned = w_rows * groups % 128 == 0 and w_rows % 16 == 0

    def quarter(matrix, start):
        return lax.dynamic_slice_in_dim(matrix, start + s * inner, inner, 1)

    qkv_own = jnp.concatenate([quarter(w_qkv, i * width) for i in range(3)], axis=1).astype(bf16)
    x_side = seq_swap(layer_input, 2)
    x_core = seq_swap(layer_input, 1)
    x_far = seq_swap(layer_input, 3)
    qkv_blocks, order = ring_gather(qkv_own, fsdp, place)
    early, qkv_second = qkv_blocks[-3:-1], qkv_blocks[3:5]
    ring_order_now = jnp.stack(order).astype(jnp.int32)
    if not aligned:
        qkv_blocks = [arrange(qkv_blocks, order).reshape(width, 3 * inner)]
        ring_order_now = jnp.zeros((1,), jnp.int32)
    key_ext, query_ext = local_call(
        tables_kernel,
        [((EXT, length), bf16), ((group_rows, EXT), bf16)],
        [
            jnp.stack([f // SPAN * length, f // SPAN * 3, f * group_rows]).astype(jnp.int32),
            doc_ids[None, :],
        ],
        2**20,
        "tables",
        spaces=[smem, vmem],
        after=[*early, x_core, x_far],
    )
    positions = f % SPAN * group_rows + jnp.arange(group_rows, dtype=jnp.int32)
    steps = jnp.arange(HEAD_DIM // 2, dtype=f32)
    freqs = jnp.exp(steps * (-2.0 * base_log / HEAD_DIM))
    angles = freqs[:, None] * positions.astype(f32)[None, :]
    cosine, sine = jnp.cos(angles), jnp.sin(angles)

    queries, own_kv, x_all, qkv_full = local_call(
        functools.partial(project_kernel, len(qkv_blocks)),
        [
            ((inner, group_rows), bf16),
            ((2 * inner, group_rows), bf16),
            ((groups, tok_rows, width), bf16),
            ((len(qkv_blocks),) + qkv_blocks[0].shape, bf16),
        ],
        [
            ring_order_now,
            seq_places,
            cosine,
            sine,
            *qkv_blocks,
            layer_input,
            x_side,
            x_core,
            x_far,
        ],
        2**32,
        "project",
        spaces=[smem, smem] + [vmem] * (len(qkv_blocks) + 6),
    )

    def ff_quarter(matrix):
        split = matrix.reshape(w_rows, fsdp, groups, w_rows)
        return lax.dynamic_index_in_dim(split, s, 2, False).reshape(w_rows, width)

    spare = 256 - inner % 256
    packed_width = 3 * width + inner + spare
    if aligned:
        (own,) = piped_call(
            functools.partial(pack_kernel, fsdp),
            [((w_rows, packed_width), bf16)],
            [
                s.reshape(1),
                w_up,
                w_gate,
                w_down,
                w_out,
                *[v[None, :] for v in (norm1_gain, norm1_bias, norm2_gain, norm2_bias)],
            ],
            "pack",
            after=[*qkv_second, x_core, x_far],
        )
    else:
        down_rows = lax.dynamic_slice_in_dim(w_down, s * w_rows, w_rows, 0)
        gains = jnp.stack([norm1_gain, norm1_bias, norm2_gain, norm2_bias], axis=1)
        own = jnp.concatenate(
            [
                ff_quarter(w_up),
                ff_quarter(w_gate),
                down_rows,
                quarter(w_out, 0),
                gains,
                jnp.zeros((w_rows, spare - 4), f32),
            ],
            axis=1,
        ).astype(bf16)
    mine, order = ring_gather(own, fsdp, place)
    steady = [jnp.int32(i) for i in range(fsdp)]
    others = [seq_swap(own, 2)[None]]
    for start in range(1, fsdp, 2):
        run = mine[start : start + 2]
        others.append(seq_swap(arrange(run, steady[: len(run)], others[-1:]), 2))
    others = arrange_runs(others, order).reshape(width, own.shape[1])
    mine = arrange(mine, order).reshape(width, own.shape[1])
    out_own, out_side = mine[:, 3 * width :], others[:, 3 * width :]
    out_core, out_far = seq_swap(out_own, 1), seq_swap(out_side, 1)
    out_full, vectors = local_call(
        outer_kernel,
        [((width, width), bf16), ((8, width), f32)],
        [seq_places, out_own, out_side, out_core, out_far],
        2**20,
        "outer",
        scratch=[pltpu.VMEM((groups,) + out_own.shape, bf16)],
        spaces=[smem] + [vmem] * 4,
    )

    def spots(*offsets):
        return jnp.stack([ring_index(spot + o, SPAN) for o in offsets]).astype(jnp.int32)

    block_flops = 8 * 256 * heads * group_rows * group_rows
    acc_out = ((heads, WIDE, group_rows), f32)
    wide_out = ((heads, group_rows, WIDE), bf16)
    tile = min(512, group_rows)
    qx, acc = local_call(
        functools.partial(first_kernel, heads, tile),
        [wide_out, acc_out],
        [spots(0), key_ext, queries, query_ext, own_kv],
        block_flops,
        "attend_own",
        spaces=[smem] + [vmem] * 4,
    )
    far = SPAN // 2
    blocks = {0: (own_kv,)}
    right, left = own_kv, own_kv
    for t in range(1, far + 1):
        if t < far:
            right, left = ring_shift(right, 1, SPAN), ring_shift(left, -1, SPAN)
            blocks[-t], blocks[t] = (right,), (left,)
            now = [-t, t]
        else:
            blocks[t] = (ring_shift(right[:inner], 1, SPAN), ring_shift(left[inner:], -1, SPAN))
            now = [t]
        refs = [ref for o in now for ref in blocks[o]]
        (acc,) = local_call(
            functools.partial(step_kernel, heads, tile, [len(blocks[o]) for o in now]),
            [acc_out],
            [spots(*now), key_ext, qx, acc, *refs],
            block_flops * len(now),
            "attend_step",
            spaces=[smem] + [vmem] * (3 + len(refs)),
            after=[mine] if t == far - 1 else [],
        )
    offsets = sorted(blocks)
    refs = [ref for o in offsets for ref in blocks[o]]
    heads_t, heads_n, qx = local_call(
        functools.partial(
            finish_kernel, heads, min(512, group_rows), [len(blocks[o]) for o in offsets]
        ),
        [((inner, group_rows), bf16), ((heads, group_rows, HEAD_DIM), f32), wide_out],
        [spots(*offsets), key_ext, qx, acc, *refs],
        block_flops // 4,
        "attend_finish",
        scratch=[
            pltpu.VMEM((SPAN, 2 * inner, group_rows), bf16),
            pltpu.VMEM(*acc_out),
            pltpu.VMEM(*wide_out),
        ],
        spaces=[smem] + [vmem] * 3 + [pl.ANY] * len(refs),
        after=[out_full],
    )

    def my_half(value, axis):
        return lax.dynamic_slice_in_dim(value, side * half_rows, half_rows, axis)

    def other_half(value, axis):
        return lax.dynamic_slice_in_dim(value, (1 - side) * half_rows, half_rows, axis)

    heads_own = my_half(heads_t, 1)
    heads_side = seq_swap(other_half(heads_t, 1), 2)
    heads_core = seq_swap(heads_own, 1)
    heads_far = seq_swap(heads_side, 1)
    half_low = ((half_rows, width), bf16)
    half_acts = [((half_rows, width), f32)] * 2 + [half_low]
    own_low, own_full = ((tok_rows, width), bf16), ((tok_rows, width), f32)
    sums_out = ((8, width), f32)
    heads_all, hidden_low, kept, sent, normed_one, rstd_one, *acts = local_call(
        forward_kernel,
        [
            ((groups, inner, half_rows), bf16),
            half_low,
            own_full,
            own_low,
            own_full,
            ((tok_rows, 128), f32),
            *half_acts,
            *half_acts,
        ],
        [
            seq_places,
            where,
            heads_own,
            heads_side,
            heads_core,
            heads_far,
            x_all.reshape(group_rows, width),
            out_full,
            vectors,
            mine,
            others,
        ],
        2**33,
        "feed_forward",
        spaces=[smem, smem] + [vmem] * 9,
    )
    result, d_second, d_branch_two, sums_two = local_call(
        second_kernel,
        [own_low, own_full, own_low, sums_out],
        [kept, seq_swap(sent, 1), out_grad, vectors],
        2**20,
        "second_norm",
    )
    d_branch_two, kept, sent, d_up, d_gate, d_up_other, d_gate_other = local_call(
        backward_kernel,
        [half_low, own_full, own_low] + [half_low] * 4,
        [
            where,
            d_branch_two,
            seq_swap(d_branch_two, 1),
            mine,
            others,
            acts[0],
            acts[1],
            acts[3],
            acts[4],
        ],
        2**33,
        "feed_back",
        spaces=[smem] + [vmem] * 8,
    )
    d_first, d_branch_one, sums_one = local_call(
        first_back_kernel,
        [own_full, own_low, sums_out],
        [kept, seq_swap(sent, 1), d_second, normed_one, rstd_one, vectors],
        2**20,
        "first_norm_back",
    )

    part = ((inner, half_rows), bf16)
    columns = ((half_rows, inner), bf16)
    d_heads_own, d_heads_sent, cols_own, cols_other = local_call(
        heads_back_kernel,
        [part, part, columns, columns],
        [where, d_branch_one, seq_swap(d_branch_one, 1), out_full],
        2**30,
        "heads_back",
        scratch=[pltpu.VMEM(*half_low)],
        spaces=[smem] + [vmem] * 3,
    )
    dox, d_heads_t = local_call(
        functools.partial(delta_kernel, heads),
        [wide_out, ((inner, group_rows), bf16)],
        [where, d_heads_own, seq_swap(d_heads_sent, 2), heads_n],
        block_flops // 4,
        "delta",
        spaces=[smem] + [vmem] * 3,
    )

    steps_out = [fsdp // 2] + [o for t in range(fsdp // 2 - 1, 0, -1) for o in (t, -t)] + [0]
    step_of = {o: i for i, o in enumerate(steps_out)}
    ring_rows = jnp.stack([ring_index(place + o, fsdp) for o in steps_out]).astype(jnp.int32)
    packed = ((fsdp, w_rows, own.shape[1]), bf16)
    cuts = [0, 3 * fsdp // 8, 5 * fsdp // 8, fsdp]
    grads_mine, *grads_other = local_call(
        grads_kernel,
        [packed] + [((b - a,) + packed[0][1:], bf16) for a, b in zip(cuts, cuts[1:])],
        [
            ring_rows,
            hidden_low,
            d_branch_two,
            heads_all,
            sums_one,
            sums_two,
            d_up,
            d_gate,
            acts[2],
            cols_own,
            d_up_other,
            d_gate_other,
            acts[5],
            cols_other,
        ],
        2**32,
        "grads",
        scratch=[pltpu.VMEM(*packed)],
        spaces=[smem] + [vmem] * 13,
    )

    got = [seq_swap(run, 2) for run in grads_other]

    def grads_part(offset):
        i = step_of[offset]
        which = sum(i >= cut for cut in cuts[1:])
        return [(grads_mine, i), (got[which], i - cuts[which])]

    d_query = jnp.zeros((inner, group_rows), f32)

    def back(offset, d_query, after):
        return local_call(
            functools.partial(back_kernel, heads, min(256, group_rows)),
            [((inner, group_rows), f32), ((2 * inner, group_rows), bf16)],
            [spots(offset), key_ext, qx, dox, queries, d_heads_t, d_query, *blocks[offset]],
            block_flops * 2,
            "attend_back",
            spaces=[smem] + [vmem] * (6 + len(blocks[offset])),
            after=after,
        )

    d_query, d_far = back(far, d_query, [])
    d_query, up = back(far - 1, d_query, [])
    d_query, down = back(1 - far, d_query, [])
    right, left = ring_shift(d_far[:inner], 1, SPAN), ring_shift(d_far[inner:], -1, SPAN)
    up = jnp.concatenate([up[:inner] + right, up[inner:]], axis=0)
    down = jnp.concatenate([down[:inner], down[inner:] + left], axis=0)
    after = [right, left]
    for t in range(far - 2, 0, -1):
        d_query, next_up = back(t, d_query, after)
        right, left = ring_shift(up, 1, SPAN), ring_shift(down, -1, SPAN)
        d_query, next_down = back(-t, d_query, [])
        after = [right, left]
        up, down = next_up + right, next_down + left
    right, left = ring_shift(up, 1, SPAN), ring_shift(down, -1, SPAN)
    d_query, d_kv = back(0, d_query, after)
    grads_sent = []
    if fsdp == SPAN:
        half = w_rows // 2
        (grads_far,) = block_sums([(grads_part(far), [])], False, [])
        up, down = block_sums(
            [
                (grads_part(far - 1), [ring_shift(grads_far[:half], 1, fsdp)]),
                (grads_part(1 - far), [ring_shift(grads_far[half:], -1, fsdp)]),
            ],
            True,
            [d_kv, got[1]],
        )
        grads_sent = [ring_shift(up, 1, fsdp), ring_shift(down, -1, fsdp)]
    grad_qkv, sent, kept = local_call(
        tail_kernel,
        [
            ((fsdp, w_rows, 3 * inner), bf16),
            ((2, tok_rows, width), bf16),
            ((2, tok_rows, width), f32),
        ],
        [
            ring_rows,
            where,
            d_query,
            d_kv,
            right,
            left,
            cosine,
            sine,
            x_all,
            qkv_full,
        ],
        2**32,
        "tail",
        scratch=[
            pltpu.VMEM((3 * inner, group_rows), bf16),
            pltpu.VMEM((fsdp, w_rows, 3 * inner), bf16),
        ],
        spaces=[smem, smem] + [vmem] * 8,
        after=grads_sent,
    )
    kept, sent = local_call(
        input_mid_kernel,
        [own_full, own_low],
        [where, kept, seq_swap(sent, 1)],
        2**20,
        "input_mid",
        spaces=[smem, vmem, vmem],
    )
    (d_input,) = local_call(
        input_end_kernel, [own_low], [d_first, kept, seq_swap(sent, 2)], 2**20, "input_end"
    )

    def qkv_part(offset):
        return [(grad_qkv, step_of[offset])]

    if fsdp == SPAN:
        qkv_own_grad, qkv_sent, qkv_first = ring_scatter(
            qkv_part, fsdp, [[], [kept]] + [[]] * (far - 3) + [[d_input]]
        )
        right, left = grads_sent
        for hop, t in enumerate(range(far - 2, 0, -1)):
            up, down = block_sums(
                [(grads_part(t), [right]), (grads_part(-t), [left])],
                False,
                [qkv_sent[hop + 1]] if hop else qkv_first,
            )
            right, left = ring_shift(up, 1, fsdp), ring_shift(down, -1, fsdp)
        (grads_own,) = block_sums([(grads_part(0), [right, left])], False, [qkv_sent[-1]])
    else:
        qkv_own_grad, *_ = ring_scatter(qkv_part, fsdp, [])
        grads_own, *_ = ring_scatter(grads_part, fsdp, [])

    def seq_gather(value, after):
        other = gate(seq_swap(value, 2), after) if after else seq_swap(value, 2)
        return [value, other, seq_swap(value, 1), seq_swap(other, 1)]

    qkv_parts = seq_gather(qkv_own_grad, [])
    parts = seq_gather(grads_own, qkv_parts[1:2])
    if aligned:
        final_qkv, final_up, final_gate, final_down, final_out, *final_vectors = local_call(
            functools.partial(unpack_all_kernel, fsdp, width),
            [(w.shape, f32) for w in (w_qkv, w_up, w_gate, w_down, w_out)]
            + [((1, w_rows), f32)] * 4,
            [seq_places, *parts, *qkv_parts],
            2**20,
            "unpack",
            scratch=[
                pltpu.VMEM((groups,) + parts[0].shape, bf16),
                pltpu.VMEM((groups, w_rows, 3 * inner), bf16),
            ],
            spaces=[smem] + [vmem] * 8,
        )
        final_vectors = [v.reshape(w_rows) for v in final_vectors]
    else:
        parts = arrange(parts, seq_order).astype(f32)

        def columns(at):
            value = parts[:, :, at : at + width].reshape(groups, w_rows, fsdp, w_rows)
            return value.transpose(1, 2, 0, 3).reshape(w_rows, groups * width)

        final_up, final_gate = columns(0), columns(width)
        final_down = parts[:, :, 2 * width : 3 * width].reshape(groups * w_rows, width)
        final_out = parts[:, :, 3 * width : 3 * width + inner].transpose(1, 0, 2)
        final_out = final_out.reshape(w_rows, width)
        final_vectors = jnp.sum(parts[:, :, 3 * width + inner :], axis=0).T
    if not aligned:
        (final_qkv,) = local_call(
            functools.partial(ordered_kernel, unpack_qkv_kernel, 4),
            [(w_qkv.shape, f32)],
            [seq_places, *qkv_parts],
            2**20,
            "unpack_qkv",
            scratch=[pltpu.VMEM((groups, w_rows, 3 * inner), bf16)],
            spaces=[smem] + [vmem] * 4,
        )
    return (
        result,
        d_input,
        final_qkv,
        final_out,
        final_vectors[0],
        final_vectors[1],
        final_up,
        final_gate,
        final_down,
        final_vectors[2],
        final_vectors[3],
    )


def solution(mesh):
    rows = P(("fsdp", "seq"), None)
    param, vector = P("fsdp", None), P("fsdp")
    in_specs = (rows, rows, P(), param, param, vector, vector, param, param, param, vector, vector)
    out_specs = (rows, rows, param, param, vector, vector, param, param, param, vector, vector)
    return jax.shard_map(local, mesh=mesh, in_specs=in_specs, out_specs=out_specs, check_vma=False)
```
